32 devices in a mesh: dp: 8 (over y, x, core), blk: 4 (over z).
Axes of the slice: x: 2, y: 2, z: 4, core: 2. Of those that a mesh axis runs over, the one named last changes fastest.
Arguments:
- tokens: bfloat16 [32768, 1024], P(('dp', 'blk')), may hold values from -6 to 6
- out_grad: bfloat16 [32768, 1024], P(('dp', 'blk')), may hold values from -6 to 6
- lengths: int32 [32], P(('dp', 'blk')), may hold values from 256 to 1024
- routes: int32 [32768, 8], P(('dp', 'blk')), may hold values from 0 to 15, all different within a row; in each aligned block of 1024 rows (0 to 1023, 1024 to 2047, ...) at most 640 rows name the same one
- attn_weight: float32 [1024, 3072], P(('dp', 'blk'))
- router_weight: float32 [1024, 16], P(('dp', 'blk')), may hold values from -0.09375 to 0.09375
- expert_weight: float32 [3, 16384, 512], P(None, ('dp', 'blk'))
- gains: float32 [2, 1024], P(None, ('dp', 'blk')), may hold values from 0.25 to 1.75
- attn_moment: float32 [1024, 3072], P(('dp', 'blk'))
- router_moment: float32 [1024, 16], P(('dp', 'blk'))
- expert_moment: float32 [3, 16384, 512], P(None, ('dp', 'blk'))
- gain_first: float32 [2, 1024], P(None, ('dp', 'blk'))
- gain_second: float32 [2, 1024], P(None, ('dp', 'blk'))
- attn_ema: float32 [1024, 3072], P(('dp', 'blk')), may hold values from -0.75 to 0.75
- router_ema: float32 [1024, 16], P(('dp', 'blk')), may hold values from -0.09375 to 0.09375
- expert_ema: float32 [3, 16384, 512], P(None, ('dp', 'blk')), may hold values from -0.1875 to 0.1875
- gain_ema: float32 [2, 1024], P(None, ('dp', 'blk')), may hold values from 0.5 to 1.5
Outputs:
- block_out: bfloat16 [32768, 1024], P(('dp', 'blk'))
- input_grad: float32 [32768, 1024], P(('dp', 'blk'))
- attn_moment_new: float32 [1024, 3072], P(('dp', 'blk'))
- router_moment_new: float32 [1024, 16], P(('dp', 'blk'))
- expert_moment_new: float32 [3, 16384, 512], P(None, ('dp', 'blk'))
- attn_new: float32 [1024, 3072], P(('dp', 'blk'))
- router_new: float32 [1024, 16], P(('dp', 'blk'))
- expert_new: float32 [3, 16384, 512], P(None, ('dp', 'blk'))
- attn_copy: bfloat16 [1024, 3072], P(('dp', 'blk'))
- router_copy: bfloat16 [1024, 16], P(('dp', 'blk'))
- expert_copy: bfloat16 [3, 16384, 512], P(None, ('dp', 'blk'))
- attn_ema_new: float32 [1024, 3072], P(('dp', 'blk'))
- router_ema_new: float32 [1024, 16], P(('dp', 'blk'))
- expert_ema_new: float32 [3, 16384, 512], P(None, ('dp', 'blk'))
- gain_first_new: float32 [2, 1024], P(None, ('dp', 'blk'))
- gain_second_new: float32 [2, 1024], P(None, ('dp', 'blk'))
- gain_new: float32 [2, 1024], P(None, ('dp', 'blk'))
- gain_copy: bfloat16 [2, 1024], P(None, ('dp', 'blk'))
- gain_ema_new: float32 [2, 1024], P(None, ('dp', 'blk'))
The draws below stay inside these ranges and needn't reach their ends.
Inputs may be any that keep to these rules, and one draw needn't show every extreme that they name: `routes`: in the rows of one device no expert is named more than 640 times.
All inputs are finite; a program needn't handle non-finite values.
Results may differ from the reference program's by a relative error of at most 0.015.
The reference program's roundings to bfloat16 on the way count: a program that leaves them out, or rounds other values in their place, can miss the bound.
Values may be sent and summed in bfloat16 or wider, within the bound.
No kernel may reach another device: no remote copies, remote signals or barrier semaphores. Data moves between devices by JAX's collectives and lax.ppermute only.
A program may use at most 640 MiB of HBM per device.

```python
import math
from functools import partial
import jax
import jax.numpy as jnp
import numpy as np
from jax import lax

D = 1024
HEADS = 16
KV_HEADS = 8
HEAD_DIM = 64
FF = 512
TOP = 8
EXPERTS = 16
SEQ = 1024
STEP = 10
ATTN_COLS = 3072
TOK_DEV = 1024
CAP = 640
SEQS = 32
TOKENS = 32768
N_DP = 8
N_BLK = 4


def column_spread(query_value, key_value, value_value, out_value):
    query_width = HEADS * HEAD_DIM
    kv_width = KV_HEADS * HEAD_DIM
    return jnp.concatenate([jnp.full((query_width,), query_value, jnp.float32), jnp.full((kv_width,), key_value, jnp.float32), jnp.full((kv_width,), value_value, jnp.float32), jnp.full((query_width,), out_value, jnp.float32)])


def owner_rise(count, rows_each, low_end, high_end):
    place = jnp.arange(count) // rows_each % N_BLK
    return low_end + (high_end - low_end) * place.astype(jnp.float32) / max(N_BLK - 1, 1)


def draw_attn_weight(key, part):
    key = jax.random.fold_in(key, 1)
    spread_row = column_spread(1.0 / math.sqrt(D // 16), 1.0 / math.sqrt(D // 16), 1.0 / math.sqrt(D), 1.0 / math.sqrt(max(D // 48, 1)))
    return jax.random.normal(key, (D, 2 * HEADS * HEAD_DIM + 2 * KV_HEADS * HEAD_DIM), jnp.float32) * spread_row[None, :]


def draw_expert_weight(key, part):
    key = jax.random.fold_in(key, 2)
    spread_row = jnp.array([1.0 / math.sqrt(D), 1.0 / math.sqrt(D), 1.0 / math.sqrt(max(FF // 256, 1))], jnp.float32)
    return jax.random.normal(key, (3, EXPERTS * D, FF), jnp.float32) * spread_row[:, None, None]


def draw_attn_moment(key, part):
    key = jax.random.fold_in(key, 3)
    noise_key, row_key = jax.random.split(key)
    shape = (D, 2 * HEADS * HEAD_DIM + 2 * KV_HEADS * HEAD_DIM)
    rows_each = D // (N_DP * N_BLK)
    noise = jax.random.normal(noise_key, shape, jnp.float32)
    rise = owner_rise(D, rows_each, 0.6, 1.8)
    row_multiplier = jax.random.uniform(row_key, (D,), jnp.float32, 0.7, 1.4)
    spread_row = column_spread(0.27, 0.38, 1.7, 0.08) * math.sqrt(TOKENS)
    return noise * (rise * row_multiplier)[:, None] * spread_row[None, :]


def draw_router_moment(key, part):
    key = jax.random.fold_in(key, 4)
    noise_key, row_key = jax.random.split(key)
    rows_each = D // (N_DP * N_BLK)
    noise = jax.random.normal(noise_key, (D, EXPERTS), jnp.float32)
    rise = owner_rise(D, rows_each, 0.6, 1.8)
    row_multiplier = jax.random.uniform(row_key, (D,), jnp.float32, 0.7, 1.4)
    return noise * (rise * row_multiplier)[:, None] * (6.3 * math.sqrt(TOKENS))


def draw_expert_moment(key, part):
    key = jax.random.fold_in(key, 5)
    noise_key, row_key = jax.random.split(key)
    rows_each = EXPERTS * D // (N_DP * N_BLK)
    shape = (3, EXPERTS * D, FF)
    noise = jax.random.normal(noise_key, shape, jnp.float32)
    rise = owner_rise(EXPERTS * D, rows_each, 0.6, 1.8)
    row_multiplier = jax.random.uniform(row_key, (3, EXPERTS * D), jnp.float32, 0.7, 1.4)
    kind_factor = jnp.array([0.17, 0.17, 0.009], jnp.float32) * math.sqrt(TOKENS)
    return noise * (rise[None, :] * row_multiplier)[:, :, None] * kind_factor[:, None, None]


def draw_gain_first(key, part):
    key = jax.random.fold_in(key, 6)
    noise = jax.random.normal(key, (2, D), jnp.float32)
    kind_factor = jnp.array([2.0, 0.8], jnp.float32) * math.sqrt(TOKENS) / 9.0
    return noise * kind_factor[:, None]


def draw_gain_second(key, part):
    key = jax.random.fold_in(key, 7)
    factor = jax.random.uniform(key, (2, D), jnp.float32, 1.0, 4.0)
    kind_factor = jnp.array([2.0, 0.8], jnp.float32) * math.sqrt(TOKENS)
    return factor * (kind_factor * kind_factor)[:, None] * (0.05 / 0.95)


def touch_ends(values, rng, least, high):
    longest = values.shape.index(max(values.shape))
    spots = []
    for shift in (0, 1):
        where = [jax.random.randint(jax.random.fold_in(rng, axis), (), 0, length) for axis, length in enumerate(values.shape)]
        where[longest] = (where[longest] + shift) % values.shape[longest]
        spots.append(tuple(where))
    return values.at[spots[0]].set(least).at[spots[1]].set(high)


def block_scale(stream_key, shape, cuts, least, high):
    def one(dim, parts):
        steps = jax.random.uniform(jax.random.fold_in(jax.random.fold_in(stream_key, 6), dim), (parts,), jnp.float32, least / len(cuts), high / len(cuts))
        return jnp.repeat(jnp.exp(steps), shape[dim] // parts).reshape((-1,) + (1,) * (len(shape) - dim - 1))

    gain = one(*cuts[0])
    for cut in cuts[1:]:
        gain = gain * one(*cut)
    return gain


def routed_block(stream_key, own, number, rows, count, top, reach, lean):
    sequence = jax.random.permutation(stream_key, count)
    packed, ordinary = load_shares(count, rows * top, reach, lean, True), load_shares(count, rows * top, reach, lean, False)
    places = jnp.arange(count)

    def named(sizes, rotation):
        used = int((sizes > 0).sum())
        fixed = max(1, used // 4)
        shifted = fixed + (places - fixed + rotation * (used - fixed)) % max(1, count - fixed)
        return jnp.zeros((count,), jnp.int32).at[sequence[jnp.where(places < fixed, places, shifted)]].set(jnp.asarray(sizes, jnp.int32))

    sizes = jnp.where(number % 4 == 0, named(packed, number // 4), named(ordinary, number - number // 4 - 1))
    mixed = jax.random.permutation(jax.random.fold_in(own, 3), count)
    giver, sink = mixed[0:count // 2 * 2:2], mixed[1:count // 2 * 2:2]
    slack = jnp.minimum(sizes[giver] - 1, reach - sizes[sink]) // 2
    slack = jnp.where((giver == sequence[0]) | (sink == sequence[0]) | (sizes[sink] == 0), 0, jnp.maximum(slack, 0))
    shifted = jax.random.randint(jax.random.fold_in(own, 4), (count // 2,), 0, 1 << 20) % (slack + 1)
    sizes = sizes.at[giver].add(-shifted).at[sink].add(shifted)
    items = jnp.searchsorted(jnp.cumsum(sizes), jnp.arange(rows * top), side="right").astype(jnp.int32)
    table = items.reshape(top, rows).T
    table = table[jax.random.permutation(jax.random.fold_in(own, 1), rows)]
    rotation = jax.random.randint(jax.random.fold_in(own, 2), (rows, 1), 0, top)
    return jnp.take_along_axis(table, (jnp.arange(top)[None, :] + rotation) % top, axis=1)


def load_shares(number_of, total, bound, lean, full):
    portions = [(1 << 20) // math.isqrt(rank ** lean) + 1 for rank in range(1, number_of + 1)]
    largest = bound if full else min(bound, max(-(-total // number_of), total * portions[0] // sum(portions)))
    least = 1 if total - largest >= number_of - 1 else 0
    given, surplus = [largest] + [least] * (number_of - 1), total - largest - least * (number_of - 1)
    while surplus > 0:
        movable = [i for i in range(1, number_of) if given[i] < largest] or [i for i in range(1, number_of) if given[i] < bound]
        whole, left = sum([portions[i] for i in movable]), surplus
        for i in movable:
            extra = min(bound - given[i], max(1, left * portions[i] // whole), surplus)
            given[i] = given[i] + extra
            surplus = surplus - extra
    return np.array(given)


def scatter_about(own_key, extent, scale, limit, shards=(), kind=jnp.bfloat16):
    values = jax.random.normal(own_key, extent, jnp.float32) * scale
    if len(shards) > 0:
        values = block_scale(own_key, extent, shards, -0.22, 0.18) * values
    return jnp.clip(values, min=-limit, max=limit).astype(kind)


def setup_inputs(seed: int = 0) -> dict:
    key_of = jax.random.split(jax.random.key(seed), 18)
    tokens = scatter_about(key_of[0], (TOKENS, D), 1.0, 6.0, ((0, 32),))
    out_grad = scatter_about(key_of[1], (TOKENS, D), 1.0, 6.0, ((0, 32),))
    lengths = touch_ends(jax.random.randint(key_of[2], (SEQS,), SEQ // 4, SEQ + 1), jax.random.fold_in(key_of[2], 1), SEQ // 4, SEQ).astype(jnp.int32)
    routes_keys = jax.random.split(jax.random.fold_in(key_of[3], 1), TOKENS // TOK_DEV)
    routes_turns = jax.random.permutation(jax.random.fold_in(key_of[3], 3), TOKENS // TOK_DEV)
    routes = jax.vmap(lambda own, number: routed_block(jax.random.fold_in(key_of[3], 2), own, number, TOK_DEV, EXPERTS, TOP, CAP, 1))(routes_keys, routes_turns).reshape((TOKENS, TOP))
    attn_weight = draw_attn_weight(jax.random.fold_in(key_of[17], 71), 0)
    router_weight = scatter_about(key_of[5], (D, EXPERTS), (4 * D) ** -0.5, 0.09375, ((0, 32),), jnp.float32)
    expert_weight = draw_expert_weight(jax.random.fold_in(key_of[17], 71), 0)
    gains = jnp.clip(1.0 + 0.15 * jax.random.normal(key_of[7], (2, D), jnp.float32), 0.25, 1.75)
    attn_moment = draw_attn_moment(jax.random.fold_in(key_of[17], 71), 0)
    router_moment = draw_router_moment(jax.random.fold_in(key_of[17], 71), 0)
    expert_moment = draw_expert_moment(jax.random.fold_in(key_of[17], 71), 0)
    gain_first = draw_gain_first(jax.random.fold_in(key_of[17], 71), 0)
    gain_second = draw_gain_second(jax.random.fold_in(key_of[17], 71), 0)
    attn_ema = scatter_about(key_of[13], (D, ATTN_COLS), (D // 16) ** -0.5, 0.75, ((0, 32),), jnp.float32)
    router_ema = scatter_about(key_of[14], (D, EXPERTS), (4 * D) ** -0.5, 0.09375, ((0, 32),), jnp.float32)
    expert_ema = scatter_about(key_of[15], (3, EXPERTS * D, FF), D ** -0.5, 0.1875, ((1, 32),), jnp.float32)
    gain_ema = jnp.clip(1.0 + 0.1 * jax.random.normal(key_of[16], (2, D), jnp.float32), 0.5, 1.5)
    return {"tokens": tokens, "out_grad": out_grad, "lengths": lengths, "routes": routes, "attn_weight": attn_weight, "router_weight": router_weight, "expert_weight": expert_weight, "gains": gains, "attn_moment": attn_moment, "router_moment": router_moment, "expert_moment": expert_moment, "gain_first": gain_first, "gain_second": gain_second, "attn_ema": attn_ema, "router_ema": router_ema, "expert_ema": expert_ema, "gain_ema": gain_ema}


@jax.custom_vjp
def low(v):
    return lax.optimization_barrier(v.astype(jnp.bfloat16)).astype(jnp.float32)

@jax.custom_vjp
def low_back(v):
    return v

def low_keep(v):
    return (low(v), None)

def low_pass(kept, grad):
    return (grad,)

def back_keep(v):
    return (v, None)

def back_low(kept, grad):
    return (low(grad),)
low.defvjp(low_keep, low_pass)
low_back.defvjp(back_keep, back_low)
NORM_EPS = 1e-05
ATTN_MULT = 0.015625
RESID_MULT = 0.22
ROPE_BASE = 10000.0
NEG_FILL = -1e+30
POLY_ONE = 3.4445
POLY_TWO = -4.775
POLY_THREE = 2.0315
ORTHO_EPS = 1e-07
MOMENTUM = 0.95
MUON_RATE = 0.6
MUON_SHAPE = 0.2
WEIGHT_DECAY = 0.01
ADAM_RATE = 0.8
BETA_ONE = 0.9
BETA_TWO = 0.95
ADAM_EPS = 1e-08
EMA_KEEP = 0.9
GAIN_EMA_KEEP = 0.6

def precise_dot(left_side, right_side):
    return jnp.dot(left_side, right_side, precision=lax.Precision.HIGHEST)

def rms_norm(values, gain_row):
    return values * lax.rsqrt(lax.optimization_barrier(jnp.mean(values * values, axis=-1, keepdims=True)) + NORM_EPS) * gain_row

def rotary_tables():
    position = jnp.arange(SEQ).astype(jnp.float32)
    inverse = ROPE_BASE ** (-jnp.arange(0, HEAD_DIM, 2).astype(jnp.float32) / HEAD_DIM)
    angles = position[:, None] * inverse[None, :]
    return (jnp.cos(angles), jnp.sin(angles))

def rotate(values, cosine_table, sine_table):
    half_width = values.shape[-1] // 2
    first_half = values[..., :half_width]
    second_half = values[..., half_width:]
    cosine = cosine_table[:, None, :]
    sine_part = sine_table[:, None, :]
    return jnp.concatenate([first_half * cosine - second_half * sine_part, second_half * cosine + first_half * sine_part], axis=-1)

def attention(normed, length, weights, cosine_table, sine_table):
    group_size = HEADS // KV_HEADS
    query_width = HEADS * HEAD_DIM
    kv_width = KV_HEADS * HEAD_DIM
    w_query = weights[:, :query_width]
    w_key = weights[:, query_width:query_width + kv_width]
    w_value = weights[:, query_width + kv_width:query_width + 2 * kv_width]
    w_out = weights[:, query_width + 2 * kv_width:]
    queries = low(rotate(low_back(precise_dot(normed, w_query)).reshape(SEQ, HEADS, HEAD_DIM), cosine_table, sine_table))
    key_rows = low(rotate(low_back(precise_dot(normed, w_key)).reshape(SEQ, KV_HEADS, HEAD_DIM), cosine_table, sine_table))
    value_rows = low(low_back(precise_dot(normed, w_value))).reshape(SEQ, KV_HEADS, HEAD_DIM)
    queries = queries.reshape(SEQ, KV_HEADS, group_size, HEAD_DIM)
    scores = low_back(jnp.einsum('qkgd,skd->kgqs', queries, key_rows, precision=lax.Precision.HIGHEST) * ATTN_MULT)
    position = jnp.arange(SEQ)
    allowed = (position[None, :] <= position[:, None]) & (position[None, :] < length)
    scores = jnp.where(allowed, scores, NEG_FILL)
    largest = lax.optimization_barrier(jnp.max(scores, axis=-1, keepdims=True))
    exponent = jnp.exp(scores - largest)
    probability = exponent / lax.optimization_barrier(jnp.sum(exponent, axis=-1, keepdims=True))
    attended = jnp.einsum('kgqs,skd->qkgd', low(probability), value_rows, precision=lax.Precision.HIGHEST)
    attended = low_back(low(attended.reshape(SEQ, query_width)))
    return low_back(precise_dot(attended, w_out.T))

def mixture(normed, route_rows, router, experts):
    logits = low_back(precise_dot(normed, router))
    chosen = jnp.take_along_axis(logits, route_rows, axis=1)
    largest = lax.optimization_barrier(jnp.max(chosen, axis=1, keepdims=True))
    exponent = jnp.exp(chosen - largest)
    gate_weights = exponent / lax.optimization_barrier(jnp.sum(exponent, axis=1, keepdims=True))
    matches = route_rows[:, :, None] == jnp.arange(EXPERTS)[None, None, :]
    combine_outputs = lax.optimization_barrier(jnp.sum(jnp.where(matches, gate_weights[:, :, None], 0.0), axis=1))
    gate_part = low_back(jnp.einsum('nd,edf->enf', normed, experts[0], precision=lax.Precision.HIGHEST))
    up_part = low_back(jnp.einsum('nd,edf->enf', normed, experts[1], precision=lax.Precision.HIGHEST))
    hidden = low(gate_part * jax.nn.sigmoid(gate_part) * up_part)
    expert_out = low_back(jnp.einsum('enf,edf->end', hidden, experts[2], precision=lax.Precision.HIGHEST))
    return jnp.einsum('ne,end->nd', combine_outputs, expert_out, precision=lax.Precision.HIGHEST)

def forward(inputs, gains, attn_weight, router_weight, expert_weight, lengths, routes):
    gain_low = low(gains)
    attn_low = low(attn_weight)
    router_low = low(router_weight)
    expert_low = low(expert_weight).reshape(3, EXPERTS, D, FF)
    cosine_table, sine_table = rotary_tables()

    def one_sequence(pieces):
        seq_rows, length, route_rows = pieces
        normed = low(rms_norm(seq_rows, gain_low[0]))
        branch = attention(normed, length, attn_low, cosine_table, sine_table)
        hidden_state = seq_rows + RESID_MULT * branch
        second = low(rms_norm(hidden_state, gain_low[1]))
        return hidden_state + RESID_MULT * mixture(second, route_rows, router_low, expert_low)
    outputs = lax.map(jax.checkpoint(one_sequence), (inputs.reshape(SEQS, SEQ, D), lengths, routes.reshape(SEQS, SEQ, TOP)))
    return outputs.reshape(SEQS * SEQ, D)

def orthogonalize(moment):
    scale_norm = jnp.sqrt(jnp.sum(moment * moment))
    newton_iterate = moment / (scale_norm + ORTHO_EPS)
    for iteration in range(5):
        gram_square = precise_dot(newton_iterate.T, newton_iterate)
        gram_product = precise_dot(newton_iterate, gram_square)
        newton_iterate = POLY_ONE * newton_iterate + POLY_TWO * gram_product + POLY_THREE * precise_dot(gram_product, gram_square)
    return newton_iterate

def muon_update(weight, ortho):
    return weight * (1.0 - MUON_RATE * WEIGHT_DECAY) - MUON_RATE * MUON_SHAPE * math.sqrt(D) * ortho

def reference(tokens, out_grad, lengths, routes, attn_weight, router_weight, expert_weight, gains, attn_moment, router_moment, expert_moment, gain_first, gain_second, attn_ema, router_ema, expert_ema, gain_ema):
    inputs = tokens.astype(jnp.float32)
    outputs, pullback = jax.vjp(partial(forward, lengths=lengths, routes=routes), inputs, gains, attn_weight, router_weight, expert_weight)
    live_rows = (jnp.arange(SEQ)[None, :] < lengths[:, None]).reshape(SEQS * SEQ, 1)
    cotangent = jnp.where(live_rows, out_grad.astype(jnp.float32), 0.0)
    grad_inputs, grad_gains, grad_attn, grad_router, grad_expert = pullback(cotangent)
    query_width = HEADS * HEAD_DIM
    kv_width = KV_HEADS * HEAD_DIM
    moment_attn = MOMENTUM * attn_moment + grad_attn
    moment_router = MOMENTUM * router_moment + grad_router
    moment_expert = MOMENTUM * expert_moment + grad_expert
    ortho_attn = jnp.concatenate([orthogonalize(moment_attn[:, :query_width]), orthogonalize(moment_attn[:, query_width:query_width + kv_width]), orthogonalize(moment_attn[:, query_width + kv_width:query_width + 2 * kv_width]), orthogonalize(moment_attn[:, query_width + 2 * kv_width:])], axis=1)
    ortho_router = orthogonalize(moment_router)
    ortho_expert = jax.vmap(orthogonalize)(moment_expert.reshape(3 * EXPERTS, D, FF)).reshape(3, EXPERTS * D, FF)
    attn_new = muon_update(attn_weight, ortho_attn)
    router_new = muon_update(router_weight, ortho_router)
    expert_new = muon_update(expert_weight, ortho_expert)
    first_new = BETA_ONE * gain_first + (1.0 - BETA_ONE) * grad_gains
    second_new = BETA_TWO * gain_second + (1.0 - BETA_TWO) * grad_gains * grad_gains
    corrected_first = first_new / (1.0 - BETA_ONE ** STEP)
    corrected_second = second_new / (1.0 - BETA_TWO ** STEP)
    gain_new = gains - ADAM_RATE * corrected_first / (jnp.sqrt(corrected_second) + ADAM_EPS)
    return (outputs.astype(jnp.bfloat16), grad_inputs, moment_attn, moment_router, moment_expert, attn_new, router_new, expert_new, attn_new.astype(jnp.bfloat16), router_new.astype(jnp.bfloat16), expert_new.astype(jnp.bfloat16), EMA_KEEP * attn_ema + (1.0 - EMA_KEEP) * attn_new, EMA_KEEP * router_ema + (1.0 - EMA_KEEP) * router_new, EMA_KEEP * expert_ema + (1.0 - EMA_KEEP) * expert_new, first_new, second_new, gain_new, gain_new.astype(jnp.bfloat16), GAIN_EMA_KEEP * gain_ema + (1.0 - GAIN_EMA_KEEP) * gain_new)
```

```python
import functools
import math

import jax
import jax.numpy as jnp
from jax import lax
from jax.experimental import pallas as pl
from jax.experimental.layout import Layout, with_layout_constraint
from jax.experimental.pallas import tpu as pltpu
from jax.sharding import PartitionSpec as P

D = 1024
HEADS = 16
KV_HEADS = 8
HEAD_DIM = 64
FF = 512
TOP = 8
EXPERTS = 16
STEP = 10
HALF = D // 2
PACK = 128
AXES = ("dp", "blk")


NORM_EPS = 1e-05
ATTN_MULT = 0.015625
RESID_MULT = 0.22
ROPE_BASE = 10000.0
NEG_FILL = -1e30
POLY_ONE = 3.4445
POLY_TWO = -4.775
POLY_THREE = 2.0315
ORTHO_EPS = 1e-07
MOMENTUM = 0.95
MUON_RATE = 0.6
MUON_SHAPE = 0.2
WEIGHT_DECAY = 0.01
ADAM_RATE = 0.8
BETA_ONE = 0.9
BETA_TWO = 0.95
ADAM_EPS = 1e-08
EMA_KEEP = 0.9
GAIN_EMA_KEEP = 0.6


def plain_dot(left_side, right_side, contract_left, contract_right):
    return lax.dot_general(
        left_side,
        right_side,
        (((contract_left,), (contract_right,)), ((), ())),
        preferred_element_type=jnp.float32,
    )


def rotary_tables(length, head_width):
    position = jnp.arange(length).astype(jnp.float32)
    inverse = ROPE_BASE ** (-jnp.arange(0, head_width, 2).astype(jnp.float32) / head_width)
    angles = position[:, None] * inverse[None, :]
    return (jnp.cos(angles), jnp.sin(angles))


def norm_back(grad_normed, unit_rows, scale_rows, gain_row):
    grad_unit = grad_normed * gain_row
    return scale_rows * (
        grad_unit - unit_rows * jnp.mean(grad_unit * unit_rows, axis=-1, keepdims=True)
    )


def pin(values):
    return with_layout_constraint(values, Layout(major_to_minor=tuple(range(values.ndim))))


def swap_bit(values, count, bit):
    pairs = [(place, place ^ bit) for place in range(count)]
    return pin(lax.ppermute(pin(values), AXES, pairs))


def after(values, *done):
    return lax.optimization_barrier((values,) + done)[0]


def low_add(left_side, right_side):
    return (left_side.astype(jnp.float32) + right_side.astype(jnp.float32)).astype(jnp.bfloat16)


def bits_below(low_bit, high_bit):
    bits = []
    while low_bit < high_bit:
        bits.append(low_bit)
        low_bit *= 2
    return bits


def gather_rows(values, axis, count, place, bits):
    for bit in bits:
        other = swap_bit(values, count, bit)
        upper = (place // bit) % 2 == 1
        values = jnp.where(
            upper,
            jnp.concatenate([other, values], axis=axis),
            jnp.concatenate([values, other], axis=axis),
        )
    return values


def reduce_rows(values, count, place, bits):
    for bit in bits:
        split = values.reshape((2, values.shape[0] // 2) + values.shape[1:])
        own = (place // bit) % 2
        keep = lax.dynamic_index_in_dim(split, own, 0, keepdims=False)
        other = swap_bit(
            lax.dynamic_index_in_dim(split, 1 - own, 0, keepdims=False), count, bit
        )
        values = low_add(keep, other)
    return values


def dot_nn(left_side, right_side):
    return plain_dot(left_side, right_side, 1, 0)


def dot_nt(left_side, right_side):
    return plain_dot(left_side, right_side, 1, 1)


def dot_tn(left_side, right_side):
    return plain_dot(left_side, right_side, 0, 0)


def turn(values, cosine, sine, lanes):
    far = jnp.where(
        lanes % HEAD_DIM < HEAD_DIM // 2,
        pltpu.roll(values, PACK - HEAD_DIM // 2, 1),
        pltpu.roll(values, HEAD_DIM // 2, 1),
    )
    return values * cosine + far * sine


def project_kernel(
    tok_ref, gain_ref, wq_ref, wkv_ref, cos_ref, sin_ref, norm_ref, q_ref, k_ref, v_ref
):
    rows = tok_ref.shape[0]
    inputs = tok_ref[...].astype(jnp.float32)
    scale = lax.rsqrt(jnp.mean(inputs * inputs, axis=-1, keepdims=True) + NORM_EPS)
    normed = (inputs * scale * gain_ref[...]).astype(jnp.bfloat16)
    norm_ref[...] = normed
    cosine, sine = cos_ref[...], sin_ref[...]
    lanes = lax.broadcasted_iota(jnp.int32, (rows, PACK), 1)
    query = dot_nn(normed, wq_ref[...])
    for start in range(0, HEADS * HEAD_DIM, PACK):
        turned = turn(query[:, start : start + PACK], cosine, sine, lanes)
        q_ref[:, start : start + PACK] = turned.astype(jnp.bfloat16) * ATTN_MULT
    both = dot_nn(normed, wkv_ref[...])
    width = KV_HEADS * HEAD_DIM
    for start in range(0, width, PACK):
        turned = turn(both[:, start : start + PACK], cosine, sine, lanes)
        k_ref[:, start : start + PACK] = turned.astype(jnp.bfloat16)
    v_ref[...] = both[:, width:].astype(jnp.bfloat16)


def project_call(tokens, gain_row, wq, wkv, cosine, sine):
    seq_rows = cosine.shape[0]
    rows = min(256, seq_rows)
    repeats = seq_rows // rows
    tok_here = tokens.shape[0]
    width = KV_HEADS * HEAD_DIM
    low = jnp.bfloat16
    return pl.pallas_call(
        project_kernel,
        grid=(tok_here // rows,),
        in_specs=[
            pl.BlockSpec((rows, D), lambda b: (b, 0)),
            pl.BlockSpec((1, D), lambda b: (0, 0)),
            pl.BlockSpec((D, HEADS * HEAD_DIM), lambda b: (0, 0)),
            pl.BlockSpec((D, 2 * width), lambda b: (0, 1)),
            pl.BlockSpec((rows, PACK), lambda b: (b % repeats, 0)),
            pl.BlockSpec((rows, PACK), lambda b: (b % repeats, 0)),
        ],
        out_specs=[
            pl.BlockSpec((rows, D), lambda b: (b, 0)),
            pl.BlockSpec((rows, HEADS * HEAD_DIM), lambda b: (b, 0)),
            pl.BlockSpec((rows, width), lambda b: (b, 0)),
            pl.BlockSpec((rows, width), lambda b: (b, 0)),
        ],
        out_shape=[
            jax.ShapeDtypeStruct((tok_here, D), low),
            jax.ShapeDtypeStruct((tok_here, HEADS * HEAD_DIM), low),
            jax.ShapeDtypeStruct((tok_here, width), low),
            jax.ShapeDtypeStruct((tok_here, width), low),
        ],
        compiler_params=pltpu.CompilerParams(
            dimension_semantics=("arbitrary",), vmem_limit_bytes=40 * 1024 * 1024
        ),
        cost_estimate=pl.CostEstimate(
            flops=8_000_000_000, bytes_accessed=14_000_000, transcendentals=0
        ),
        name="project",
    )(tokens, gain_row, wq, wkv, cosine, sine)


def attend_kernel(len_ref, q_ref, k_ref, v_ref, *refs):
    o_ref, lse_ref = refs[-2:]
    seq_len = q_ref.shape[0]
    rows = min(256, seq_len)
    length = len_ref[0, 0]
    for first in range(0, seq_len, rows):
        keys = first + rows
        key_index = lax.broadcasted_iota(jnp.int32, (rows, keys), 1)
        query_index = first + lax.broadcasted_iota(jnp.int32, (rows, keys), 0)
        bias = jnp.where((key_index <= query_index) & (key_index < length), 0.0, NEG_FILL)
        lanes = lax.broadcasted_iota(jnp.int32, (rows, PACK), 1)
        totals = jnp.zeros((rows, PACK), jnp.float32)
        for head in range(4):
            shared = (head // 2) * HEAD_DIM
            key_rows = k_ref[:keys, shared : shared + HEAD_DIM]
            value_rows = v_ref[:keys, shared : shared + HEAD_DIM]
            query = q_ref[first:keys, head * HEAD_DIM : (head + 1) * HEAD_DIM]
            scores = dot_nt(query, key_rows) + bias
            largest = jnp.max(scores, axis=1, keepdims=True)
            exponent = jnp.exp(scores - largest)
            total = jnp.sum(exponent, axis=1, keepdims=True)
            probability = (exponent * (1.0 / total)).astype(jnp.bfloat16)
            o_ref[first:keys, head * HEAD_DIM : (head + 1) * HEAD_DIM] = dot_nn(
                probability, value_rows
            ).astype(jnp.bfloat16)
            totals = jnp.where(lanes == head, largest + jnp.log(total), totals)
        lse_ref[0, :, first:keys] = totals.T[:8]


def attend_call(lengths, query, key_rows, value_rows, seq_len, done):
    tok_here = query.shape[0]
    seqs = tok_here // seq_len
    groups = KV_HEADS // 2
    return pl.pallas_call(
        attend_kernel,
        grid=(seqs, groups),
        in_specs=[
            pl.BlockSpec((1, 1), lambda s, g: (s, 0), memory_space=pltpu.SMEM),
            pl.BlockSpec((seq_len, 4 * HEAD_DIM), lambda s, g: (s, g)),
            pl.BlockSpec((seq_len, PACK), lambda s, g: (s, g)),
            pl.BlockSpec((seq_len, PACK), lambda s, g: (s, g)),
        ]
        + [pl.BlockSpec(memory_space=pl.ANY)] * len(done),
        out_specs=[
            pl.BlockSpec((seq_len, 4 * HEAD_DIM), lambda s, g: (s, g)),
            pl.BlockSpec((1, 8, seq_len), lambda s, g: (g, 0, s)),
        ],
        out_shape=[
            jax.ShapeDtypeStruct((tok_here, HEADS * HEAD_DIM), jnp.bfloat16),
            jax.ShapeDtypeStruct((groups, 8, tok_here), jnp.float32),
        ],
        compiler_params=pltpu.CompilerParams(
            dimension_semantics=("arbitrary", "arbitrary"), vmem_limit_bytes=40 * 1024 * 1024
        ),
        cost_estimate=pl.CostEstimate(
            flops=20_000_000_000, bytes_accessed=8_000_000, transcendentals=12_000_000
        ),
        name="attend",
    )(lengths.reshape(seqs, 1), query, key_rows, value_rows, *done)


def attend_back_kernel(
    len_ref,
    q_ref,
    k_ref,
    v_ref,
    do_ref,
    lse_ref,
    cos_ref,
    sin_ref,
    *refs,
):
    dq_ref, dk_ref, dv_ref, k_acc, v_acc = refs[-5:]
    seq_len = q_ref.shape[0]
    rows = min(256, seq_len)
    length = len_ref[0, 0]
    k_acc[...] = jnp.zeros_like(k_acc)
    v_acc[...] = jnp.zeros_like(v_acc)
    lanes = lax.broadcasted_iota(jnp.int32, (rows, PACK), 1)
    turned_keys = [
        k_ref[:, shared : shared + HEAD_DIM].T for shared in (0, HEAD_DIM)
    ]
    for first in range(0, seq_len, rows):
        keys = first + rows
        key_index = lax.broadcasted_iota(jnp.int32, (keys, rows), 0)
        query_index = first + lax.broadcasted_iota(jnp.int32, (keys, rows), 1)
        bias = jnp.where((key_index <= query_index) & (key_index < length), 0.0, NEG_FILL)
        for pair in range(2):
            shared = pair * HEAD_DIM
            key_rows = k_ref[:keys, shared : shared + HEAD_DIM]
            value_rows = v_ref[:keys, shared : shared + HEAD_DIM]
            key_grad = None
            value_grad = None
            query_grads = []
            for head in (2 * pair, 2 * pair + 1):
                query = q_ref[first:keys, head * HEAD_DIM : (head + 1) * HEAD_DIM]
                grad = do_ref[first:keys, head * HEAD_DIM : (head + 1) * HEAD_DIM]
                scores = dot_nt(key_rows, query) + bias
                probability = jnp.exp(scores - lse_ref[0, head : head + 1, first:keys])
                prob_grad = dot_nt(value_rows, grad)
                inner = jnp.sum(probability * prob_grad, axis=0, keepdims=True)
                score_grad = (probability * (prob_grad - inner)).astype(jnp.bfloat16)
                key_part = dot_nn(score_grad, query)
                value_part = dot_nn(probability.astype(jnp.bfloat16), grad)
                key_grad = key_part if key_grad is None else key_grad + key_part
                value_grad = value_part if value_grad is None else value_grad + value_part
                query_grads.append(dot_nn(turned_keys[pair][:, :keys], score_grad))
            k_acc[:keys, shared : shared + HEAD_DIM] += key_grad
            v_acc[:keys, shared : shared + HEAD_DIM] += value_grad
            query_grad = jnp.concatenate(query_grads, axis=0).T * ATTN_MULT
            dq_ref[first:keys, pair * PACK : (pair + 1) * PACK] = turn(
                query_grad, cos_ref[first:keys, :], -sin_ref[first:keys, :], lanes
            ).astype(jnp.bfloat16)
    for first in range(0, seq_len, rows):
        keys = first + rows
        dk_ref[first:keys, :] = turn(
            k_acc[first:keys, :], cos_ref[first:keys, :], -sin_ref[first:keys, :], lanes
        ).astype(jnp.bfloat16)
        dv_ref[first:keys, :] = v_acc[first:keys, :].astype(jnp.bfloat16)


def attend_back_call(
    part, lengths, query, key_rows, value_rows, grad, totals, cosine, sine, held, done
):
    tok_here = query.shape[0]
    seq_len = cosine.shape[0]
    seqs = tok_here // seq_len
    groups = KV_HEADS // 4
    skip = part * groups
    wide = pl.BlockSpec((seq_len, 4 * HEAD_DIM), lambda s, g: (s, g + skip))
    narrow = pl.BlockSpec((seq_len, PACK), lambda s, g: (s, g + skip))
    table = pl.BlockSpec((seq_len, PACK), lambda s, g: (0, 0))
    return pl.pallas_call(
        attend_back_kernel,
        grid=(seqs, groups),
        in_specs=[
            pl.BlockSpec((1, 1), lambda s, g: (s, 0), memory_space=pltpu.SMEM),
            wide,
            narrow,
            narrow,
            wide,
            pl.BlockSpec((1, 8, seq_len), lambda s, g: (g + skip, 0, s)),
            table,
            table,
        ]
        + [pl.BlockSpec(memory_space=pl.ANY)] * (len(held) + len(done)),
        out_specs=[wide, narrow, narrow],
        out_shape=[
            jax.ShapeDtypeStruct((tok_here, HEADS * HEAD_DIM), jnp.bfloat16),
            jax.ShapeDtypeStruct((tok_here, KV_HEADS * HEAD_DIM), jnp.bfloat16),
            jax.ShapeDtypeStruct((tok_here, KV_HEADS * HEAD_DIM), jnp.bfloat16),
        ],
        input_output_aliases={8 + index: index for index in range(len(held))},
        scratch_shapes=[
            pltpu.VMEM((seq_len, PACK), jnp.float32),
            pltpu.VMEM((seq_len, PACK), jnp.float32),
        ],
        compiler_params=pltpu.CompilerParams(
            dimension_semantics=("arbitrary", "arbitrary"), vmem_limit_bytes=40 * 1024 * 1024
        ),
        cost_estimate=pl.CostEstimate(
            flops=24_000_000_000, bytes_accessed=8_000_000, transcendentals=6_000_000
        ),
        name="attend_back",
    )(
        lengths.reshape(seqs, 1),
        query,
        key_rows,
        value_rows,
        grad,
        totals,
        cosine,
        sine,
        *held,
        *done,
    )


def expert_kernel(waits, first, *refs):
    n2_ref, n2t_ref, dy_ref, gate_ref = refs[:4]
    wb_own_ref, wb_other_ref, wg_own_ref, wg_other_ref = refs[4:8]
    outs = refs[8 + waits :]
    own_ref, pair_ref, dgate_ref, grad_own_ref, grad_other_ref = outs[:5]
    m_acc, dn_acc, g_acc, u_acc, d_acc = outs[5:]
    step = pl.program_id(0)
    block = pl.program_id(1)
    blocks = pl.num_programs(1)
    rows = n2_ref.shape[0]
    place = pl.ds(pl.multiple_of(block * rows, rows), rows)
    lane = lax.broadcasted_iota(jnp.int32, (rows, PACK), 1)
    wg_own, wg_other = wg_own_ref[0, 0], wg_other_ref[0, 0]
    wu_own, wu_other = wb_own_ref[0, 0], wb_other_ref[0, 0]
    wd_own, wd_other = wb_own_ref[1, 0], wb_other_ref[1, 0]
    column = lane == step + first
    gate = jnp.sum(jnp.where(column, gate_ref[...], 0.0), axis=1, keepdims=True)
    dm = RESID_MULT * dy_ref[...].astype(jnp.float32)
    dout = (gate * dm).astype(jnp.bfloat16)
    ug = dot_nn(n2_ref[:, :HALF], wg_own) + dot_nn(n2_ref[:, HALF:], wg_other)
    uu = dot_nn(n2_ref[:, :HALF], wu_own) + dot_nn(n2_ref[:, HALF:], wu_other)
    dh = dot_nn(dout[:, :HALF], wd_own) + dot_nn(dout[:, HALF:], wd_other)
    sig = 1.0 / (1.0 + jnp.exp(-ug))
    silu = ug * sig
    hidden = (silu * uu).astype(jnp.bfloat16)
    dug = (dh * uu * sig * (1.0 + ug * (1.0 - sig))).astype(jnp.bfloat16)
    duu = (dh * silu).astype(jnp.bfloat16)
    y_own = dot_nt(hidden, wd_own)
    y_other = dot_nt(hidden, wd_other)
    n2t = n2t_ref[...]
    g_acc[...] = jnp.where(block == 0, 0.0, g_acc[...]) + dot_nn(n2t, dug)
    dgate = jnp.sum(dm[:, :HALF] * y_own, axis=1, keepdims=True) + jnp.sum(
        dm[:, HALF:] * y_other, axis=1, keepdims=True
    )
    dgate_ref[place, :] = jnp.where(
        column, dgate, jnp.where(step == 0, 0.0, dgate_ref[place, :])
    )
    m_acc[place, :HALF] = jnp.where(step == 0, 0.0, m_acc[place, :HALF]) + gate * y_own
    m_acc[place, HALF:] = jnp.where(step == 0, 0.0, m_acc[place, HALF:]) + gate * y_other
    u_acc[...] = jnp.where(block == 0, 0.0, u_acc[...]) + dot_nn(n2t, duu)
    dn_acc[place, :HALF] = (
        jnp.where(step == 0, 0.0, dn_acc[place, :HALF]) + dot_nt(dug, wg_own) + dot_nt(duu, wu_own)
    )
    dn_acc[place, HALF:] = (
        jnp.where(step == 0, 0.0, dn_acc[place, HALF:])
        + dot_nt(dug, wg_other)
        + dot_nt(duu, wu_other)
    )
    d_acc[...] = jnp.where(block == 0, 0.0, d_acc[...]) + dot_tn(hidden, dout)
    last = step == pl.num_programs(0) - 1

    @pl.when(last & (block < blocks // 2))
    def _():
        own_ref[0] = m_acc[place, :].astype(jnp.bfloat16)
        own_ref[1] = dn_acc[place, :].astype(jnp.bfloat16)

    @pl.when(last & (block >= blocks // 2))
    def _():
        pair_ref[0] = m_acc[place, :].astype(jnp.bfloat16)
        pair_ref[1] = dn_acc[place, :].astype(jnp.bfloat16)

    @pl.when(block == blocks - 1)
    def _():
        grad_own_ref[0, 0] = g_acc[:HALF, :].astype(jnp.bfloat16)
        grad_own_ref[1, 0] = u_acc[:HALF, :].astype(jnp.bfloat16)
        grad_own_ref[2, 0] = d_acc[:, :HALF].astype(jnp.bfloat16)
        grad_other_ref[0, 0] = g_acc[HALF:, :].astype(jnp.bfloat16)
        grad_other_ref[1, 0] = u_acc[HALF:, :].astype(jnp.bfloat16)
        grad_other_ref[2, 0] = d_acc[:, HALF:].astype(jnp.bfloat16)


def expert_call(first, n2, n2t, dy, gates, weights, done):
    tokens_all = n2.shape[0]
    rows = min(512, tokens_all // 2)
    half_blocks = tokens_all // rows // 2
    steps = weights[0].shape[1]

    def own_block(step, block):
        return (0, jnp.where(step == steps - 1, jnp.minimum(block, half_blocks - 1), 0), 0)

    def pair_block(step, block):
        return (0, jnp.where(step == steps - 1, jnp.maximum(block - half_blocks, 0), 0), 0)

    low = jnp.bfloat16

    def pieces(kinds):
        return pl.BlockSpec((kinds, 1, HALF, FF), lambda s, b: (0, s, 0, 0))

    half_shape = jax.ShapeDtypeStruct((2, tokens_all // 2, D), low)
    piece_shape = jax.ShapeDtypeStruct((3, steps, HALF, FF), low)
    outputs = pl.pallas_call(
        functools.partial(expert_kernel, len(done), first),
        grid=(steps, 2 * half_blocks),
        in_specs=[
            pl.BlockSpec((rows, D), lambda s, b: (b, 0)),
            pl.BlockSpec((D, rows), lambda s, b: (0, b)),
            pl.BlockSpec((rows, D), lambda s, b: (b, 0)),
            pl.BlockSpec((rows, PACK), lambda s, b: (b, 0)),
            pieces(2),
            pieces(2),
            pieces(1),
            pieces(1),
        ]
        + [pl.BlockSpec(memory_space=pl.ANY)] * len(done),
        out_specs=[
            pl.BlockSpec((2, rows, D), own_block, pipeline_mode=pl.Buffered(1)),
            pl.BlockSpec((2, rows, D), pair_block, pipeline_mode=pl.Buffered(1)),
            pl.BlockSpec((tokens_all, PACK), lambda s, b: (0, 0)),
            pieces(3),
            pieces(3),
        ],
        out_shape=[
            half_shape,
            half_shape,
            jax.ShapeDtypeStruct((tokens_all, PACK), jnp.float32),
            piece_shape,
            piece_shape,
        ],
        scratch_shapes=[
            pltpu.VMEM((tokens_all, D), jnp.float32),
            pltpu.VMEM((tokens_all, D), jnp.float32),
            pltpu.VMEM((D, FF), jnp.float32),
            pltpu.VMEM((D, FF), jnp.float32),
            pltpu.VMEM((FF, D), jnp.float32),
        ],
        compiler_params=pltpu.CompilerParams(
            dimension_semantics=("arbitrary", "arbitrary"), vmem_limit_bytes=60 * 1024 * 1024
        ),
        cost_estimate=pl.CostEstimate(
            flops=9 * 2 * tokens_all * D * FF * steps * 3 // 2,
            bytes_accessed=48 * 1024 * 1024,
            transcendentals=steps * tokens_all * FF,
        ),
        name="experts",
    )(n2, n2t, dy, gates, *weights, *done)
    return outputs


def high_dot(left_side, right_side):
    return jnp.matmul(left_side, right_side, precision=lax.Precision.HIGH)


def gram_of(rows):
    return jnp.einsum("...oe,...ol->...el", rows, rows, precision=lax.Precision.HIGH)


def polynomial(gram):
    eye = jnp.eye(gram.shape[-1], dtype=jnp.float32)
    return POLY_ONE * eye + POLY_TWO * gram + POLY_THREE * high_dot(gram, gram)


def ortho_rows(own_rows, all_rows):
    squares = jnp.sum(all_rows * all_rows, axis=(-2, -1), keepdims=True)
    scale = 1.0 / (jnp.sqrt(squares) + ORTHO_EPS)
    gram = gram_of(all_rows * scale)
    product = None
    for iteration in range(5):
        factor = polynomial(gram)
        product = factor if product is None else high_dot(product, factor)
        if iteration < 4:
            gram = high_dot(high_dot(gram, factor), factor)
    return high_dot(own_rows * scale, product)


def ortho_block(block, gram_mask, halves):
    squares = jnp.sum(block * block, axis=0)
    width = squares.shape[0] // 2
    lower, upper = jnp.sum(squares[:width]), jnp.sum(squares[width:])
    column = jnp.arange(squares.shape[0])
    own = jnp.where(column < width, lower, upper)
    scale = 1.0 / (jnp.sqrt(jnp.where(halves, own, lower + upper)) + ORTHO_EPS)
    iterate = block * scale[None, :]
    for iteration in range(5):
        gram = gram_of(iterate) * gram_mask
        change = POLY_TWO * gram + POLY_THREE * high_dot(gram, gram)
        iterate = POLY_ONE * iterate + high_dot(iterate, change)
    return iterate


def take_half(values, axis, own):
    keep = lax.dynamic_index_in_dim(values, own, axis, keepdims=False)
    send = lax.dynamic_index_in_dim(values, 1 - own, axis, keepdims=False)
    return keep, send


def reduce_to_owner(values, bits, count, place, order):
    left = bits[::-1]
    width = values.shape[1]
    for bit in order:
        before = 2 ** left.index(bit)
        left.remove(bit)
        split = values.reshape(before, 2, values.shape[0] // (2 * before), width)
        keep, send = take_half(split, 1, (place // bit) % 2)
        values = low_add(keep, swap_bit(send, count, bit)).reshape(-1, width)
    return values


def gather_from_owners(values, count, place, order, held=()):
    held = list(held)
    for bit in order:
        other = swap_bit(values, count, bit)
        held.append(bit)
        held.sort(reverse=True)
        after_bits = 2 ** (len(held) - 1 - held.index(bit))
        upper = (place // bit) % 2 == 1
        width = values.shape[1]
        pieces = (2 ** (len(held) - 1) // after_bits, 1, -1, width)
        own, other = values.reshape(pieces), other.reshape(pieces)
        values = jnp.where(
            upper,
            jnp.concatenate([other, own], axis=1),
            jnp.concatenate([own, other], axis=1),
        ).reshape(-1, width)
    return values


def muon_update(weight, ortho):
    return weight * (1.0 - MUON_RATE * WEIGHT_DECAY) - MUON_RATE * MUON_SHAPE * math.sqrt(D) * ortho


def shards(
    tokens,
    out_grad,
    lengths,
    routes,
    attn_weight,
    router_weight,
    expert_weight,
    gains,
    attn_moment,
    router_moment,
    expert_moment,
    gain_first,
    gain_second,
    attn_ema,
    router_ema,
    expert_ema,
    gain_ema,
):
    seqs_here = lengths.shape[0]
    tok_here = tokens.shape[0]
    seq_len = tok_here // seqs_here
    query_width = HEADS * HEAD_DIM
    kv_width = KV_HEADS * HEAD_DIM
    qkv_width = query_width + 2 * kv_width
    n_dp, n_blk = lax.axis_size("dp"), lax.axis_size("blk")
    count = n_dp * n_blk
    place = lax.axis_index(AXES)
    own_rows = expert_weight.shape[1]
    parts = D // own_rows
    half_bit, pair_bit = parts // 2, n_blk
    bit_z, bit_x, bit_y = [bit for bit in bits_below(parts, count) if bit != pair_bit]
    low_bits = bits_below(1, parts)
    upper_half = (place // half_bit) % 2 == 1
    groups = ((0, 0), (1, 0), (1, 1), (0, 1))
    far_bits = [
        far_x * bit_x + far_y * bit_y + far_z * bit_z
        for far_x, far_y in groups
        for far_z in range(2)
    ]
    own_experts = [(place ^ bits) // parts for bits in far_bits]
    pair_experts = [(place ^ pair_bit ^ bits) // parts for bits in far_bits]
    expert_ids = jnp.stack(own_experts + pair_experts)

    def relative(values):
        swapped = jnp.concatenate([values[:, HALF:], values[:, :HALF]], axis=1)
        return jnp.where(upper_half, swapped, values)

    attn_cols = attn_weight.shape[1]
    attn_low = attn_weight.astype(jnp.bfloat16)
    small_low = jnp.concatenate(
        [
            router_weight.astype(jnp.bfloat16),
            gains.astype(jnp.bfloat16).T,
            jnp.zeros((attn_weight.shape[0], PACK - EXPERTS - 2), jnp.bfloat16),
        ],
        axis=1,
    )
    full_packed = lax.all_gather(
        jnp.concatenate([attn_low, small_low], axis=1), AXES, axis=0, tiled=True
    )
    w_query = full_packed[:, :query_width]
    w_shared = full_packed[:, query_width:qkv_width]
    w_out = full_packed[:, qkv_width:attn_cols]
    full_router = full_packed[:, attn_cols : attn_cols + EXPERTS]
    full_gains = full_packed[:, attn_cols + EXPERTS : attn_cols + EXPERTS + 2].T
    early_bits = bits_below(1, half_bit)
    own_half = gather_rows(expert_weight.astype(jnp.bfloat16), 1, count, place, early_bits)
    level_one = (((1, 0, 0), half_bit), ((0, 1, 0), bit_x), ((0, 0, 1), bit_y))
    gather_last = (
        {(1, 1, 0): bit_x, (0, 1, 1): bit_y, (1, 0, 1): bit_y, (1, 1, 1): bit_x},
        {(1, 1, 0): half_bit, (0, 1, 1): bit_y, (1, 0, 1): half_bit, (1, 1, 1): bit_x},
    )
    hop_of = {half_bit: 0, bit_x: 1, bit_y: 2}

    def before_hop(chunk, bit):
        return tuple(
            side ^ 1 if index == hop_of[bit] else side for index, side in enumerate(chunk)
        )

    chunks = [{}, {}]
    before = None
    for part, kinds in enumerate((slice(1, 3), slice(0, 1))):
        own = own_half[kinds]
        if before is not None:
            own = after(own, before)
        before = swap_bit(own, count, bit_z)
        chunks[part][0, 0, 0] = after(jnp.stack([own, before], axis=1), full_packed)
        for chunk, bit in level_one:
            chunks[part][chunk] = swap_bit(chunks[part][0, 0, 0], count, bit)
    for chunk in ((1, 1, 0), (0, 1, 1), (1, 0, 1), (1, 1, 1)):
        for part in range(2):
            bit = gather_last[part][chunk]
            chunks[part][chunk] = swap_bit(chunks[part][before_hop(chunk, bit)], count, bit)
    gain_one = full_gains[0].astype(jnp.float32)
    gain_two = full_gains[1].astype(jnp.float32)
    inputs = tokens.astype(jnp.float32)
    cosine, sine = rotary_tables(seq_len, HEAD_DIM)
    cosine = jnp.concatenate([cosine] * 4, axis=1)
    sine = jnp.concatenate([-sine, sine, -sine, sine], axis=1)
    normed_one, query, key_rows, value_rows = project_call(
        tokens, gain_one[None], full_packed, full_packed, cosine, sine
    )
    position = jnp.arange(seq_len)
    live_rows = (position[None, :] < lengths[:, None]).reshape(tok_here, 1)
    live_grad = jnp.where(live_rows, out_grad, jnp.zeros_like(out_grad))
    live_relative = after(relative(live_grad), normed_one)
    both_grad = jnp.concatenate([live_relative, swap_bit(live_relative, count, pair_bit)])
    rows_each = attn_moment.shape[0]
    block_width = attn_cols // 3

    def spread(values):
        return lax.all_to_all(values, "blk", split_axis=0, concat_axis=0, tiled=True)

    old_pieces = [attn_moment[:, :block_width], attn_moment[:, block_width : 2 * block_width]]
    old_pieces += [
        attn_moment[:, 2 * block_width :],
        jnp.pad(router_moment, ((0, 0), (0, block_width - EXPERTS))),
    ]
    old_tasks = jnp.pad(jnp.stack(old_pieces), ((0, n_blk - 4), (0, 0), (0, 0)))
    old_tasks = spread(old_tasks).reshape(n_blk * rows_each, block_width)
    attended, totals = attend_call(
        lengths,
        query,
        key_rows,
        value_rows,
        seq_len,
        [chunks[1][0, 0, 0], old_tasks],
    )
    branch = plain_dot(attended, w_out, 1, 1)
    branch = after(branch, *[chunks[0][chunk] for chunk, _ in level_one])
    hidden_state = inputs + RESID_MULT * branch
    scale_two = lax.rsqrt(jnp.mean(hidden_state * hidden_state, axis=-1, keepdims=True) + NORM_EPS)
    unit_two = hidden_state * scale_two
    normed_two = (unit_two * gain_two).astype(jnp.bfloat16)
    pick = (jnp.arange(EXPERTS)[:, None] == expert_ids[None, :]).astype(jnp.bfloat16)
    router_here = jnp.dot(full_router, pick, preferred_element_type=jnp.float32).astype(
        jnp.bfloat16
    )
    logits = jnp.dot(normed_two, router_here, preferred_element_type=jnp.float32)
    used = jnp.any(routes[:, :, None] == expert_ids[None, None, :], axis=1)
    chosen_top = jnp.max(jnp.where(used, logits, NEG_FILL), axis=1, keepdims=True)
    exponent = jnp.where(used, jnp.exp(jnp.where(used, logits - chosen_top, 0.0)), 0.0)
    gate_weights = exponent / jnp.sum(exponent, axis=1, keepdims=True)
    second = relative(normed_two)
    other_second = swap_bit(second, count, pair_bit)
    gates_here = jnp.pad(gate_weights[:, :8], ((0, 0), (0, PACK - 8)))
    gates_there = jnp.pad(gate_weights[:, 8:], ((0, 0), (0, PACK - 8)))
    other_gates = swap_bit(gates_there, count, pair_bit)
    both_second = jnp.concatenate([second, other_second])
    turned = second.T
    both_turned = jnp.concatenate([turned, swap_bit(turned, count, pair_bit)], axis=1)
    both_gates = jnp.concatenate([gates_here, other_gates])
    own_parts, pair_parts, dgates = [], [], []
    grads, moved = {}, {}

    def send(chunk, bit):
        moved[chunk] = swap_bit(grads[chunk], count, bit)

    waits = {
        (0, 0): lambda: [chunks[part][0, 1, 0] for part in range(2)]
        + [chunks[part][0, 0, 1] for part in range(2)],
        (1, 0): lambda: [],
        (1, 1): lambda: [moved[1, 0, 0], pair_parts[0]],
        (0, 1): lambda: [moved[1, 1, 0], pair_parts[1]],
    }
    for turn_index, (far_x, far_y) in enumerate(groups):
        weights = [chunks[part][half, far_x, far_y] for part in range(2) for half in range(2)]
        own_part, pair_part, dgate, grad_own, grad_other = expert_call(
            2 * turn_index,
            both_second,
            both_turned,
            both_grad,
            both_gates,
            weights,
            waits[far_x, far_y](),
        )
        own_parts.append(own_part)
        pair_parts.append(swap_bit(pair_part, count, pair_bit))
        dgates.append(dgate)
        grads[0, far_x, far_y] = grad_own
        grads[1, far_x, far_y] = grad_other
        if (far_x, far_y) == (0, 0):
            send((1, 0, 0), half_bit)
        if (far_x, far_y) == (1, 0):
            send((1, 1, 0), half_bit)
        if (far_x, far_y) == (1, 1):
            send((1, 1, 1), bit_x)
            send((0, 1, 1), bit_y)

    def total_of(*pieces):
        total = pieces[0].astype(jnp.float32)
        for piece in pieces[1:]:
            total = total + piece.astype(jnp.float32)
        return total.astype(jnp.bfloat16)

    last_other, grads[0, 0, 1], own_parts[3], dgates[3], *others = (
        lax.optimization_barrier(
            (
                grads[1, 0, 1],
                grads[0, 0, 1],
                own_parts[3],
                dgates[3],
                moved[1, 1, 1],
                moved[0, 1, 1],
                pair_parts[2],
            )
        )
    )
    moved[1, 1, 1], moved[0, 1, 1], pair_parts[2] = others
    half_y = [
        swap_bit(total_of(last_other[kind], moved[1, 1, 1][kind]), count, half_bit)
        for kind in range(3)
    ]
    grads[0, 1, 0] = total_of(grads[0, 1, 0], moved[1, 1, 0], moved[0, 1, 1])
    send((0, 1, 0), bit_x)
    dgate_sum = (dgates[0] + dgates[1]) + (dgates[2] + dgates[3])
    pair_dgates = swap_bit(dgate_sum[tok_here:], count, pair_bit)

    def gather_sum(parts):
        total = None
        for part in parts:
            part = part.astype(jnp.float32)
            total = part if total is None else total + part
        return relative(total)

    grad_normed_two = gather_sum([part[1] for part in own_parts + pair_parts])
    grad_gates = jnp.concatenate([dgate_sum[:tok_here, :8], pair_dgates[:, :8]], axis=1)
    grad_out = live_grad.astype(jnp.float32)
    inner_sum = jnp.sum(gate_weights * grad_gates, axis=1, keepdims=True)
    grad_logits = (gate_weights * (grad_gates - inner_sum)).astype(jnp.bfloat16)
    grad_normed_two = grad_normed_two + plain_dot(grad_logits, router_here, 1, 1)
    grad_router = jnp.matmul(
        plain_dot(normed_two, grad_logits, 0, 0),
        pick.astype(jnp.float32).T,
        precision=lax.Precision.HIGHEST,
    )
    grad_hidden_state = grad_out + norm_back(grad_normed_two, unit_two, scale_two, gain_two)
    grad_gain_two = jnp.sum(grad_normed_two * unit_two, axis=0)
    grad_branch = (RESID_MULT * grad_hidden_state).astype(jnp.bfloat16)
    grad_w_out = plain_dot(grad_branch, attended, 0, 0)
    dp_bits = bits_below(n_blk, count)
    far_dp = [bit for bit in dp_bits if bit not in (pair_bit, bit_x, bit_y)]
    first_x = [pair_bit, bit_x, bit_y] + far_dp
    first_y = [pair_bit, bit_y, bit_x] + far_dp

    def to_dp(values, order):
        return reduce_to_owner(values, dp_bits, count, place, order)

    low_grad_out = pin(grad_w_out.astype(jnp.bfloat16))
    grad_attended = jnp.dot(grad_branch, w_out, preferred_element_type=jnp.float32).astype(
        jnp.bfloat16
    )
    last_own = after(grads[0, 0, 1], grad_attended)
    from_y = [
        swap_bit(total_of(last_own[kind], half_y[kind]), count, bit_y) for kind in range(3)
    ]
    def attend_back(part, held, done):
        return attend_back_call(
            part,
            lengths,
            query,
            key_rows,
            value_rows,
            grad_attended,
            totals,
            cosine,
            sine,
            held,
            done,
        )

    grad_query, grad_key, grad_value = attend_back(
        1, attend_back(0, [], half_y), [moved[0, 1, 0]]
    )
    late_parts = after(tuple(own_parts + pair_parts), grad_query)
    block_out = (hidden_state + RESID_MULT * gather_sum([part[0] for part in late_parts])).astype(
        jnp.bfloat16
    )
    low_grad = [
        pin(plain_dot(normed_one, piece, 0, 0).astype(jnp.bfloat16))
        for piece in (grad_query, grad_key, grad_value)
    ]
    nearest = after(grads[0, 0, 0], low_grad[0])
    expert_sums = [
        total_of(nearest[kind], moved[1, 0, 0][kind], moved[0, 1, 0][kind], from_y[kind])
        for kind in range(3)
    ]
    late_query = after(grad_query, *from_y)
    grad_normed_one = (
        plain_dot(late_query, w_query, 1, 1)
        + plain_dot(grad_key, w_shared[:, :kv_width], 1, 1)
        + plain_dot(grad_value, w_shared[:, kv_width:], 1, 1)
    )
    scale_one = lax.rsqrt(jnp.mean(inputs * inputs, axis=-1, keepdims=True) + NORM_EPS)
    unit_one = inputs * scale_one
    input_grad = grad_hidden_state + norm_back(grad_normed_one, unit_one, scale_one, gain_one)
    grad_gain_one = jnp.sum(grad_normed_one * unit_one, axis=0)
    grad_small = jnp.concatenate(
        [
            grad_router,
            jnp.stack([grad_gain_one, grad_gain_two], axis=1),
            jnp.zeros((D, PACK - EXPERTS - 2), jnp.float32),
        ],
        axis=1,
    ).astype(jnp.bfloat16)
    query_sum = to_dp(low_grad[0], first_x)
    shared_sum = to_dp(jnp.concatenate([low_grad[1], low_grad[2], pin(grad_small)], axis=1), first_y)
    out_sum = to_dp(after(low_grad_out, grad_query), first_x)

    def as_tasks(first, second, third, small):
        small = jnp.pad(small, ((0, 0), (0, block_width - PACK)))
        tasks = jnp.stack([first, second, third, small])
        return jnp.pad(tasks, ((0, n_blk - 4), (0, 0), (0, 0)))

    task_parts = spread(
        as_tasks(
            query_sum, shared_sum[:, :block_width], out_sum, shared_sum[:, block_width:]
        )
    )
    task_block = MOMENTUM * old_tasks + jnp.sum(task_parts.astype(jnp.float32), axis=0)
    moment_rows = spread(task_block.reshape(n_blk, rows_each, block_width))
    moment_attn = jnp.concatenate([moment_rows[0], moment_rows[1], moment_rows[2]], axis=1)
    moment_router = moment_rows[3][:, :EXPERTS]
    gain_grad = moment_rows[3][:, EXPERTS : EXPERTS + 2].T
    used_columns = (jnp.arange(block_width) < EXPERTS) | (lax.axis_index("blk") != 3)
    task_block = jnp.where(used_columns, task_block, 0.0)
    wide_x, wide_y = far_dp + [bit_y, bit_x], far_dp + [bit_x, bit_y]
    sides = [
        gather_from_owners(task_block[:, : block_width // 2], count, place, wide_x),
        gather_from_owners(task_block[:, block_width // 2 :], count, place, wide_y),
    ]
    moment_expert, ortho_expert = [], []
    for kind in range(3):
        total = expert_sums[kind]
        total = total[0].astype(jnp.float32) + swap_bit(total[1], count, bit_z).astype(jnp.float32)
        total = total.T if kind == 2 else total
        if early_bits:
            total = reduce_rows(total.astype(jnp.bfloat16), count, place, early_bits[::-1])
        moment = MOMENTUM * expert_moment[kind] + total.astype(jnp.float32)
        group_rows = moment
        for bit in low_bits:
            group_rows = jnp.concatenate([group_rows, swap_bit(group_rows, count, bit)])
        if kind == 1:
            group_rows = after(group_rows, task_block)
        if kind == 2:
            group_rows = after(group_rows, *sides)
        moment_expert.append(moment)
        ortho_expert.append(ortho_rows(moment, group_rows))
    attn_block = jnp.concatenate(
        [gather_from_owners(side, count, place, [pair_bit], wide_x) for side in sides], axis=1
    )
    column_half = jnp.arange(block_width) >= block_width // 2
    halves = lax.axis_index("blk") == 1
    gram_mask = jnp.where(
        (column_half[:, None] == column_half[None, :]) | ~halves, 1.0, 0.0
    ).astype(jnp.float32)
    attn_iter = ortho_block(attn_block, gram_mask, halves)
    returned = lax.dynamic_slice_in_dim(
        attn_iter, lax.axis_index("dp") * (n_blk * rows_each), n_blk * rows_each, 0
    )
    returned = spread(returned.reshape(n_blk, rows_each, block_width))
    ortho_attn = jnp.concatenate([returned[0], returned[1], returned[2]], axis=1)
    ortho_router = returned[3][:, :EXPERTS]
    moment_expert = jnp.stack(moment_expert)
    attn_new = muon_update(attn_weight, ortho_attn)
    router_new = muon_update(router_weight, ortho_router)
    expert_new = muon_update(expert_weight, jnp.stack(ortho_expert))
    first_new = BETA_ONE * gain_first + (1.0 - BETA_ONE) * gain_grad
    second_new = BETA_TWO * gain_second + (1.0 - BETA_TWO) * gain_grad * gain_grad
    corrected_first = first_new / (1.0 - BETA_ONE**STEP)
    corrected_second = second_new / (1.0 - BETA_TWO**STEP)
    gain_new = gains - ADAM_RATE * corrected_first / (jnp.sqrt(corrected_second) + ADAM_EPS)
    return (
        block_out,
        input_grad,
        moment_attn,
        moment_router,
        moment_expert,
        attn_new,
        router_new,
        expert_new,
        attn_new.astype(jnp.bfloat16),
        router_new.astype(jnp.bfloat16),
        expert_new.astype(jnp.bfloat16),
        EMA_KEEP * attn_ema + (1.0 - EMA_KEEP) * attn_new,
        EMA_KEEP * router_ema + (1.0 - EMA_KEEP) * router_new,
        EMA_KEEP * expert_ema + (1.0 - EMA_KEEP) * expert_new,
        first_new,
        second_new,
        gain_new,
        gain_new.astype(jnp.bfloat16),
        GAIN_EMA_KEEP * gain_ema + (1.0 - GAIN_EMA_KEEP) * gain_new,
    )


def solution(mesh):
    placed = (
        P(("dp", "blk"), None),
        P(("dp", "blk"), None),
        P(("dp", "blk")),
        P(("dp", "blk"), None),
        P(("dp", "blk"), None),
        P(("dp", "blk"), None),
        P(None, ("dp", "blk"), None),
        P(None, ("dp", "blk")),
        P(("dp", "blk"), None),
        P(("dp", "blk"), None),
        P(None, ("dp", "blk"), None),
        P(None, ("dp", "blk")),
        P(None, ("dp", "blk")),
        P(("dp", "blk"), None),
        P(("dp", "blk"), None),
        P(None, ("dp", "blk"), None),
        P(None, ("dp", "blk")),
    )
    return jax.shard_map(
        shards,
        mesh=mesh,
        in_specs=placed,
        out_specs=(
            P(("dp", "blk"), None),
            P(("dp", "blk"), None),
            P(("dp", "blk"), None),
            P(("dp", "blk"), None),
            P(None, ("dp", "blk"), None),
            P(("dp", "blk"), None),
            P(("dp", "blk"), None),
            P(None, ("dp", "blk"), None),
            P(("dp", "blk"), None),
            P(("dp", "blk"), None),
            P(None, ("dp", "blk"), None),
            P(("dp", "blk"), None),
            P(("dp", "blk"), None),
            P(None, ("dp", "blk"), None),
            P(None, ("dp", "blk")),
            P(None, ("dp", "blk")),
            P(None, ("dp", "blk")),
            P(None, ("dp", "blk")),
            P(None, ("dp", "blk")),
        ),
        check_vma=False,
    )
```

```python
import functools
import math

import jax
import jax.numpy as jnp
from jax import lax
from jax.experimental import pallas as pl
from jax.experimental.layout import Layout, with_layout_constraint
from jax.experimental.pallas import tpu as pltpu
from jax.sharding import PartitionSpec as P

D = 1024
HEADS = 16
KV_HEADS = 8
HEAD_DIM = 64
FF = 512
TOP = 8
EXPERTS = 16
STEP = 10
HALF = D // 2
PACK = 128
AXES = ("dp", "blk")


NORM_EPS = 1e-05
ATTN_MULT = 0.015625
RESID_MULT = 0.22
ROPE_BASE = 10000.0
NEG_FILL = -1e30
POLY_ONE = 3.4445
POLY_TWO = -4.775
POLY_THREE = 2.0315
ORTHO_EPS = 1e-07
MOMENTUM = 0.95
MUON_RATE = 0.6
MUON_SHAPE = 0.2
WEIGHT_DECAY = 0.01
ADAM_RATE = 0.8
BETA_ONE = 0.9
BETA_TWO = 0.95
ADAM_EPS = 1e-08
EMA_KEEP = 0.9
GAIN_EMA_KEEP = 0.6


def plain_dot(left_side, right_side, contract_left, contract_right):
    return lax.dot_general(
        left_side,
        right_side,
        (((contract_left,), (contract_right,)), ((), ())),
        preferred_element_type=jnp.float32,
    )


def rotary_tables(length, head_width):
    position = jnp.arange(length).astype(jnp.float32)
    inverse = ROPE_BASE ** (-jnp.arange(0, head_width, 2).astype(jnp.float32) / head_width)
    angles = position[:, None] * inverse[None, :]
    return (jnp.cos(angles), jnp.sin(angles))


def norm_back(grad_normed, unit_rows, scale_rows, gain_row):
    grad_unit = grad_normed * gain_row
    return scale_rows * (
        grad_unit - unit_rows * jnp.mean(grad_unit * unit_rows, axis=-1, keepdims=True)
    )


def pin(values):
    return with_layout_constraint(values, Layout(major_to_minor=tuple(range(values.ndim))))


def swap_bit(values, count, bit):
    pairs = [(place, place ^ bit) for place in range(count)]
    return pin(lax.ppermute(pin(values), AXES, pairs))


def after(values, *done):
    return lax.optimization_barrier((values,) + done)[0]


def low_add(left_side, right_side):
    return (left_side.astype(jnp.float32) + right_side.astype(jnp.float32)).astype(jnp.bfloat16)


def bits_below(low_bit, high_bit):
    bits = []
    while low_bit < high_bit:
        bits.append(low_bit)
        low_bit *= 2
    return bits


def gather_rows(values, axis, count, place, bits):
    for bit in bits:
        other = swap_bit(values, count, bit)
        upper = (place // bit) % 2 == 1
        values = jnp.where(
            upper,
            jnp.concatenate([other, values], axis=axis),
            jnp.concatenate([values, other], axis=axis),
        )
    return values


def reduce_rows(values, count, place, bits):
    for bit in bits:
        split = values.reshape((2, values.shape[0] // 2) + values.shape[1:])
        own = (place // bit) % 2
        keep = lax.dynamic_index_in_dim(split, own, 0, keepdims=False)
        other = swap_bit(
            lax.dynamic_index_in_dim(split, 1 - own, 0, keepdims=False), count, bit
        )
        values = low_add(keep, other)
    return values


def dot_nn(left_side, right_side):
    return plain_dot(left_side, right_side, 1, 0)


def dot_nt(left_side, right_side):
    return plain_dot(left_side, right_side, 1, 1)


def dot_tn(left_side, right_side):
    return plain_dot(left_side, right_side, 0, 0)


def turn(values, cosine, sine, lanes):
    far = jnp.where(
        lanes % HEAD_DIM < HEAD_DIM // 2,
        pltpu.roll(values, PACK - HEAD_DIM // 2, 1),
        pltpu.roll(values, HEAD_DIM // 2, 1),
    )
    return values * cosine + far * sine


def project_kernel(
    tok_ref, gain_ref, wq_ref, wkv_ref, cos_ref, sin_ref, norm_ref, q_ref, k_ref, v_ref
):
    rows = tok_ref.shape[0]
    inputs = tok_ref[...].astype(jnp.float32)
    scale = lax.rsqrt(jnp.mean(inputs * inputs, axis=-1, keepdims=True) + NORM_EPS)
    normed = (inputs * scale * gain_ref[...]).astype(jnp.bfloat16)
    norm_ref[...] = normed
    cosine, sine = cos_ref[...], sin_ref[...]
    lanes = lax.broadcasted_iota(jnp.int32, (rows, PACK), 1)
    query = dot_nn(normed, wq_ref[...])
    for start in range(0, HEADS * HEAD_DIM, PACK):
        turned = turn(query[:, start : start + PACK], cosine, sine, lanes)
        q_ref[:, start : start + PACK] = turned.astype(jnp.bfloat16) * ATTN_MULT
    both = dot_nn(normed, wkv_ref[...])
    width = KV_HEADS * HEAD_DIM
    for start in range(0, width, PACK):
        turned = turn(both[:, start : start + PACK], cosine, sine, lanes)
        k_ref[:, start : start + PACK] = turned.astype(jnp.bfloat16)
    v_ref[...] = both[:, width:].astype(jnp.bfloat16)


def project_call(tokens, gain_row, wq, wkv, cosine, sine):
    seq_rows = cosine.shape[0]
    rows = min(256, seq_rows)
    repeats = seq_rows // rows
    tok_here = tokens.shape[0]
    width = KV_HEADS * HEAD_DIM
    low = jnp.bfloat16
    return pl.pallas_call(
        project_kernel,
        grid=(tok_here // rows,),
        in_specs=[
            pl.BlockSpec((rows, D), lambda b: (b, 0)),
            pl.BlockSpec((1, D), lambda b: (0, 0)),
            pl.BlockSpec((D, HEADS * HEAD_DIM), lambda b: (0, 0)),
            pl.BlockSpec((D, 2 * width), lambda b: (0, 1)),
            pl.BlockSpec((rows, PACK), lambda b: (b % repeats, 0)),
            pl.BlockSpec((rows, PACK), lambda b: (b % repeats, 0)),
        ],
        out_specs=[
            pl.BlockSpec((rows, D), lambda b: (b, 0)),
            pl.BlockSpec((rows, HEADS * HEAD_DIM), lambda b: (b, 0)),
            pl.BlockSpec((rows, width), lambda b: (b, 0)),
            pl.BlockSpec((rows, width), lambda b: (b, 0)),
        ],
        out_shape=[
            jax.ShapeDtypeStruct((tok_here, D), low),
            jax.ShapeDtypeStruct((tok_here, HEADS * HEAD_DIM), low),
            jax.ShapeDtypeStruct((tok_here, width), low),
            jax.ShapeDtypeStruct((tok_here, width), low),
        ],
        compiler_params=pltpu.CompilerParams(
            dimension_semantics=("arbitrary",), vmem_limit_bytes=40 * 1024 * 1024
        ),
        cost_estimate=pl.CostEstimate(
            flops=8_000_000_000, bytes_accessed=14_000_000, transcendentals=0
        ),
        name="project",
    )(tokens, gain_row, wq, wkv, cosine, sine)


def attend_kernel(len_ref, q_ref, k_ref, v_ref, *refs):
    o_ref, lse_ref = refs[-2:]
    seq_len = q_ref.shape[0]
    rows = min(256, seq_len)
    length = len_ref[0, 0]
    for first in range(0, seq_len, rows):
        keys = first + rows
        key_index = lax.broadcasted_iota(jnp.int32, (rows, keys), 1)
        query_index = first + lax.broadcasted_iota(jnp.int32, (rows, keys), 0)
        bias = jnp.where((key_index <= query_index) & (key_index < length), 0.0, NEG_FILL)
        lanes = lax.broadcasted_iota(jnp.int32, (rows, PACK), 1)
        totals = jnp.zeros((rows, PACK), jnp.float32)
        for head in range(4):
            shared = (head // 2) * HEAD_DIM
            key_rows = k_ref[:keys, shared : shared + HEAD_DIM]
            value_rows = v_ref[:keys, shared : shared + HEAD_DIM]
            query = q_ref[first:keys, head * HEAD_DIM : (head + 1) * HEAD_DIM]
            scores = dot_nt(query, key_rows) + bias
            largest = jnp.max(scores, axis=1, keepdims=True)
            exponent = jnp.exp(scores - largest)
            total = jnp.sum(exponent, axis=1, keepdims=True)
            probability = (exponent * (1.0 / total)).astype(jnp.bfloat16)
            o_ref[first:keys, head * HEAD_DIM : (head + 1) * HEAD_DIM] = dot_nn(
                probability, value_rows
            ).astype(jnp.bfloat16)
            totals = jnp.where(lanes == head, largest + jnp.log(total), totals)
        lse_ref[0, :, first:keys] = totals.T[:8]


def attend_call(lengths, query, key_rows, value_rows, seq_len, done):
    tok_here = query.shape[0]
    seqs = tok_here // seq_len
    groups = KV_HEADS // 2
    return pl.pallas_call(
        attend_kernel,
        grid=(seqs, groups),
        in_specs=[
            pl.BlockSpec((1, 1), lambda s, g: (s, 0), memory_space=pltpu.SMEM),
            pl.BlockSpec((seq_len, 4 * HEAD_DIM), lambda s, g: (s, g)),
            pl.BlockSpec((seq_len, PACK), lambda s, g: (s, g)),
            pl.BlockSpec((seq_len, PACK), lambda s, g: (s, g)),
        ]
        + [pl.BlockSpec(memory_space=pl.ANY)] * len(done),
        out_specs=[
            pl.BlockSpec((seq_len, 4 * HEAD_DIM), lambda s, g: (s, g)),
            pl.BlockSpec((1, 8, seq_len), lambda s, g: (g, 0, s)),
        ],
        out_shape=[
            jax.ShapeDtypeStruct((tok_here, HEADS * HEAD_DIM), jnp.bfloat16),
            jax.ShapeDtypeStruct((groups, 8, tok_here), jnp.float32),
        ],
        compiler_params=pltpu.CompilerParams(
            dimension_semantics=("arbitrary", "arbitrary"), vmem_limit_bytes=40 * 1024 * 1024
        ),
        cost_estimate=pl.CostEstimate(
            flops=20_000_000_000, bytes_accessed=8_000_000, transcendentals=12_000_000
        ),
        name="attend",
    )(lengths.reshape(seqs, 1), query, key_rows, value_rows, *done)


def attend_back_kernel(
    len_ref,
    q_ref,
    k_ref,
    v_ref,
    do_ref,
    lse_ref,
    cos_ref,
    sin_ref,
    *refs,
):
    dq_ref, dk_ref, dv_ref, k_acc, v_acc = refs[-5:]
    seq_len = q_ref.shape[0]
    rows = min(256, seq_len)
    length = len_ref[0, 0]
    k_acc[...] = jnp.zeros_like(k_acc)
    v_acc[...] = jnp.zeros_like(v_acc)
    lanes = lax.broadcasted_iota(jnp.int32, (rows, PACK), 1)
    turned_keys = [
        k_ref[:, shared : shared + HEAD_DIM].T for shared in (0, HEAD_DIM)
    ]
    for first in range(0, seq_len, rows):
        keys = first + rows
        key_index = lax.broadcasted_iota(jnp.int32, (keys, rows), 0)
        query_index = first + lax.broadcasted_iota(jnp.int32, (keys, rows), 1)
        bias = jnp.where((key_index <= query_index) & (key_index < length), 0.0, NEG_FILL)
        for pair in range(2):
            shared = pair * HEAD_DIM
            key_rows = k_ref[:keys, shared : shared + HEAD_DIM]
            value_rows = v_ref[:keys, shared : shared + HEAD_DIM]
            key_grad = None
            value_grad = None
            query_grads = []
            for head in (2 * pair, 2 * pair + 1):
                query = q_ref[first:keys, head * HEAD_DIM : (head + 1) * HEAD_DIM]
                grad = do_ref[first:keys, head * HEAD_DIM : (head + 1) * HEAD_DIM]
                scores = dot_nt(key_rows, query) + bias
                probability = jnp.exp(scores - lse_ref[0, head : head + 1, first:keys])
                prob_grad = dot_nt(value_rows, grad)
                inner = jnp.sum(probability * prob_grad, axis=0, keepdims=True)
                score_grad = (probability * (prob_grad - inner)).astype(jnp.bfloat16)
                key_part = dot_nn(score_grad, query)
                value_part = dot_nn(probability.astype(jnp.bfloat16), grad)
                key_grad = key_part if key_grad is None else key_grad + key_part
                value_grad = value_part if value_grad is None else value_grad + value_part
                query_grads.append(dot_nn(turned_keys[pair][:, :keys], score_grad))
            k_acc[:keys, shared : shared + HEAD_DIM] += key_grad
            v_acc[:keys, shared : shared + HEAD_DIM] += value_grad
            query_grad = jnp.concatenate(query_grads, axis=0).T * ATTN_MULT
            dq_ref[first:keys, pair * PACK : (pair + 1) * PACK] = turn(
                query_grad, cos_ref[first:keys, :], -sin_ref[first:keys, :], lanes
            ).astype(jnp.bfloat16)
    for first in range(0, seq_len, rows):
        keys = first + rows
        dk_ref[first:keys, :] = turn(
            k_acc[first:keys, :], cos_ref[first:keys, :], -sin_ref[first:keys, :], lanes
        ).astype(jnp.bfloat16)
        dv_ref[first:keys, :] = v_acc[first:keys, :].astype(jnp.bfloat16)


def attend_back_call(
    part, lengths, query, key_rows, value_rows, grad, totals, cosine, sine, held, done
):
    tok_here = query.shape[0]
    seq_len = cosine.shape[0]
    seqs = tok_here // seq_len
    groups = KV_HEADS // 4
    skip = part * groups
    wide = pl.BlockSpec((seq_len, 4 * HEAD_DIM), lambda s, g: (s, g + skip))
    narrow = pl.BlockSpec((seq_len, PACK), lambda s, g: (s, g + skip))
    table = pl.BlockSpec((seq_len, PACK), lambda s, g: (0, 0))
    return pl.pallas_call(
        attend_back_kernel,
        grid=(seqs, groups),
        in_specs=[
            pl.BlockSpec((1, 1), lambda s, g: (s, 0), memory_space=pltpu.SMEM),
            wide,
            narrow,
            narrow,
            wide,
            pl.BlockSpec((1, 8, seq_len), lambda s, g: (g + skip, 0, s)),
            table,
            table,
        ]
        + [pl.BlockSpec(memory_space=pl.ANY)] * (len(held) + len(done)),
        out_specs=[wide, narrow, narrow],
        out_shape=[
            jax.ShapeDtypeStruct((tok_here, HEADS * HEAD_DIM), jnp.bfloat16),
            jax.ShapeDtypeStruct((tok_here, KV_HEADS * HEAD_DIM), jnp.bfloat16),
            jax.ShapeDtypeStruct((tok_here, KV_HEADS * HEAD_DIM), jnp.bfloat16),
        ],
        input_output_aliases={8 + index: index for index in range(len(held))},
        scratch_shapes=[
            pltpu.VMEM((seq_len, PACK), jnp.float32),
            pltpu.VMEM((seq_len, PACK), jnp.float32),
        ],
        compiler_params=pltpu.CompilerParams(
            dimension_semantics=("arbitrary", "arbitrary"), vmem_limit_bytes=40 * 1024 * 1024
        ),
        cost_estimate=pl.CostEstimate(
            flops=24_000_000_000, bytes_accessed=8_000_000, transcendentals=6_000_000
        ),
        name="attend_back",
    )(
        lengths.reshape(seqs, 1),
        query,
        key_rows,
        value_rows,
        grad,
        totals,
        cosine,
        sine,
        *held,
        *done,
    )


def expert_kernel(waits, first, *refs):
    n2_ref, dy_ref, gate_ref = refs[:3]
    wg_own_ref, wg_other_ref, wb_own_ref, wb_other_ref = refs[3:7]
    outs = refs[7 + waits :]
    own_ref, pair_ref, dgate_ref, grad_own_ref, grad_other_ref = outs[:5]
    m_acc, dn_acc, g_acc, u_acc, d_acc, turned_ref = outs[5:]
    step = pl.program_id(0)
    block = pl.program_id(1)
    blocks = pl.num_programs(1)
    rows = n2_ref.shape[0]
    place = pl.ds(pl.multiple_of(block * rows, rows), rows)
    lane = lax.broadcasted_iota(jnp.int32, (rows, PACK), 1)

    @pl.when(step == 0)
    def _():
        turned_ref[:, place] = n2_ref[...].T

    wg_own, wg_other = wg_own_ref[0, 0], wg_other_ref[0, 0]
    wu_own, wu_other = wb_own_ref[0, 0], wb_other_ref[0, 0]
    wd_own, wd_other = wb_own_ref[1, 0], wb_other_ref[1, 0]
    column = lane == step + first
    gate = jnp.sum(jnp.where(column, gate_ref[...], 0.0), axis=1, keepdims=True)
    dm = RESID_MULT * dy_ref[...].astype(jnp.float32)
    dout = (gate * dm).astype(jnp.bfloat16)
    ug = dot_nn(n2_ref[:, :HALF], wg_own) + dot_nn(n2_ref[:, HALF:], wg_other)
    uu = dot_nn(n2_ref[:, :HALF], wu_own) + dot_nn(n2_ref[:, HALF:], wu_other)
    dh = dot_nn(dout[:, :HALF], wd_own) + dot_nn(dout[:, HALF:], wd_other)
    sig = 1.0 / (1.0 + jnp.exp(-ug))
    silu = ug * sig
    hidden = (silu * uu).astype(jnp.bfloat16)
    dug = (dh * uu * sig * (1.0 + ug * (1.0 - sig))).astype(jnp.bfloat16)
    duu = (dh * silu).astype(jnp.bfloat16)
    y_own = dot_nt(hidden, wd_own)
    y_other = dot_nt(hidden, wd_other)
    n2t = turned_ref[:, place]
    g_acc[...] = jnp.where(block == 0, 0.0, g_acc[...]) + dot_nn(n2t, dug)
    dgate = jnp.sum(dm[:, :HALF] * y_own, axis=1, keepdims=True) + jnp.sum(
        dm[:, HALF:] * y_other, axis=1, keepdims=True
    )
    dgate_ref[place, :] = jnp.where(
        column, dgate, jnp.where(step == 0, 0.0, dgate_ref[place, :])
    )
    m_acc[place, :HALF] = jnp.where(step == 0, 0.0, m_acc[place, :HALF]) + gate * y_own
    m_acc[place, HALF:] = jnp.where(step == 0, 0.0, m_acc[place, HALF:]) + gate * y_other
    u_acc[...] = jnp.where(block == 0, 0.0, u_acc[...]) + dot_nn(n2t, duu)
    dn_acc[place, :HALF] = (
        jnp.where(step == 0, 0.0, dn_acc[place, :HALF]) + dot_nt(dug, wg_own) + dot_nt(duu, wu_own)
    )
    dn_acc[place, HALF:] = (
        jnp.where(step == 0, 0.0, dn_acc[place, HALF:])
        + dot_nt(dug, wg_other)
        + dot_nt(duu, wu_other)
    )
    d_acc[...] = jnp.where(block == 0, 0.0, d_acc[...]) + dot_tn(hidden, dout)
    last = step == pl.num_programs(0) - 1

    @pl.when(last & (block < blocks // 2))
    def _():
        own_ref[0] = m_acc[place, :].astype(jnp.bfloat16)
        own_ref[1] = dn_acc[place, :].astype(jnp.bfloat16)

    @pl.when(last & (block >= blocks // 2))
    def _():
        pair_ref[0] = m_acc[place, :].astype(jnp.bfloat16)
        pair_ref[1] = dn_acc[place, :].astype(jnp.bfloat16)

    @pl.when(block == blocks - 1)
    def _():
        grad_own_ref[0, 0] = g_acc[:HALF, :].astype(jnp.bfloat16)
        grad_own_ref[1, 0] = u_acc[:HALF, :].astype(jnp.bfloat16)
        grad_own_ref[2, 0] = d_acc[:, :HALF].astype(jnp.bfloat16)
        grad_other_ref[0, 0] = g_acc[HALF:, :].astype(jnp.bfloat16)
        grad_other_ref[1, 0] = u_acc[HALF:, :].astype(jnp.bfloat16)
        grad_other_ref[2, 0] = d_acc[:, HALF:].astype(jnp.bfloat16)


def expert_call(first, n2, dy, gates, weights, done):
    tokens_all = n2.shape[0]
    rows = min(512, tokens_all // 2)
    half_blocks = tokens_all // rows // 2
    steps = weights[0].shape[1]

    def own_block(step, block):
        return (0, jnp.where(step == steps - 1, jnp.minimum(block, half_blocks - 1), 0), 0)

    def pair_block(step, block):
        return (0, jnp.where(step == steps - 1, jnp.maximum(block - half_blocks, 0), 0), 0)

    low = jnp.bfloat16

    def pieces(kinds):
        return pl.BlockSpec((kinds, 1, HALF, FF), lambda s, b: (0, s, 0, 0))

    half_shape = jax.ShapeDtypeStruct((2, tokens_all // 2, D), low)
    piece_shape = jax.ShapeDtypeStruct((3, steps, HALF, FF), low)
    outputs = pl.pallas_call(
        functools.partial(expert_kernel, len(done), first),
        grid=(steps, 2 * half_blocks),
        in_specs=[
            pl.BlockSpec((rows, D), lambda s, b: (b, 0)),
            pl.BlockSpec((rows, D), lambda s, b: (b, 0)),
            pl.BlockSpec((rows, PACK), lambda s, b: (b, 0)),
            pieces(1),
            pieces(1),
            pieces(2),
            pieces(2),
        ]
        + [pl.BlockSpec(memory_space=pl.ANY)] * len(done),
        out_specs=[
            pl.BlockSpec((2, rows, D), own_block, pipeline_mode=pl.Buffered(1)),
            pl.BlockSpec((2, rows, D), pair_block, pipeline_mode=pl.Buffered(1)),
            pl.BlockSpec((tokens_all, PACK), lambda s, b: (0, 0)),
            pieces(3),
            pieces(3),
        ],
        out_shape=[
            half_shape,
            half_shape,
            jax.ShapeDtypeStruct((tokens_all, PACK), jnp.float32),
            piece_shape,
            piece_shape,
        ],
        scratch_shapes=[
            pltpu.VMEM((tokens_all, D), jnp.float32),
            pltpu.VMEM((tokens_all, D), jnp.float32),
            pltpu.VMEM((D, FF), jnp.float32),
            pltpu.VMEM((D, FF), jnp.float32),
            pltpu.VMEM((FF, D), jnp.float32),
            pltpu.VMEM((D, tokens_all), low),
        ],
        compiler_params=pltpu.CompilerParams(
            dimension_semantics=("arbitrary", "arbitrary"), vmem_limit_bytes=62 * 1024 * 1024
        ),
        cost_estimate=pl.CostEstimate(
            flops=9 * 2 * tokens_all * D * FF * steps * 3 // 2,
            bytes_accessed=48 * 1024 * 1024,
            transcendentals=steps * tokens_all * FF,
        ),
        name="experts",
    )(n2, dy, gates, *weights, *done)
    return outputs


def split_high(values):
    high = values.astype(jnp.bfloat16)
    return high, (values - high.astype(jnp.float32)).astype(jnp.bfloat16)


def triple_dot(left_side, right_side):
    left_high, left_low = left_side
    right_high, right_low = right_side
    return dot_nn(left_high, right_high) + (
        dot_nn(left_high, right_low) + dot_nn(left_low, right_high)
    )


def symmetric_product(left_pair, right_pair, size, put):
    tile = min(256, size)
    for first in range(0, size, tile):
        rows = slice(first, first + tile)
        part = triple_dot(
            tuple(side[rows, :] for side in left_pair),
            tuple(side[:, first:] for side in right_pair),
        )
        put(rows, slice(first, size), part)
        for second in range(first + tile, size, tile):
            columns = slice(second, second + tile)
            put(columns, rows, part[:, second - first : second - first + tile].T)


def store_pair(pair, rows, columns, values):
    high, low = split_high(values)
    pair[0][rows, columns] = high
    pair[1][rows, columns] = low


def ortho_block_kernel(halves_ref, m_ref, x_ref, xh, xl, th, tl, gram, gh, gl, sh, sl):
    size = m_ref.shape[0]
    tile = 256
    halves = halves_ref[0] == 1
    half = size // 2

    def square_sum(columns):
        total = jnp.zeros((1, half), jnp.float32)
        for first in range(0, size, tile):
            piece = m_ref[first : first + tile, columns]
            total = total + jnp.sum(piece * piece, axis=0, keepdims=True)
        return jnp.sum(total)

    lower, upper = square_sum(slice(0, half)), square_sum(slice(half, size))
    whole = lower + upper

    def scale_of(own):
        squares = jnp.full((1, half), jnp.where(halves, own, whole), jnp.float32)
        return 1.0 / (jnp.sqrt(squares) + ORTHO_EPS)

    for columns, own in ((slice(0, half), lower), (slice(half, size), upper)):
        scale = scale_of(own)
        for first in range(0, size, tile):
            rows = slice(first, first + tile)
            x_ref[rows, columns] = m_ref[rows, columns] * scale

    def mask(rows, columns, values):
        row = rows.start + lax.broadcasted_iota(jnp.int32, values.shape, 0)
        column = columns.start + lax.broadcasted_iota(jnp.int32, values.shape, 1)
        return jnp.where(((row < half) != (column < half)) & halves, 0.0, values)

    def put_gram(rows, columns, values):
        values = mask(rows, columns, values)
        gram[rows, columns] = values
        store_pair((gh, gl), rows, columns, values)

    def put_change(rows, columns, values):
        values = POLY_TWO * gram[rows, columns] + POLY_THREE * values
        store_pair((sh, sl), rows, columns, values)

    def iterate(iteration, carry):
        for first in range(0, size, tile):
            rows = slice(first, first + tile)
            high, low = split_high(x_ref[rows, :])
            xh[rows, :] = high
            xl[rows, :] = low
            th[:, rows] = high.T
            tl[:, rows] = low.T
        symmetric_product((th, tl), (xh, xl), size, put_gram)
        symmetric_product((gh, gl), (gh, gl), size, put_change)
        for first in range(0, size, tile):
            rows = slice(first, first + tile)
            change = triple_dot((xh[rows, :], xl[rows, :]), (sh[...], sl[...]))
            x_ref[rows, :] = POLY_ONE * x_ref[rows, :] + change
        return carry

    lax.fori_loop(0, 5, iterate, 0)


def ortho_block_call(block, halves):
    size = block.shape[0]
    low = pltpu.VMEM((size, size), jnp.bfloat16)
    return pl.pallas_call(
        ortho_block_kernel,
        in_specs=[
            pl.BlockSpec(memory_space=pltpu.SMEM),
            pl.BlockSpec(memory_space=pltpu.VMEM),
        ],
        out_specs=pl.BlockSpec(memory_space=pltpu.VMEM),
        out_shape=jax.ShapeDtypeStruct((size, size), jnp.float32),
        scratch_shapes=[low] * 4 + [pltpu.VMEM((size, size), jnp.float32)] + [low] * 4,
        compiler_params=pltpu.CompilerParams(vmem_limit_bytes=56 * 1024 * 1024),
        cost_estimate=pl.CostEstimate(
            flops=5 * 9 * 2 * size**3, bytes_accessed=8 * size * size, transcendentals=0
        ),
        name="ortho_block",
    )(halves.reshape(1), block)


def ortho_rows_kernel(m_ref, o_ref, xh, xl, th, tl, gram, pair_g, pair_p, pair_t, product, pair_q):
    rows_all, size = m_ref.shape[1:]
    own = o_ref.shape[1]
    tile = 256
    squares = jnp.zeros((1, size), jnp.float32)
    for first in range(0, rows_all, tile):
        piece = m_ref[0, first : first + tile, :]
        squares = squares + jnp.sum(piece * piece, axis=0, keepdims=True)
    total = jnp.full((1, size), jnp.sum(squares), jnp.float32)
    scale = 1.0 / (jnp.sqrt(total) + ORTHO_EPS)
    for first in range(0, rows_all, tile):
        rows = slice(first, first + tile)
        high, low = split_high(m_ref[0, rows, :] * scale)
        xh[rows, :] = high
        xl[rows, :] = low
        th[:, rows] = high.T
        tl[:, rows] = low.T
    pair_g, pair_p, pair_t, pair_q = [
        (pair.at[0], pair.at[1]) for pair in (pair_g, pair_p, pair_t, pair_q)
    ]

    def put_gram(rows, columns, values):
        gram[rows, columns] = values
        store_pair(pair_g, rows, columns, values)

    def put_factor(rows, columns, values):
        row = rows.start + lax.broadcasted_iota(jnp.int32, values.shape, 0)
        column = columns.start + lax.broadcasted_iota(jnp.int32, values.shape, 1)
        values = POLY_TWO * gram[rows, columns] + POLY_THREE * values
        values = values + jnp.where(row == column, POLY_ONE, 0.0)
        product[rows, columns] = values
        store_pair(pair_p, rows, columns, values)

    def put_turn(rows, columns, values):
        store_pair(pair_t, rows, columns, values)

    def put_product(rows, columns, values):
        product[rows, columns] = values

    def keep_product():
        for first in range(0, size, tile):
            rows = slice(first, first + tile)
            store_pair(pair_q, rows, slice(0, size), product[rows, :])

    symmetric_product((th, tl), (xh, xl), size, put_gram)
    symmetric_product(pair_g, pair_g, size, put_factor)
    keep_product()

    def iterate(iteration, carry):
        symmetric_product(pair_g, pair_p, size, put_turn)
        symmetric_product(pair_t, pair_p, size, put_gram)
        symmetric_product(pair_g, pair_g, size, put_factor)
        symmetric_product(pair_q, pair_p, size, put_product)
        keep_product()
        return carry

    lax.fori_loop(0, 4, iterate, 0)
    o_ref[0] = triple_dot((xh[:own, :], xl[:own, :]), (pair_q[0][...], pair_q[1][...]))


def ortho_rows_call(group_rows, own_rows):
    kinds, rows_all, size = group_rows.shape
    low = jnp.bfloat16
    pair = pltpu.VMEM((2, size, size), low)
    square = pltpu.VMEM((size, size), jnp.float32)
    return pl.pallas_call(
        ortho_rows_kernel,
        grid=(kinds,),
        in_specs=[pl.BlockSpec((1, rows_all, size), lambda k: (k, 0, 0))],
        out_specs=pl.BlockSpec((1, own_rows, size), lambda k: (k, 0, 0)),
        out_shape=jax.ShapeDtypeStruct((kinds, own_rows, size), jnp.float32),
        scratch_shapes=[pltpu.VMEM((rows_all, size), low)] * 2
        + [pltpu.VMEM((size, rows_all), low)] * 2
        + [square, pair, pair, pair, square, pair],
        compiler_params=pltpu.CompilerParams(
            dimension_semantics=("arbitrary",), vmem_limit_bytes=40 * 1024 * 1024
        ),
        cost_estimate=pl.CostEstimate(
            flops=kinds * 60 * 2 * size**3, bytes_accessed=16 * size * size, transcendentals=0
        ),
        name="ortho_rows",
    )(group_rows)


def take_half(values, axis, own):
    keep = lax.dynamic_index_in_dim(values, own, axis, keepdims=False)
    send = lax.dynamic_index_in_dim(values, 1 - own, axis, keepdims=False)
    return keep, send


def reduce_to_owner(values, bits, count, place, order):
    left = bits[::-1]
    width = values.shape[1]
    for bit in order:
        before = 2 ** left.index(bit)
        left.remove(bit)
        split = values.reshape(before, 2, values.shape[0] // (2 * before), width)
        keep, send = take_half(split, 1, (place // bit) % 2)
        values = low_add(keep, swap_bit(send, count, bit)).reshape(-1, width)
    return values


def gather_from_owners(values, count, place, order, held=()):
    held = list(held)
    for bit in order:
        other = swap_bit(values, count, bit)
        held.append(bit)
        held.sort(reverse=True)
        after_bits = 2 ** (len(held) - 1 - held.index(bit))
        upper = (place // bit) % 2 == 1
        width = values.shape[1]
        pieces = (2 ** (len(held) - 1) // after_bits, 1, -1, width)
        own, other = values.reshape(pieces), other.reshape(pieces)
        values = jnp.where(
            upper,
            jnp.concatenate([other, own], axis=1),
            jnp.concatenate([own, other], axis=1),
        ).reshape(-1, width)
    return values


def muon_update(weight, ortho):
    return weight * (1.0 - MUON_RATE * WEIGHT_DECAY) - MUON_RATE * MUON_SHAPE * math.sqrt(D) * ortho


def shards(
    tokens,
    out_grad,
    lengths,
    routes,
    attn_weight,
    router_weight,
    expert_weight,
    gains,
    attn_moment,
    router_moment,
    expert_moment,
    gain_first,
    gain_second,
    attn_ema,
    router_ema,
    expert_ema,
    gain_ema,
):
    seqs_here = lengths.shape[0]
    tok_here = tokens.shape[0]
    seq_len = tok_here // seqs_here
    query_width = HEADS * HEAD_DIM
    kv_width = KV_HEADS * HEAD_DIM
    qkv_width = query_width + 2 * kv_width
    n_dp, n_blk = lax.axis_size("dp"), lax.axis_size("blk")
    count = n_dp * n_blk
    place = lax.axis_index(AXES)
    own_rows = expert_weight.shape[1]
    parts = D // own_rows
    half_bit, pair_bit = parts // 2, n_blk
    bit_z, bit_x, bit_y = [bit for bit in bits_below(parts, count) if bit != pair_bit]
    low_bits = bits_below(1, parts)
    upper_half = (place // half_bit) % 2 == 1
    groups = ((0, 0), (1, 0), (1, 1), (0, 1))
    far_bits = [
        far_x * bit_x + far_y * bit_y + far_z * bit_z
        for far_x, far_y in groups
        for far_z in range(2)
    ]
    own_experts = [(place ^ bits) // parts for bits in far_bits]
    pair_experts = [(place ^ pair_bit ^ bits) // parts for bits in far_bits]
    expert_ids = jnp.stack(own_experts + pair_experts)

    def relative(values):
        swapped = jnp.concatenate([values[:, HALF:], values[:, :HALF]], axis=1)
        return jnp.where(upper_half, swapped, values)

    attn_cols = attn_weight.shape[1]
    attn_low = attn_weight.astype(jnp.bfloat16)
    small_low = jnp.concatenate(
        [
            router_weight.astype(jnp.bfloat16),
            gains.astype(jnp.bfloat16).T,
            jnp.zeros((attn_weight.shape[0], PACK - EXPERTS - 2), jnp.bfloat16),
        ],
        axis=1,
    )
    full_packed = lax.all_gather(
        jnp.concatenate([attn_low, small_low], axis=1), AXES, axis=0, tiled=True
    )
    w_query = full_packed[:, :query_width]
    w_shared = full_packed[:, query_width:qkv_width]
    w_out = full_packed[:, qkv_width:attn_cols]
    full_router = full_packed[:, attn_cols : attn_cols + EXPERTS]
    full_gains = full_packed[:, attn_cols + EXPERTS : attn_cols + EXPERTS + 2].T
    early_bits = bits_below(1, half_bit)
    own_half = gather_rows(expert_weight.astype(jnp.bfloat16), 1, count, place, early_bits)
    level_one = (((1, 0, 0), half_bit), ((0, 1, 0), bit_x), ((0, 0, 1), bit_y))
    gather_last = (
        {(1, 1, 0): half_bit, (0, 1, 1): bit_y, (1, 0, 1): half_bit, (1, 1, 1): bit_x},
        {(1, 1, 0): bit_x, (0, 1, 1): bit_y, (1, 0, 1): bit_y, (1, 1, 1): bit_x},
    )
    hop_of = {half_bit: 0, bit_x: 1, bit_y: 2}

    def before_hop(chunk, bit):
        return tuple(
            side ^ 1 if index == hop_of[bit] else side for index, side in enumerate(chunk)
        )

    chunks = [{}, {}]
    before = None
    for part, kinds in enumerate((slice(0, 1), slice(1, 3))):
        own = own_half[kinds]
        own = after(own, full_packed if before is None else before)
        before = swap_bit(own, count, bit_z)
        chunks[part][0, 0, 0] = jnp.stack([own, before], axis=1)
        for chunk, bit in level_one:
            chunks[part][chunk] = swap_bit(chunks[part][0, 0, 0], count, bit)
    for chunk in ((1, 1, 0), (0, 1, 1), (1, 0, 1), (1, 1, 1)):
        for part in range(2):
            bit = gather_last[part][chunk]
            chunks[part][chunk] = swap_bit(chunks[part][before_hop(chunk, bit)], count, bit)
    gain_one = full_gains[0].astype(jnp.float32)
    gain_two = full_gains[1].astype(jnp.float32)
    inputs = tokens.astype(jnp.float32)
    cosine, sine = rotary_tables(seq_len, HEAD_DIM)
    cosine = jnp.concatenate([cosine] * 4, axis=1)
    sine = jnp.concatenate([-sine, sine, -sine, sine], axis=1)
    normed_one, query, key_rows, value_rows = project_call(
        tokens, gain_one[None], full_packed, full_packed, cosine, sine
    )
    position = jnp.arange(seq_len)
    live_rows = (position[None, :] < lengths[:, None]).reshape(tok_here, 1)
    live_grad = jnp.where(live_rows, out_grad, jnp.zeros_like(out_grad))
    live_relative = after(relative(live_grad), normed_one)
    both_grad = jnp.concatenate([live_relative, swap_bit(live_relative, count, pair_bit)])
    rows_each = attn_moment.shape[0]
    block_width = attn_cols // 3

    def spread(values):
        return lax.all_to_all(values, "blk", split_axis=0, concat_axis=0, tiled=True)

    old_pieces = [attn_moment[:, :block_width], attn_moment[:, block_width : 2 * block_width]]
    old_pieces += [
        attn_moment[:, 2 * block_width :],
        jnp.pad(router_moment, ((0, 0), (0, block_width - EXPERTS))),
    ]
    old_tasks = jnp.pad(jnp.stack(old_pieces), ((0, n_blk - 4), (0, 0), (0, 0)))
    old_tasks = spread(old_tasks).reshape(n_blk * rows_each, block_width)
    attended, totals = attend_call(
        lengths,
        query,
        key_rows,
        value_rows,
        seq_len,
        [chunks[0][0, 0, 0], old_tasks],
    )
    branch = plain_dot(attended, w_out, 1, 1)
    branch = after(branch, chunks[1][0, 0, 0], *[chunks[0][chunk] for chunk, _ in level_one])
    hidden_state = inputs + RESID_MULT * branch
    scale_two = lax.rsqrt(jnp.mean(hidden_state * hidden_state, axis=-1, keepdims=True) + NORM_EPS)
    unit_two = hidden_state * scale_two
    normed_two = (unit_two * gain_two).astype(jnp.bfloat16)
    pick = (jnp.arange(EXPERTS)[:, None] == expert_ids[None, :]).astype(jnp.bfloat16)
    router_here = jnp.dot(full_router, pick, preferred_element_type=jnp.float32).astype(
        jnp.bfloat16
    )
    logits = jnp.dot(normed_two, router_here, preferred_element_type=jnp.float32)
    used = jnp.any(routes[:, :, None] == expert_ids[None, None, :], axis=1)
    chosen_top = jnp.max(jnp.where(used, logits, NEG_FILL), axis=1, keepdims=True)
    exponent = jnp.where(used, jnp.exp(jnp.where(used, logits - chosen_top, 0.0)), 0.0)
    gate_weights = exponent / jnp.sum(exponent, axis=1, keepdims=True)
    second = relative(normed_two)
    other_second = swap_bit(second, count, pair_bit)
    gates_here = jnp.pad(gate_weights[:, :8], ((0, 0), (0, PACK - 8)))
    gates_there = jnp.pad(gate_weights[:, 8:], ((0, 0), (0, PACK - 8)))
    other_gates = swap_bit(gates_there, count, pair_bit)
    both_second = jnp.concatenate([second, other_second])
    both_gates = jnp.concatenate([gates_here, other_gates])
    own_parts, pair_parts, dgates = [], [], []
    grads, moved = {}, {}

    def send(chunk, bit):
        moved[chunk] = swap_bit(grads[chunk], count, bit)

    waits = {
        (0, 0): lambda: [chunks[part][0, 1, 0] for part in range(2)]
        + [chunks[part][0, 0, 1] for part in range(2)],
        (1, 0): lambda: [],
        (1, 1): lambda: [moved[1, 0, 0], pair_parts[0]],
        (0, 1): lambda: [moved[1, 1, 0], pair_parts[1]],
    }
    for turn_index, (far_x, far_y) in enumerate(groups):
        weights = [chunks[part][half, far_x, far_y] for part in range(2) for half in range(2)]
        own_part, pair_part, dgate, grad_own, grad_other = expert_call(
            2 * turn_index,
            both_second,
            both_grad,
            both_gates,
            weights,
            waits[far_x, far_y](),
        )
        own_parts.append(own_part)
        pair_parts.append(swap_bit(pair_part, count, pair_bit))
        dgates.append(dgate)
        grads[0, far_x, far_y] = grad_own
        grads[1, far_x, far_y] = grad_other
        if (far_x, far_y) == (0, 0):
            send((1, 0, 0), half_bit)
        if (far_x, far_y) == (1, 0):
            send((1, 1, 0), half_bit)
        if (far_x, far_y) == (1, 1):
            send((1, 1, 1), bit_x)
            send((0, 1, 1), bit_y)

    def total_of(*pieces):
        total = pieces[0].astype(jnp.float32)
        for piece in pieces[1:]:
            total = total + piece.astype(jnp.float32)
        return total.astype(jnp.bfloat16)

    last_other, grads[0, 0, 1], own_parts[3], dgates[3], *others = (
        lax.optimization_barrier(
            (
                grads[1, 0, 1],
                grads[0, 0, 1],
                own_parts[3],
                dgates[3],
                moved[1, 1, 1],
                moved[0, 1, 1],
                pair_parts[2],
            )
        )
    )
    moved[1, 1, 1], moved[0, 1, 1], pair_parts[2] = others
    half_y = [
        swap_bit(total_of(last_other[kind], moved[1, 1, 1][kind]), count, half_bit)
        for kind in range(3)
    ]
    grads[0, 1, 0] = total_of(grads[0, 1, 0], moved[1, 1, 0], moved[0, 1, 1])
    send((0, 1, 0), bit_x)
    dgate_sum = (dgates[0] + dgates[1]) + (dgates[2] + dgates[3])
    pair_dgates = swap_bit(dgate_sum[tok_here:], count, pair_bit)

    def gather_sum(parts):
        total = None
        for part in parts:
            part = part.astype(jnp.float32)
            total = part if total is None else total + part
        return relative(total)

    grad_normed_two = gather_sum([part[1] for part in own_parts + pair_parts])
    grad_gates = jnp.concatenate([dgate_sum[:tok_here, :8], pair_dgates[:, :8]], axis=1)
    grad_out = live_grad.astype(jnp.float32)
    inner_sum = jnp.sum(gate_weights * grad_gates, axis=1, keepdims=True)
    grad_logits = (gate_weights * (grad_gates - inner_sum)).astype(jnp.bfloat16)
    grad_normed_two = grad_normed_two + plain_dot(grad_logits, router_here, 1, 1)
    grad_router = jnp.matmul(
        plain_dot(normed_two, grad_logits, 0, 0),
        pick.astype(jnp.float32).T,
        precision=lax.Precision.HIGHEST,
    )
    grad_hidden_state = grad_out + norm_back(grad_normed_two, unit_two, scale_two, gain_two)
    grad_gain_two = jnp.sum(grad_normed_two * unit_two, axis=0)
    grad_branch = (RESID_MULT * grad_hidden_state).astype(jnp.bfloat16)
    grad_w_out = plain_dot(grad_branch, attended, 0, 0)
    dp_bits = bits_below(n_blk, count)
    far_dp = [bit for bit in dp_bits if bit not in (pair_bit, bit_x, bit_y)]
    first_x = [pair_bit, bit_x, bit_y] + far_dp
    first_y = [pair_bit, bit_y, bit_x] + far_dp

    def to_dp(values, order):
        return reduce_to_owner(values, dp_bits, count, place, order)

    low_grad_out = pin(grad_w_out.astype(jnp.bfloat16))
    grad_attended = jnp.dot(grad_branch, w_out, preferred_element_type=jnp.float32).astype(
        jnp.bfloat16
    )
    def attend_back(part, held, done):
        return attend_back_call(
            part,
            lengths,
            query,
            key_rows,
            value_rows,
            grad_attended,
            totals,
            cosine,
            sine,
            held,
            done,
        )

    first_heads = attend_back(0, [], [])
    last_own, half_y, _ = lax.optimization_barrier((grads[0, 0, 1], half_y, first_heads[0]))
    from_y = [
        swap_bit(total_of(last_own[kind], half_y[kind]), count, bit_y) for kind in range(3)
    ]
    grad_query, grad_key, grad_value = attend_back(
        1, first_heads, half_y + [moved[0, 1, 0]]
    )
    late_parts = after(tuple(own_parts + pair_parts), grad_query)
    block_out = (hidden_state + RESID_MULT * gather_sum([part[0] for part in late_parts])).astype(
        jnp.bfloat16
    )
    low_grad = [
        pin(plain_dot(normed_one, piece, 0, 0).astype(jnp.bfloat16))
        for piece in (grad_query, grad_key, grad_value)
    ]
    nearest, from_y, _ = lax.optimization_barrier((grads[0, 0, 0], from_y, low_grad[0]))
    expert_sums = [
        total_of(nearest[kind], moved[1, 0, 0][kind], moved[0, 1, 0][kind], from_y[kind])
        for kind in range(3)
    ]
    late_query = after(grad_query, *from_y)
    grad_normed_one = (
        plain_dot(late_query, w_query, 1, 1)
        + plain_dot(grad_key, w_shared[:, :kv_width], 1, 1)
        + plain_dot(grad_value, w_shared[:, kv_width:], 1, 1)
    )
    scale_one = lax.rsqrt(jnp.mean(inputs * inputs, axis=-1, keepdims=True) + NORM_EPS)
    unit_one = inputs * scale_one
    input_grad = grad_hidden_state + norm_back(grad_normed_one, unit_one, scale_one, gain_one)
    grad_gain_one = jnp.sum(grad_normed_one * unit_one, axis=0)
    grad_small = jnp.concatenate(
        [
            grad_router,
            jnp.stack([grad_gain_one, grad_gain_two], axis=1),
            jnp.zeros((D, PACK - EXPERTS - 2), jnp.float32),
        ],
        axis=1,
    ).astype(jnp.bfloat16)
    wide_sum = to_dp(
        jnp.concatenate([low_grad[0], after(low_grad_out, grad_query)], axis=1), first_x
    )
    query_sum, out_sum = wide_sum[:, :query_width], wide_sum[:, query_width:]
    shared_sum = to_dp(jnp.concatenate([low_grad[1], low_grad[2], pin(grad_small)], axis=1), first_y)

    def as_tasks(first, second, third, small):
        small = jnp.pad(small, ((0, 0), (0, block_width - PACK)))
        tasks = jnp.stack([first, second, third, small])
        return jnp.pad(tasks, ((0, n_blk - 4), (0, 0), (0, 0)))

    task_parts = spread(
        as_tasks(
            query_sum, shared_sum[:, :block_width], out_sum, shared_sum[:, block_width:]
        )
    )
    task_block = MOMENTUM * old_tasks + jnp.sum(task_parts.astype(jnp.float32), axis=0)
    moment_rows = spread(task_block.reshape(n_blk, rows_each, block_width))
    moment_attn = jnp.concatenate([moment_rows[0], moment_rows[1], moment_rows[2]], axis=1)
    moment_router = moment_rows[3][:, :EXPERTS]
    gain_grad = moment_rows[3][:, EXPERTS : EXPERTS + 2].T
    used_columns = (jnp.arange(block_width) < EXPERTS) | (lax.axis_index("blk") != 3)
    task_block = jnp.where(used_columns, task_block, 0.0)
    wide_x, wide_y = far_dp + [bit_y, bit_x], far_dp + [bit_x, bit_y]
    sides = [
        gather_from_owners(task_block[:, : block_width // 2], count, place, wide_x),
        gather_from_owners(task_block[:, block_width // 2 :], count, place, wide_y),
    ]
    attn_block = jnp.concatenate(
        [gather_from_owners(side, count, place, [pair_bit], wide_x) for side in sides], axis=1
    )
    moment_expert, group_rows = [], []
    for kind in range(3):
        total = after(expert_sums[kind], wide_sum, shared_sum)
        from_z = after(swap_bit(expert_sums[kind][1], count, bit_z), wide_sum, shared_sum)
        total = total[0].astype(jnp.float32) + from_z.astype(jnp.float32)
        total = total.T if kind == 2 else total
        if early_bits:
            total = reduce_rows(total.astype(jnp.bfloat16), count, place, early_bits[::-1])
        moment = MOMENTUM * expert_moment[kind] + total.astype(jnp.float32)
        rows = pin(moment)
        for bit in low_bits[:-1]:
            rows = jnp.concatenate([rows, swap_bit(rows, count, bit)])
        moment_expert.append(moment)
        group_rows.append((rows, swap_bit(rows, count, low_bits[-1])))
    attn_block = after(attn_block, *moment_expert)
    attn_iter = ortho_block_call(attn_block, (lax.axis_index("blk") == 1).astype(jnp.int32))
    group_rows = after(tuple(group_rows), attn_iter)
    group_rows = jnp.stack([jnp.concatenate(pieces) for pieces in group_rows])
    ortho_expert = ortho_rows_call(group_rows, own_rows)
    returned = lax.dynamic_slice_in_dim(
        attn_iter, lax.axis_index("dp") * (n_blk * rows_each), n_blk * rows_each, 0
    )
    returned = spread(returned.reshape(n_blk, rows_each, block_width))
    ortho_attn = jnp.concatenate([returned[0], returned[1], returned[2]], axis=1)
    ortho_router = returned[3][:, :EXPERTS]
    moment_expert = jnp.stack(moment_expert)
    attn_new = muon_update(attn_weight, ortho_attn)
    router_new = muon_update(router_weight, ortho_router)
    expert_new = muon_update(expert_weight, ortho_expert)
    first_new = BETA_ONE * gain_first + (1.0 - BETA_ONE) * gain_grad
    second_new = BETA_TWO * gain_second + (1.0 - BETA_TWO) * gain_grad * gain_grad
    corrected_first = first_new / (1.0 - BETA_ONE**STEP)
    corrected_second = second_new / (1.0 - BETA_TWO**STEP)
    gain_new = gains - ADAM_RATE * corrected_first / (jnp.sqrt(corrected_second) + ADAM_EPS)
    return (
        block_out,
        input_grad,
        moment_attn,
        moment_router,
        moment_expert,
        attn_new,
        router_new,
        expert_new,
        attn_new.astype(jnp.bfloat16),
        router_new.astype(jnp.bfloat16),
        expert_new.astype(jnp.bfloat16),
        EMA_KEEP * attn_ema + (1.0 - EMA_KEEP) * attn_new,
        EMA_KEEP * router_ema + (1.0 - EMA_KEEP) * router_new,
        EMA_KEEP * expert_ema + (1.0 - EMA_KEEP) * expert_new,
        first_new,
        second_new,
        gain_new,
        gain_new.astype(jnp.bfloat16),
        GAIN_EMA_KEEP * gain_ema + (1.0 - GAIN_EMA_KEEP) * gain_new,
    )


def solution(mesh):
    placed = (
        P(("dp", "blk"), None),
        P(("dp", "blk"), None),
        P(("dp", "blk")),
        P(("dp", "blk"), None),
        P(("dp", "blk"), None),
        P(("dp", "blk"), None),
        P(None, ("dp", "blk"), None),
        P(None, ("dp", "blk")),
        P(("dp", "blk"), None),
        P(("dp", "blk"), None),
        P(None, ("dp", "blk"), None),
        P(None, ("dp", "blk")),
        P(None, ("dp", "blk")),
        P(("dp", "blk"), None),
        P(("dp", "blk"), None),
        P(None, ("dp", "blk"), None),
        P(None, ("dp", "blk")),
    )
    return jax.shard_map(
        shards,
        mesh=mesh,
        in_specs=placed,
        out_specs=(
            P(("dp", "blk"), None),
            P(("dp", "blk"), None),
            P(("dp", "blk"), None),
            P(("dp", "blk"), None),
            P(None, ("dp", "blk"), None),
            P(("dp", "blk"), None),
            P(("dp", "blk"), None),
            P(None, ("dp", "blk"), None),
            P(("dp", "blk"), None),
            P(("dp", "blk"), None),
            P(None, ("dp", "blk"), None),
            P(("dp", "blk"), None),
            P(("dp", "blk"), None),
            P(None, ("dp", "blk"), None),
            P(None, ("dp", "blk")),
            P(None, ("dp", "blk")),
            P(None, ("dp", "blk")),
            P(None, ("dp", "blk")),
            P(None, ("dp", "blk")),
        ),
        check_vma=False,
    )
```

```python
import functools
import math

import jax
import jax.numpy as jnp
from jax import lax
from jax.experimental import pallas as pl
from jax.experimental.layout import Layout, with_layout_constraint
from jax.experimental.pallas import tpu as pltpu
from jax.sharding import PartitionSpec as P

D = 1024
HEADS = 16
KV_HEADS = 8
HEAD_DIM = 64
FF = 512
TOP = 8
EXPERTS = 16
STEP = 10
HALF = D // 2
PACK = 128
AXES = ("dp", "blk")


NORM_EPS = 1e-05
ATTN_MULT = 0.015625
RESID_MULT = 0.22
ROPE_BASE = 10000.0
NEG_FILL = -1e30
POLY_ONE = 3.4445
POLY_TWO = -4.775
POLY_THREE = 2.0315
ORTHO_EPS = 1e-07
MOMENTUM = 0.95
MUON_RATE = 0.6
MUON_SHAPE = 0.2
WEIGHT_DECAY = 0.01
ADAM_RATE = 0.8
BETA_ONE = 0.9
BETA_TWO = 0.95
ADAM_EPS = 1e-08
EMA_KEEP = 0.9
GAIN_EMA_KEEP = 0.6


def plain_dot(left_side, right_side, contract_left, contract_right):
    return lax.dot_general(
        left_side,
        right_side,
        (((contract_left,), (contract_right,)), ((), ())),
        preferred_element_type=jnp.float32,
    )


def rotary_tables(length, head_width):
    position = jnp.arange(length).astype(jnp.float32)
    inverse = ROPE_BASE ** (-jnp.arange(0, head_width, 2).astype(jnp.float32) / head_width)
    angles = position[:, None] * inverse[None, :]
    return (jnp.cos(angles), jnp.sin(angles))


def norm_back(grad_normed, unit_rows, scale_rows, gain_row):
    grad_unit = grad_normed * gain_row
    return scale_rows * (
        grad_unit - unit_rows * jnp.mean(grad_unit * unit_rows, axis=-1, keepdims=True)
    )


def pin(values):
    return with_layout_constraint(values, Layout(major_to_minor=tuple(range(values.ndim))))


def swap_bit(values, count, bit):
    pairs = [(place, place ^ bit) for place in range(count)]
    return pin(lax.ppermute(pin(values), AXES, pairs))


def after(values, *done):
    return lax.optimization_barrier((values,) + done)[0]


def low_add(left_side, right_side):
    return (left_side.astype(jnp.float32) + right_side.astype(jnp.float32)).astype(jnp.bfloat16)


def bits_below(low_bit, high_bit):
    bits = []
    while low_bit < high_bit:
        bits.append(low_bit)
        low_bit *= 2
    return bits


def gather_rows(values, axis, count, place, bits):
    for bit in bits:
        other = swap_bit(values, count, bit)
        upper = (place // bit) % 2 == 1
        values = jnp.where(
            upper,
            jnp.concatenate([other, values], axis=axis),
            jnp.concatenate([values, other], axis=axis),
        )
    return values


def reduce_rows(values, count, place, bits):
    for bit in bits:
        split = values.reshape((2, values.shape[0] // 2) + values.shape[1:])
        own = (place // bit) % 2
        keep = lax.dynamic_index_in_dim(split, own, 0, keepdims=False)
        other = swap_bit(
            lax.dynamic_index_in_dim(split, 1 - own, 0, keepdims=False), count, bit
        )
        values = low_add(keep, other)
    return values


def dot_nn(left_side, right_side):
    return plain_dot(left_side, right_side, 1, 0)


def dot_nt(left_side, right_side):
    return plain_dot(left_side, right_side, 1, 1)


def dot_tn(left_side, right_side):
    return plain_dot(left_side, right_side, 0, 0)


def turn(values, cosine, sine, lanes):
    far = jnp.where(
        lanes % HEAD_DIM < HEAD_DIM // 2,
        pltpu.roll(values, PACK - HEAD_DIM // 2, 1),
        pltpu.roll(values, HEAD_DIM // 2, 1),
    )
    return values * cosine + far * sine


def project_kernel(
    tok_ref, gain_ref, wq_ref, wkv_ref, cos_ref, sin_ref, norm_ref, q_ref, k_ref, v_ref
):
    rows = tok_ref.shape[0]
    inputs = tok_ref[...].astype(jnp.float32)
    scale = lax.rsqrt(jnp.mean(inputs * inputs, axis=-1, keepdims=True) + NORM_EPS)
    normed = (inputs * scale * gain_ref[...]).astype(jnp.bfloat16)
    norm_ref[...] = normed
    cosine, sine = cos_ref[...], sin_ref[...]
    lanes = lax.broadcasted_iota(jnp.int32, (rows, PACK), 1)
    query = dot_nn(normed, wq_ref[...])
    for start in range(0, HEADS * HEAD_DIM, PACK):
        turned = turn(query[:, start : start + PACK], cosine, sine, lanes)
        q_ref[:, start : start + PACK] = turned.astype(jnp.bfloat16) * ATTN_MULT
    both = dot_nn(normed, wkv_ref[...])
    width = KV_HEADS * HEAD_DIM
    for start in range(0, width, PACK):
        turned = turn(both[:, start : start + PACK], cosine, sine, lanes)
        k_ref[:, start : start + PACK] = turned.astype(jnp.bfloat16)
    v_ref[...] = both[:, width:].astype(jnp.bfloat16)


def project_call(tokens, gain_row, wq, wkv, cosine, sine):
    seq_rows = cosine.shape[0]
    rows = min(256, seq_rows)
    repeats = seq_rows // rows
    tok_here = tokens.shape[0]
    width = KV_HEADS * HEAD_DIM
    low = jnp.bfloat16
    return pl.pallas_call(
        project_kernel,
        grid=(tok_here // rows,),
        in_specs=[
            pl.BlockSpec((rows, D), lambda b: (b, 0)),
            pl.BlockSpec((1, D), lambda b: (0, 0)),
            pl.BlockSpec((D, HEADS * HEAD_DIM), lambda b: (0, 0)),
            pl.BlockSpec((D, 2 * width), lambda b: (0, 1)),
            pl.BlockSpec((rows, PACK), lambda b: (b % repeats, 0)),
            pl.BlockSpec((rows, PACK), lambda b: (b % repeats, 0)),
        ],
        out_specs=[
            pl.BlockSpec((rows, D), lambda b: (b, 0)),
            pl.BlockSpec((rows, HEADS * HEAD_DIM), lambda b: (b, 0)),
            pl.BlockSpec((rows, width), lambda b: (b, 0)),
            pl.BlockSpec((rows, width), lambda b: (b, 0)),
        ],
        out_shape=[
            jax.ShapeDtypeStruct((tok_here, D), low),
            jax.ShapeDtypeStruct((tok_here, HEADS * HEAD_DIM), low),
            jax.ShapeDtypeStruct((tok_here, width), low),
            jax.ShapeDtypeStruct((tok_here, width), low),
        ],
        compiler_params=pltpu.CompilerParams(
            dimension_semantics=("arbitrary",), vmem_limit_bytes=40 * 1024 * 1024
        ),
        cost_estimate=pl.CostEstimate(
            flops=8_000_000_000, bytes_accessed=14_000_000, transcendentals=0
        ),
        name="project",
    )(tokens, gain_row, wq, wkv, cosine, sine)


def attend_kernel(len_ref, q_ref, k_ref, v_ref, *refs):
    o_ref, lse_ref = refs[-2:]
    seq_len = q_ref.shape[0]
    rows = min(256, seq_len)
    length = len_ref[0, 0]
    for first in range(0, seq_len, rows):
        keys = first + rows
        key_index = lax.broadcasted_iota(jnp.int32, (rows, keys), 1)
        query_index = first + lax.broadcasted_iota(jnp.int32, (rows, keys), 0)
        bias = jnp.where((key_index <= query_index) & (key_index < length), 0.0, NEG_FILL)
        lanes = lax.broadcasted_iota(jnp.int32, (rows, PACK), 1)
        totals = jnp.zeros((rows, PACK), jnp.float32)
        for head in range(4):
            shared = (head // 2) * HEAD_DIM
            key_rows = k_ref[:keys, shared : shared + HEAD_DIM]
            value_rows = v_ref[:keys, shared : shared + HEAD_DIM]
            query = q_ref[first:keys, head * HEAD_DIM : (head + 1) * HEAD_DIM]
            scores = dot_nt(query, key_rows) + bias
            largest = jnp.max(scores, axis=1, keepdims=True)
            exponent = jnp.exp(scores - largest)
            total = jnp.sum(exponent, axis=1, keepdims=True)
            probability = (exponent * (1.0 / total)).astype(jnp.bfloat16)
            o_ref[first:keys, head * HEAD_DIM : (head + 1) * HEAD_DIM] = dot_nn(
                probability, value_rows
            ).astype(jnp.bfloat16)
            totals = jnp.where(lanes == head, largest + jnp.log(total), totals)
        lse_ref[0, :, first:keys] = totals.T[:8]


def attend_call(lengths, query, key_rows, value_rows, seq_len, done):
    tok_here = query.shape[0]
    seqs = tok_here // seq_len
    groups = KV_HEADS // 2
    return pl.pallas_call(
        attend_kernel,
        grid=(seqs, groups),
        in_specs=[
            pl.BlockSpec((1, 1), lambda s, g: (s, 0), memory_space=pltpu.SMEM),
            pl.BlockSpec((seq_len, 4 * HEAD_DIM), lambda s, g: (s, g)),
            pl.BlockSpec((seq_len, PACK), lambda s, g: (s, g)),
            pl.BlockSpec((seq_len, PACK), lambda s, g: (s, g)),
        ]
        + [pl.BlockSpec(memory_space=pl.ANY)] * len(done),
        out_specs=[
            pl.BlockSpec((seq_len, 4 * HEAD_DIM), lambda s, g: (s, g)),
            pl.BlockSpec((1, 8, seq_len), lambda s, g: (g, 0, s)),
        ],
        out_shape=[
            jax.ShapeDtypeStruct((tok_here, HEADS * HEAD_DIM), jnp.bfloat16),
            jax.ShapeDtypeStruct((groups, 8, tok_here), jnp.float32),
        ],
        compiler_params=pltpu.CompilerParams(
            dimension_semantics=("arbitrary", "arbitrary"), vmem_limit_bytes=40 * 1024 * 1024
        ),
        cost_estimate=pl.CostEstimate(
            flops=20_000_000_000, bytes_accessed=8_000_000, transcendentals=12_000_000
        ),
        name="attend",
    )(lengths.reshape(seqs, 1), query, key_rows, value_rows, *done)


def attend_back_kernel(
    len_ref,
    q_ref,
    k_ref,
    v_ref,
    do_ref,
    lse_ref,
    cos_ref,
    sin_ref,
    *refs,
):
    dq_ref, dk_ref, dv_ref, k_acc, v_acc = refs[-5:]
    seq_len = q_ref.shape[0]
    rows = min(256, seq_len)
    length = len_ref[0, 0]
    k_acc[...] = jnp.zeros_like(k_acc)
    v_acc[...] = jnp.zeros_like(v_acc)
    lanes = lax.broadcasted_iota(jnp.int32, (rows, PACK), 1)
    turned_keys = [
        k_ref[:, shared : shared + HEAD_DIM].T for shared in (0, HEAD_DIM)
    ]
    for first in range(0, seq_len, rows):
        keys = first + rows
        key_index = lax.broadcasted_iota(jnp.int32, (keys, rows), 0)
        query_index = first + lax.broadcasted_iota(jnp.int32, (keys, rows), 1)
        bias = jnp.where((key_index <= query_index) & (key_index < length), 0.0, NEG_FILL)
        for pair in range(2):
            shared = pair * HEAD_DIM
            key_rows = k_ref[:keys, shared : shared + HEAD_DIM]
            value_rows = v_ref[:keys, shared : shared + HEAD_DIM]
            key_grad = None
            value_grad = None
            query_grads = []
            for head in (2 * pair, 2 * pair + 1):
                query = q_ref[first:keys, head * HEAD_DIM : (head + 1) * HEAD_DIM]
                grad = do_ref[first:keys, head * HEAD_DIM : (head + 1) * HEAD_DIM]
                scores = dot_nt(key_rows, query) + bias
                probability = jnp.exp(scores - lse_ref[0, head : head + 1, first:keys])
                prob_grad = dot_nt(value_rows, grad)
                inner = jnp.sum(probability * prob_grad, axis=0, keepdims=True)
                score_grad = (probability * (prob_grad - inner)).astype(jnp.bfloat16)
                key_part = dot_nn(score_grad, query)
                value_part = dot_nn(probability.astype(jnp.bfloat16), grad)
                key_grad = key_part if key_grad is None else key_grad + key_part
                value_grad = value_part if value_grad is None else value_grad + value_part
                query_grads.append(dot_nn(turned_keys[pair][:, :keys], score_grad))
            k_acc[:keys, shared : shared + HEAD_DIM] += key_grad
            v_acc[:keys, shared : shared + HEAD_DIM] += value_grad
            query_grad = jnp.concatenate(query_grads, axis=0).T * ATTN_MULT
            dq_ref[first:keys, pair * PACK : (pair + 1) * PACK] = turn(
                query_grad, cos_ref[first:keys, :], -sin_ref[first:keys, :], lanes
            ).astype(jnp.bfloat16)
    for first in range(0, seq_len, rows):
        keys = first + rows
        dk_ref[first:keys, :] = turn(
            k_acc[first:keys, :], cos_ref[first:keys, :], -sin_ref[first:keys, :], lanes
        ).astype(jnp.bfloat16)
        dv_ref[first:keys, :] = v_acc[first:keys, :].astype(jnp.bfloat16)


def attend_back_call(
    part, lengths, query, key_rows, value_rows, grad, totals, cosine, sine, held, done
):
    tok_here = query.shape[0]
    seq_len = cosine.shape[0]
    seqs = tok_here // seq_len
    groups = KV_HEADS // 4
    skip = part * groups
    wide = pl.BlockSpec((seq_len, 4 * HEAD_DIM), lambda s, g: (s, g + skip))
    narrow = pl.BlockSpec((seq_len, PACK), lambda s, g: (s, g + skip))
    table = pl.BlockSpec((seq_len, PACK), lambda s, g: (0, 0))
    return pl.pallas_call(
        attend_back_kernel,
        grid=(seqs, groups),
        in_specs=[
            pl.BlockSpec((1, 1), lambda s, g: (s, 0), memory_space=pltpu.SMEM),
            wide,
            narrow,
            narrow,
            wide,
            pl.BlockSpec((1, 8, seq_len), lambda s, g: (g + skip, 0, s)),
            table,
            table,
        ]
        + [pl.BlockSpec(memory_space=pl.ANY)] * (len(held) + len(done)),
        out_specs=[wide, narrow, narrow],
        out_shape=[
            jax.ShapeDtypeStruct((tok_here, HEADS * HEAD_DIM), jnp.bfloat16),
            jax.ShapeDtypeStruct((tok_here, KV_HEADS * HEAD_DIM), jnp.bfloat16),
            jax.ShapeDtypeStruct((tok_here, KV_HEADS * HEAD_DIM), jnp.bfloat16),
        ],
        input_output_aliases={8 + index: index for index in range(len(held))},
        scratch_shapes=[
            pltpu.VMEM((seq_len, PACK), jnp.float32),
            pltpu.VMEM((seq_len, PACK), jnp.float32),
        ],
        compiler_params=pltpu.CompilerParams(
            dimension_semantics=("arbitrary", "arbitrary"), vmem_limit_bytes=40 * 1024 * 1024
        ),
        cost_estimate=pl.CostEstimate(
            flops=24_000_000_000, bytes_accessed=8_000_000, transcendentals=6_000_000
        ),
        name="attend_back",
    )(
        lengths.reshape(seqs, 1),
        query,
        key_rows,
        value_rows,
        grad,
        totals,
        cosine,
        sine,
        *held,
        *done,
    )


def expert_kernel(waits, first, *refs):
    n2_ref, dy_ref, gate_ref = refs[:3]
    own_w_ref, other_w_ref = refs[3:5]
    outs = refs[5 + waits :]
    own_ref, pair_ref, dgate_ref, grad_own_ref, grad_other_ref = outs[:5]
    m_acc, dn_acc, g_acc, u_acc, d_acc, turned_ref = outs[5:]
    step = pl.program_id(0)
    block = pl.program_id(1)
    blocks = pl.num_programs(1)
    rows = n2_ref.shape[0]
    place = pl.ds(pl.multiple_of(block * rows, rows), rows)
    lane = lax.broadcasted_iota(jnp.int32, (rows, PACK), 1)

    @pl.when(step == 0)
    def _():
        turned_ref[:, place] = n2_ref[...].T

    wg_own, wg_other = own_w_ref[0, 0], other_w_ref[0, 0]
    wu_own, wu_other = own_w_ref[1, 0], other_w_ref[1, 0]
    wd_own, wd_other = own_w_ref[2, 0], other_w_ref[2, 0]
    column = lane == step + first
    gate = jnp.sum(jnp.where(column, gate_ref[...], 0.0), axis=1, keepdims=True)
    dm = RESID_MULT * dy_ref[...].astype(jnp.float32)
    dout = (gate * dm).astype(jnp.bfloat16)
    ug = dot_nn(n2_ref[:, :HALF], wg_own) + dot_nn(n2_ref[:, HALF:], wg_other)
    uu = dot_nn(n2_ref[:, :HALF], wu_own) + dot_nn(n2_ref[:, HALF:], wu_other)
    dh = dot_nn(dout[:, :HALF], wd_own) + dot_nn(dout[:, HALF:], wd_other)
    sig = 1.0 / (1.0 + jnp.exp(-ug))
    silu = ug * sig
    hidden = (silu * uu).astype(jnp.bfloat16)
    dug = (dh * uu * sig * (1.0 + ug * (1.0 - sig))).astype(jnp.bfloat16)
    duu = (dh * silu).astype(jnp.bfloat16)
    y_own = dot_nt(hidden, wd_own)
    y_other = dot_nt(hidden, wd_other)
    n2t = turned_ref[:, place]
    g_acc[...] = jnp.where(block == 0, 0.0, g_acc[...]) + dot_nn(n2t, dug)
    dgate = jnp.sum(dm[:, :HALF] * y_own, axis=1, keepdims=True) + jnp.sum(
        dm[:, HALF:] * y_other, axis=1, keepdims=True
    )
    dgate_ref[place, :] = jnp.where(
        column, dgate, jnp.where(step == 0, 0.0, dgate_ref[place, :])
    )
    m_acc[place, :HALF] = jnp.where(step == 0, 0.0, m_acc[place, :HALF]) + gate * y_own
    m_acc[place, HALF:] = jnp.where(step == 0, 0.0, m_acc[place, HALF:]) + gate * y_other
    u_acc[...] = jnp.where(block == 0, 0.0, u_acc[...]) + dot_nn(n2t, duu)
    dn_acc[place, :HALF] = (
        jnp.where(step == 0, 0.0, dn_acc[place, :HALF]) + dot_nt(dug, wg_own) + dot_nt(duu, wu_own)
    )
    dn_acc[place, HALF:] = (
        jnp.where(step == 0, 0.0, dn_acc[place, HALF:])
        + dot_nt(dug, wg_other)
        + dot_nt(duu, wu_other)
    )
    d_acc[...] = jnp.where(block == 0, 0.0, d_acc[...]) + dot_tn(hidden, dout)
    last = step == pl.num_programs(0) - 1

    @pl.when(last & (block < blocks // 2))
    def _():
        own_ref[0] = m_acc[place, :].astype(jnp.bfloat16)
        own_ref[1] = dn_acc[place, :].astype(jnp.bfloat16)

    @pl.when(last & (block >= blocks // 2))
    def _():
        pair_ref[0] = m_acc[place, :].astype(jnp.bfloat16)
        pair_ref[1] = dn_acc[place, :].astype(jnp.bfloat16)

    @pl.when(block == blocks - 1)
    def _():
        grad_own_ref[0, 0] = g_acc[:HALF, :].astype(jnp.bfloat16)
        grad_own_ref[1, 0] = u_acc[:HALF, :].astype(jnp.bfloat16)
        grad_own_ref[2, 0] = d_acc[:, :HALF].astype(jnp.bfloat16)
        grad_other_ref[0, 0] = g_acc[HALF:, :].astype(jnp.bfloat16)
        grad_other_ref[1, 0] = u_acc[HALF:, :].astype(jnp.bfloat16)
        grad_other_ref[2, 0] = d_acc[:, HALF:].astype(jnp.bfloat16)


def expert_call(first, n2, dy, gates, weights, done):
    tokens_all = n2.shape[0]
    rows = min(512, tokens_all // 2)
    half_blocks = tokens_all // rows // 2
    steps = weights[0].shape[1]

    def own_block(step, block):
        return (0, jnp.where(step == steps - 1, jnp.minimum(block, half_blocks - 1), 0), 0)

    def pair_block(step, block):
        return (0, jnp.where(step == steps - 1, jnp.maximum(block - half_blocks, 0), 0), 0)

    low = jnp.bfloat16

    def pieces(kinds):
        return pl.BlockSpec((kinds, 1, HALF, FF), lambda s, b: (0, s, 0, 0))

    half_shape = jax.ShapeDtypeStruct((2, tokens_all // 2, D), low)
    piece_shape = jax.ShapeDtypeStruct((3, steps, HALF, FF), low)
    outputs = pl.pallas_call(
        functools.partial(expert_kernel, len(done), first),
        grid=(steps, 2 * half_blocks),
        in_specs=[
            pl.BlockSpec((rows, D), lambda s, b: (b, 0)),
            pl.BlockSpec((rows, D), lambda s, b: (b, 0)),
            pl.BlockSpec((rows, PACK), lambda s, b: (b, 0)),
            pieces(3),
            pieces(3),
        ]
        + [pl.BlockSpec(memory_space=pl.ANY)] * len(done),
        out_specs=[
            pl.BlockSpec((2, rows, D), own_block, pipeline_mode=pl.Buffered(1)),
            pl.BlockSpec((2, rows, D), pair_block, pipeline_mode=pl.Buffered(1)),
            pl.BlockSpec((tokens_all, PACK), lambda s, b: (0, 0)),
            pieces(3),
            pieces(3),
        ],
        out_shape=[
            half_shape,
            half_shape,
            jax.ShapeDtypeStruct((tokens_all, PACK), jnp.float32),
            piece_shape,
            piece_shape,
        ],
        scratch_shapes=[
            pltpu.VMEM((tokens_all, D), jnp.float32),
            pltpu.VMEM((tokens_all, D), jnp.float32),
            pltpu.VMEM((D, FF), jnp.float32),
            pltpu.VMEM((D, FF), jnp.float32),
            pltpu.VMEM((FF, D), jnp.float32),
            pltpu.VMEM((D, tokens_all), low),
        ],
        compiler_params=pltpu.CompilerParams(
            dimension_semantics=("arbitrary", "arbitrary"), vmem_limit_bytes=62 * 1024 * 1024
        ),
        cost_estimate=pl.CostEstimate(
            flops=9 * 2 * tokens_all * D * FF * steps * 3 // 2,
            bytes_accessed=48 * 1024 * 1024,
            transcendentals=steps * tokens_all * FF,
        ),
        name="experts",
    )(n2, dy, gates, *weights, *done)
    return outputs


def split_high(values):
    high = values.astype(jnp.bfloat16)
    return high, (values - high.astype(jnp.float32)).astype(jnp.bfloat16)


def triple_dot(left_side, right_side):
    left_high, left_low = left_side
    right_high, right_low = right_side
    return dot_nn(left_high, right_high) + (
        dot_nn(left_high, right_low) + dot_nn(left_low, right_high)
    )


def symmetric_product(left_pair, right_pair, size, put):
    tile = min(256, size)
    for first in range(0, size, tile):
        rows = slice(first, first + tile)
        part = triple_dot(
            tuple(side[rows, :] for side in left_pair),
            tuple(side[:, first:] for side in right_pair),
        )
        put(rows, slice(first, size), part)
        for second in range(first + tile, size, tile):
            columns = slice(second, second + tile)
            put(columns, rows, part[:, second - first : second - first + tile].T)


def store_pair(pair, rows, columns, values):
    high, low = split_high(values)
    pair[0][rows, columns] = high
    pair[1][rows, columns] = low


def ortho_block_kernel(halves_ref, m_ref, x_ref, xh, xl, th, tl, gram, gh, gl, sh, sl):
    size = m_ref.shape[0]
    tile = 256
    halves = halves_ref[0] == 1
    half = size // 2

    def square_sum(columns):
        total = jnp.zeros((1, half), jnp.float32)
        for first in range(0, size, tile):
            piece = m_ref[first : first + tile, columns]
            total = total + jnp.sum(piece * piece, axis=0, keepdims=True)
        return jnp.sum(total)

    lower, upper = square_sum(slice(0, half)), square_sum(slice(half, size))
    whole = lower + upper

    def scale_of(own):
        squares = jnp.full((1, half), jnp.where(halves, own, whole), jnp.float32)
        return 1.0 / (jnp.sqrt(squares) + ORTHO_EPS)

    for columns, own in ((slice(0, half), lower), (slice(half, size), upper)):
        scale = scale_of(own)
        for first in range(0, size, tile):
            rows = slice(first, first + tile)
            x_ref[rows, columns] = m_ref[rows, columns] * scale

    def mask(rows, columns, values):
        row = rows.start + lax.broadcasted_iota(jnp.int32, values.shape, 0)
        column = columns.start + lax.broadcasted_iota(jnp.int32, values.shape, 1)
        return jnp.where(((row < half) != (column < half)) & halves, 0.0, values)

    def put_gram(rows, columns, values):
        values = mask(rows, columns, values)
        gram[rows, columns] = values
        store_pair((gh, gl), rows, columns, values)

    def put_change(rows, columns, values):
        values = POLY_TWO * gram[rows, columns] + POLY_THREE * values
        store_pair((sh, sl), rows, columns, values)

    def iterate(iteration, carry):
        for first in range(0, size, tile):
            rows = slice(first, first + tile)
            high, low = split_high(x_ref[rows, :])
            xh[rows, :] = high
            xl[rows, :] = low
            th[:, rows] = high.T
            tl[:, rows] = low.T
        symmetric_product((th, tl), (xh, xl), size, put_gram)
        symmetric_product((gh, gl), (gh, gl), size, put_change)
        for first in range(0, size, tile):
            rows = slice(first, first + tile)
            change = triple_dot((xh[rows, :], xl[rows, :]), (sh[...], sl[...]))
            x_ref[rows, :] = POLY_ONE * x_ref[rows, :] + change
        return carry

    lax.fori_loop(0, 5, iterate, 0)


def ortho_block_call(block, halves):
    size = block.shape[0]
    low = pltpu.VMEM((size, size), jnp.bfloat16)
    return pl.pallas_call(
        ortho_block_kernel,
        in_specs=[
            pl.BlockSpec(memory_space=pltpu.SMEM),
            pl.BlockSpec(memory_space=pltpu.VMEM),
        ],
        out_specs=pl.BlockSpec(memory_space=pltpu.VMEM),
        out_shape=jax.ShapeDtypeStruct((size, size), jnp.float32),
        scratch_shapes=[low] * 4 + [pltpu.VMEM((size, size), jnp.float32)] + [low] * 4,
        compiler_params=pltpu.CompilerParams(vmem_limit_bytes=56 * 1024 * 1024),
        cost_estimate=pl.CostEstimate(
            flops=5 * 9 * 2 * size**3, bytes_accessed=8 * size * size, transcendentals=0
        ),
        name="ortho_block",
    )(halves.reshape(1), block)


def ortho_rows_kernel(m_ref, o_ref, xh, xl, th, tl, gram, pair_g, pair_p, pair_t, product, pair_q):
    rows_all, size = m_ref.shape[1:]
    own = o_ref.shape[1]
    tile = 256
    squares = jnp.zeros((1, size), jnp.float32)
    for first in range(0, rows_all, tile):
        piece = m_ref[0, first : first + tile, :]
        squares = squares + jnp.sum(piece * piece, axis=0, keepdims=True)
    total = jnp.full((1, size), jnp.sum(squares), jnp.float32)
    scale = 1.0 / (jnp.sqrt(total) + ORTHO_EPS)
    for first in range(0, rows_all, tile):
        rows = slice(first, first + tile)
        high, low = split_high(m_ref[0, rows, :] * scale)
        xh[rows, :] = high
        xl[rows, :] = low
        th[:, rows] = high.T
        tl[:, rows] = low.T
    pair_g, pair_p, pair_t, pair_q = [
        (pair.at[0], pair.at[1]) for pair in (pair_g, pair_p, pair_t, pair_q)
    ]

    def put_gram(rows, columns, values):
        gram[rows, columns] = values
        store_pair(pair_g, rows, columns, values)

    def put_factor(rows, columns, values):
        row = rows.start + lax.broadcasted_iota(jnp.int32, values.shape, 0)
        column = columns.start + lax.broadcasted_iota(jnp.int32, values.shape, 1)
        values = POLY_TWO * gram[rows, columns] + POLY_THREE * values
        values = values + jnp.where(row == column, POLY_ONE, 0.0)
        product[rows, columns] = values
        store_pair(pair_p, rows, columns, values)

    def put_turn(rows, columns, values):
        store_pair(pair_t, rows, columns, values)

    def put_product(rows, columns, values):
        product[rows, columns] = values

    def keep_product():
        for first in range(0, size, tile):
            rows = slice(first, first + tile)
            store_pair(pair_q, rows, slice(0, size), product[rows, :])

    symmetric_product((th, tl), (xh, xl), size, put_gram)
    symmetric_product(pair_g, pair_g, size, put_factor)
    keep_product()

    def iterate(iteration, carry):
        symmetric_product(pair_g, pair_p, size, put_turn)
        symmetric_product(pair_t, pair_p, size, put_gram)
        symmetric_product(pair_g, pair_g, size, put_factor)
        symmetric_product(pair_q, pair_p, size, put_product)
        keep_product()
        return carry

    lax.fori_loop(0, 4, iterate, 0)
    o_ref[0] = triple_dot((xh[:own, :], xl[:own, :]), (pair_q[0][...], pair_q[1][...]))


def ortho_rows_call(group_rows, own_rows):
    kinds, rows_all, size = group_rows.shape
    low = jnp.bfloat16
    pair = pltpu.VMEM((2, size, size), low)
    square = pltpu.VMEM((size, size), jnp.float32)
    return pl.pallas_call(
        ortho_rows_kernel,
        grid=(kinds,),
        in_specs=[pl.BlockSpec((1, rows_all, size), lambda k: (k, 0, 0))],
        out_specs=pl.BlockSpec((1, own_rows, size), lambda k: (k, 0, 0)),
        out_shape=jax.ShapeDtypeStruct((kinds, own_rows, size), jnp.float32),
        scratch_shapes=[pltpu.VMEM((rows_all, size), low)] * 2
        + [pltpu.VMEM((size, rows_all), low)] * 2
        + [square, pair, pair, pair, square, pair],
        compiler_params=pltpu.CompilerParams(
            dimension_semantics=("arbitrary",), vmem_limit_bytes=40 * 1024 * 1024
        ),
        cost_estimate=pl.CostEstimate(
            flops=kinds * 60 * 2 * size**3, bytes_accessed=16 * size * size, transcendentals=0
        ),
        name="ortho_rows",
    )(group_rows)


def take_half(values, axis, own):
    keep = lax.dynamic_index_in_dim(values, own, axis, keepdims=False)
    send = lax.dynamic_index_in_dim(values, 1 - own, axis, keepdims=False)
    return keep, send


def reduce_to_owner(values, bits, count, place, order):
    left = bits[::-1]
    width = values.shape[1]
    for bit in order:
        before = 2 ** left.index(bit)
        left.remove(bit)
        split = values.reshape(before, 2, values.shape[0] // (2 * before), width)
        keep, send = take_half(split, 1, (place // bit) % 2)
        values = low_add(keep, swap_bit(send, count, bit)).reshape(-1, width)
    return values


def gather_from_owners(values, count, place, order, held=()):
    held = list(held)
    for bit in order:
        other = swap_bit(values, count, bit)
        held.append(bit)
        held.sort(reverse=True)
        after_bits = 2 ** (len(held) - 1 - held.index(bit))
        upper = (place // bit) % 2 == 1
        width = values.shape[1]
        pieces = (2 ** (len(held) - 1) // after_bits, 1, -1, width)
        own, other = values.reshape(pieces), other.reshape(pieces)
        values = jnp.where(
            upper,
            jnp.concatenate([other, own], axis=1),
            jnp.concatenate([own, other], axis=1),
        ).reshape(-1, width)
    return values


def muon_update(weight, ortho):
    return weight * (1.0 - MUON_RATE * WEIGHT_DECAY) - MUON_RATE * MUON_SHAPE * math.sqrt(D) * ortho


def shards(
    tokens,
    out_grad,
    lengths,
    routes,
    attn_weight,
    router_weight,
    expert_weight,
    gains,
    attn_moment,
    router_moment,
    expert_moment,
    gain_first,
    gain_second,
    attn_ema,
    router_ema,
    expert_ema,
    gain_ema,
):
    seqs_here = lengths.shape[0]
    tok_here = tokens.shape[0]
    seq_len = tok_here // seqs_here
    query_width = HEADS * HEAD_DIM
    kv_width = KV_HEADS * HEAD_DIM
    qkv_width = query_width + 2 * kv_width
    n_dp, n_blk = lax.axis_size("dp"), lax.axis_size("blk")
    count = n_dp * n_blk
    place = lax.axis_index(AXES)
    own_rows = expert_weight.shape[1]
    parts = D // own_rows
    half_bit, pair_bit = parts // 2, n_blk
    bit_z, bit_x, bit_y = [bit for bit in bits_below(parts, count) if bit != pair_bit]
    low_bits = bits_below(1, parts)
    upper_half = (place // half_bit) % 2 == 1
    groups = ((0, 0), (1, 0), (1, 1), (0, 1))
    far_bits = [
        far_x * bit_x + far_y * bit_y + far_z * bit_z
        for far_x, far_y in groups
        for far_z in range(2)
    ]
    own_experts = [(place ^ bits) // parts for bits in far_bits]
    pair_experts = [(place ^ pair_bit ^ bits) // parts for bits in far_bits]
    expert_ids = jnp.stack(own_experts + pair_experts)

    def relative(values):
        swapped = jnp.concatenate([values[:, HALF:], values[:, :HALF]], axis=1)
        return jnp.where(upper_half, swapped, values)

    attn_cols = attn_weight.shape[1]
    attn_low = attn_weight.astype(jnp.bfloat16)
    small_low = jnp.concatenate(
        [
            router_weight.astype(jnp.bfloat16),
            gains.astype(jnp.bfloat16).T,
            jnp.zeros((attn_weight.shape[0], PACK - EXPERTS - 2), jnp.bfloat16),
        ],
        axis=1,
    )
    full_packed = lax.all_gather(
        jnp.concatenate([attn_low, small_low], axis=1), AXES, axis=0, tiled=True
    )
    w_query = full_packed[:, :query_width]
    w_shared = full_packed[:, query_width:qkv_width]
    w_out = full_packed[:, qkv_width:attn_cols]
    full_router = full_packed[:, attn_cols : attn_cols + EXPERTS]
    full_gains = full_packed[:, attn_cols + EXPERTS : attn_cols + EXPERTS + 2].T
    early_bits = bits_below(1, half_bit)
    own_half = gather_rows(expert_weight.astype(jnp.bfloat16), 1, count, place, early_bits)
    level_one = (((1, 0, 0), half_bit), ((0, 1, 0), bit_x), ((0, 0, 1), bit_y))
    level_two = (((1, 1, 0), bit_x), ((0, 1, 1), bit_y), ((1, 0, 1), half_bit))
    hop_of = {half_bit: 0, bit_x: 1, bit_y: 2}

    def before_hop(chunk, bit):
        return tuple(
            side ^ 1 if index == hop_of[bit] else side for index, side in enumerate(chunk)
        )

    chunks = {(0, 0, 0): jnp.stack([own_half, swap_bit(own_half, count, bit_z)], axis=1)}
    for chunk, bit in level_one:
        chunks[chunk] = swap_bit(chunks[before_hop(chunk, bit)], count, bit)
    gain_one = full_gains[0].astype(jnp.float32)
    gain_two = full_gains[1].astype(jnp.float32)
    inputs = tokens.astype(jnp.float32)
    cosine, sine = rotary_tables(seq_len, HEAD_DIM)
    cosine = jnp.concatenate([cosine] * 4, axis=1)
    sine = jnp.concatenate([-sine, sine, -sine, sine], axis=1)
    normed_one, query, key_rows, value_rows = project_call(
        tokens, gain_one[None], full_packed, full_packed, cosine, sine
    )
    position = jnp.arange(seq_len)
    live_rows = (position[None, :] < lengths[:, None]).reshape(tok_here, 1)
    live_grad = jnp.where(live_rows, out_grad, jnp.zeros_like(out_grad))
    live_relative = after(relative(live_grad), normed_one)
    both_grad = jnp.concatenate([live_relative, swap_bit(live_relative, count, pair_bit)])
    rows_each = attn_moment.shape[0]
    block_width = attn_cols // 3

    def spread(values):
        return lax.all_to_all(values, "blk", split_axis=0, concat_axis=0, tiled=True)

    old_pieces = [attn_moment[:, :block_width], attn_moment[:, block_width : 2 * block_width]]
    old_pieces += [
        attn_moment[:, 2 * block_width :],
        jnp.pad(router_moment, ((0, 0), (0, block_width - EXPERTS))),
    ]
    old_tasks = jnp.pad(jnp.stack(old_pieces), ((0, n_blk - 4), (0, 0), (0, 0)))
    old_tasks = spread(old_tasks).reshape(n_blk * rows_each, block_width)
    attended, totals = attend_call(
        lengths,
        query,
        key_rows,
        value_rows,
        seq_len,
        [chunks[0, 0, 0], old_tasks],
    )
    branch = plain_dot(attended, w_out, 1, 1)
    for chunk, bit in level_two:
        chunks[chunk] = swap_bit(after(chunks[before_hop(chunk, bit)], branch), count, bit)
    hidden_state = inputs + RESID_MULT * branch
    scale_two = lax.rsqrt(jnp.mean(hidden_state * hidden_state, axis=-1, keepdims=True) + NORM_EPS)
    unit_two = hidden_state * scale_two
    normed_two = (unit_two * gain_two).astype(jnp.bfloat16)
    pick = (jnp.arange(EXPERTS)[:, None] == expert_ids[None, :]).astype(jnp.bfloat16)
    router_here = jnp.dot(full_router, pick, preferred_element_type=jnp.float32).astype(
        jnp.bfloat16
    )
    logits = jnp.dot(normed_two, router_here, preferred_element_type=jnp.float32)
    used = jnp.any(routes[:, :, None] == expert_ids[None, None, :], axis=1)
    chosen_top = jnp.max(jnp.where(used, logits, NEG_FILL), axis=1, keepdims=True)
    exponent = jnp.where(used, jnp.exp(jnp.where(used, logits - chosen_top, 0.0)), 0.0)
    gate_weights = exponent / jnp.sum(exponent, axis=1, keepdims=True)
    second = relative(normed_two)
    other_second = swap_bit(second, count, pair_bit)
    gates_here = jnp.pad(gate_weights[:, :8], ((0, 0), (0, PACK - 8)))
    gates_there = jnp.pad(gate_weights[:, 8:], ((0, 0), (0, PACK - 8)))
    other_gates = swap_bit(gates_there, count, pair_bit)
    both_second = jnp.concatenate([second, other_second])
    both_gates = jnp.concatenate([gates_here, other_gates])
    own_parts, pair_parts, dgates = [], [], []
    grads, moved = {}, {}

    def send(chunk, bit):
        moved[chunk] = swap_bit(grads[chunk], count, bit)

    waits = {
        (0, 0): lambda: [chunks[0, 1, 0], chunks[0, 0, 1]],
        (1, 0): lambda: [chunks[0, 1, 1], chunks[1, 0, 1]],
        (1, 1): lambda: [moved[1, 0, 0], pair_parts[0]],
        (0, 1): lambda: [moved[1, 1, 0], pair_parts[1]],
    }
    for turn_index, (far_x, far_y) in enumerate(groups):
        weights = [chunks[half, far_x, far_y] for half in range(2)]
        own_part, pair_part, dgate, grad_own, grad_other = expert_call(
            2 * turn_index,
            both_second,
            both_grad,
            both_gates,
            weights,
            waits[far_x, far_y](),
        )
        own_parts.append(own_part)
        pair_parts.append(swap_bit(pair_part, count, pair_bit))
        dgates.append(dgate)
        grads[0, far_x, far_y] = grad_own
        grads[1, far_x, far_y] = grad_other
        if (far_x, far_y) == (0, 0):
            send((1, 0, 0), half_bit)
            chunks[1, 1, 1] = swap_bit(after(chunks[1, 0, 1], own_part), count, bit_x)
        if (far_x, far_y) == (1, 0):
            send((1, 1, 0), half_bit)
        if (far_x, far_y) == (1, 1):
            send((1, 1, 1), bit_x)
            send((0, 1, 1), bit_y)

    def total_of(*pieces):
        total = pieces[0].astype(jnp.float32)
        for piece in pieces[1:]:
            total = total + piece.astype(jnp.float32)
        return total.astype(jnp.bfloat16)

    last_other, grads[0, 0, 1], own_parts[3], dgates[3], *others = (
        lax.optimization_barrier(
            (
                grads[1, 0, 1],
                grads[0, 0, 1],
                own_parts[3],
                dgates[3],
                moved[1, 1, 1],
                moved[0, 1, 1],
                pair_parts[2],
            )
        )
    )
    moved[1, 1, 1], moved[0, 1, 1], pair_parts[2] = others
    half_y = [
        swap_bit(total_of(last_other[kind], moved[1, 1, 1][kind]), count, half_bit)
        for kind in range(3)
    ]
    grads[0, 1, 0] = total_of(grads[0, 1, 0], moved[1, 1, 0], moved[0, 1, 1])
    send((0, 1, 0), bit_x)
    dgate_sum = (dgates[0] + dgates[1]) + (dgates[2] + dgates[3])
    pair_dgates = swap_bit(dgate_sum[tok_here:], count, pair_bit)

    def gather_sum(parts):
        total = None
        for part in parts:
            part = part.astype(jnp.float32)
            total = part if total is None else total + part
        return relative(total)

    grad_normed_two = gather_sum([part[1] for part in own_parts + pair_parts])
    grad_gates = jnp.concatenate([dgate_sum[:tok_here, :8], pair_dgates[:, :8]], axis=1)
    grad_out = live_grad.astype(jnp.float32)
    inner_sum = jnp.sum(gate_weights * grad_gates, axis=1, keepdims=True)
    grad_logits = (gate_weights * (grad_gates - inner_sum)).astype(jnp.bfloat16)
    grad_normed_two = grad_normed_two + plain_dot(grad_logits, router_here, 1, 1)
    grad_router = jnp.matmul(
        plain_dot(normed_two, grad_logits, 0, 0),
        pick.astype(jnp.float32).T,
        precision=lax.Precision.HIGHEST,
    )
    grad_hidden_state = grad_out + norm_back(grad_normed_two, unit_two, scale_two, gain_two)
    grad_gain_two = jnp.sum(grad_normed_two * unit_two, axis=0)
    grad_branch = (RESID_MULT * grad_hidden_state).astype(jnp.bfloat16)
    grad_w_out = plain_dot(grad_branch, attended, 0, 0)
    dp_bits = bits_below(n_blk, count)
    far_dp = [bit for bit in dp_bits if bit not in (pair_bit, bit_x, bit_y)]
    first_x = [pair_bit, bit_x, bit_y] + far_dp
    first_y = [pair_bit, bit_y, bit_x] + far_dp

    def to_dp(values, order):
        return reduce_to_owner(values, dp_bits, count, place, order)

    low_grad_out = pin(grad_w_out.astype(jnp.bfloat16))
    grad_attended = jnp.dot(grad_branch, w_out, preferred_element_type=jnp.float32).astype(
        jnp.bfloat16
    )
    def attend_back(part, held, done):
        return attend_back_call(
            part,
            lengths,
            query,
            key_rows,
            value_rows,
            grad_attended,
            totals,
            cosine,
            sine,
            held,
            done,
        )

    first_heads = attend_back(0, [], [])
    last_own, half_y[:2], _ = lax.optimization_barrier(
        (grads[0, 0, 1], half_y[:2], first_heads[0])
    )
    grad_query, grad_key, grad_value = attend_back(1, first_heads, half_y[:2] + [moved[0, 1, 0]])
    half_y[2], _ = lax.optimization_barrier((half_y[2], grad_query))
    from_y = [
        swap_bit(total_of(last_own[kind], half_y[kind]), count, bit_y) for kind in range(3)
    ]
    late_parts = after(tuple(own_parts + pair_parts), grad_query)
    block_out = (hidden_state + RESID_MULT * gather_sum([part[0] for part in late_parts])).astype(
        jnp.bfloat16
    )
    grad_query, from_y[0] = lax.optimization_barrier((grad_query, from_y[0]))
    low_grad = [
        pin(plain_dot(normed_one, piece, 0, 0).astype(jnp.bfloat16))
        for piece in (grad_query, grad_key, grad_value)
    ]
    grad_normed_one = (
        plain_dot(grad_query, w_query, 1, 1)
        + plain_dot(grad_key, w_shared[:, :kv_width], 1, 1)
        + plain_dot(grad_value, w_shared[:, kv_width:], 1, 1)
    )
    nearest, from_y[:2], grad_normed_one, low_grad[1:] = lax.optimization_barrier(
        (grads[0, 0, 0], from_y[:2], grad_normed_one, low_grad[1:])
    )
    scale_one = lax.rsqrt(jnp.mean(inputs * inputs, axis=-1, keepdims=True) + NORM_EPS)
    unit_one = inputs * scale_one
    input_grad = grad_hidden_state + norm_back(grad_normed_one, unit_one, scale_one, gain_one)
    grad_gain_one = jnp.sum(grad_normed_one * unit_one, axis=0)
    grad_small = jnp.concatenate(
        [
            grad_router,
            jnp.stack([grad_gain_one, grad_gain_two], axis=1),
            jnp.zeros((D, PACK - EXPERTS - 2), jnp.float32),
        ],
        axis=1,
    ).astype(jnp.bfloat16)
    wide_sum = to_dp(
        jnp.concatenate([low_grad[0], after(low_grad_out, grad_query)], axis=1), first_x
    )
    query_sum, out_sum = wide_sum[:, :query_width], wide_sum[:, query_width:]
    shared_sum = to_dp(jnp.concatenate([low_grad[1], low_grad[2], pin(grad_small)], axis=1), first_y)

    def as_tasks(first, second, third, small):
        small = jnp.pad(small, ((0, 0), (0, block_width - PACK)))
        tasks = jnp.stack([first, second, third, small])
        return jnp.pad(tasks, ((0, n_blk - 4), (0, 0), (0, 0)))

    task_parts = spread(
        as_tasks(
            query_sum, shared_sum[:, :block_width], out_sum, shared_sum[:, block_width:]
        )
    )
    task_block = MOMENTUM * old_tasks + jnp.sum(task_parts.astype(jnp.float32), axis=0)
    moment_rows = spread(task_block.reshape(n_blk, rows_each, block_width))
    moment_attn = jnp.concatenate([moment_rows[0], moment_rows[1], moment_rows[2]], axis=1)
    moment_router = moment_rows[3][:, :EXPERTS]
    gain_grad = moment_rows[3][:, EXPERTS : EXPERTS + 2].T
    used_columns = (jnp.arange(block_width) < EXPERTS) | (lax.axis_index("blk") != 3)
    task_block = jnp.where(used_columns, task_block, 0.0)
    wide_x, wide_y = far_dp + [bit_y, bit_x], far_dp + [bit_x, bit_y]
    sides = [
        gather_from_owners(task_block[:, : block_width // 2], count, place, wide_x),
        gather_from_owners(task_block[:, block_width // 2 :], count, place, wide_y),
    ]
    attn_block = jnp.concatenate(
        [gather_from_owners(side, count, place, [pair_bit], wide_x) for side in sides], axis=1
    )
    from_y[2] = after(from_y[2], wide_sum)
    expert_sums = [
        total_of(nearest[kind], moved[1, 0, 0][kind], moved[0, 1, 0][kind], from_y[kind])
        for kind in range(3)
    ]
    moment_expert, group_rows = [], []
    for kind in range(3):
        total = after(expert_sums[kind], wide_sum, shared_sum)
        from_z = after(swap_bit(expert_sums[kind][1], count, bit_z), wide_sum, shared_sum)
        total = total[0].astype(jnp.float32) + from_z.astype(jnp.float32)
        total = total.T if kind == 2 else total
        if early_bits:
            total = reduce_rows(total.astype(jnp.bfloat16), count, place, early_bits[::-1])
        moment = MOMENTUM * expert_moment[kind] + total.astype(jnp.float32)
        rows = pin(moment)
        for bit in low_bits[:-1]:
            rows = jnp.concatenate([rows, swap_bit(rows, count, bit)])
        moment_expert.append(moment)
        group_rows.append((rows, swap_bit(rows, count, low_bits[-1])))
    attn_block = after(attn_block, *moment_expert)
    attn_iter = ortho_block_call(attn_block, (lax.axis_index("blk") == 1).astype(jnp.int32))
    group_rows = after(tuple(group_rows), attn_iter)
    group_rows = jnp.stack([jnp.concatenate(pieces) for pieces in group_rows])
    ortho_expert = ortho_rows_call(group_rows, own_rows)
    returned = lax.dynamic_slice_in_dim(
        attn_iter, lax.axis_index("dp") * (n_blk * rows_each), n_blk * rows_each, 0
    )
    returned = spread(returned.reshape(n_blk, rows_each, block_width))
    ortho_attn = jnp.concatenate([returned[0], returned[1], returned[2]], axis=1)
    ortho_router = returned[3][:, :EXPERTS]
    moment_expert = jnp.stack(moment_expert)
    attn_new = muon_update(attn_weight, ortho_attn)
    router_new = muon_update(router_weight, ortho_router)
    expert_new = muon_update(expert_weight, ortho_expert)
    first_new = BETA_ONE * gain_first + (1.0 - BETA_ONE) * gain_grad
    second_new = BETA_TWO * gain_second + (1.0 - BETA_TWO) * gain_grad * gain_grad
    corrected_first = first_new / (1.0 - BETA_ONE**STEP)
    corrected_second = second_new / (1.0 - BETA_TWO**STEP)
    gain_new = gains - ADAM_RATE * corrected_first / (jnp.sqrt(corrected_second) + ADAM_EPS)
    return (
        block_out,
        input_grad,
        moment_attn,
        moment_router,
        moment_expert,
        attn_new,
        router_new,
        expert_new,
        attn_new.astype(jnp.bfloat16),
        router_new.astype(jnp.bfloat16),
        expert_new.astype(jnp.bfloat16),
        EMA_KEEP * attn_ema + (1.0 - EMA_KEEP) * attn_new,
        EMA_KEEP * router_ema + (1.0 - EMA_KEEP) * router_new,
        EMA_KEEP * expert_ema + (1.0 - EMA_KEEP) * expert_new,
        first_new,
        second_new,
        gain_new,
        gain_new.astype(jnp.bfloat16),
        GAIN_EMA_KEEP * gain_ema + (1.0 - GAIN_EMA_KEEP) * gain_new,
    )


def solution(mesh):
    placed = (
        P(("dp", "blk"), None),
        P(("dp", "blk"), None),
        P(("dp", "blk")),
        P(("dp", "blk"), None),
        P(("dp", "blk"), None),
        P(("dp", "blk"), None),
        P(None, ("dp", "blk"), None),
        P(None, ("dp", "blk")),
        P(("dp", "blk"), None),
        P(("dp", "blk"), None),
        P(None, ("dp", "blk"), None),
        P(None, ("dp", "blk")),
        P(None, ("dp", "blk")),
        P(("dp", "blk"), None),
        P(("dp", "blk"), None),
        P(None, ("dp", "blk"), None),
        P(None, ("dp", "blk")),
    )
    return jax.shard_map(
        shards,
        mesh=mesh,
        in_specs=placed,
        out_specs=(
            P(("dp", "blk"), None),
            P(("dp", "blk"), None),
            P(("dp", "blk"), None),
            P(("dp", "blk"), None),
            P(None, ("dp", "blk"), None),
            P(("dp", "blk"), None),
            P(("dp", "blk"), None),
            P(None, ("dp", "blk"), None),
            P(("dp", "blk"), None),
            P(("dp", "blk"), None),
            P(None, ("dp", "blk"), None),
            P(("dp", "blk"), None),
            P(("dp", "blk"), None),
            P(None, ("dp", "blk"), None),
            P(None, ("dp", "blk")),
            P(None, ("dp", "blk")),
            P(None, ("dp", "blk")),
            P(None, ("dp", "blk")),
            P(None, ("dp", "blk")),
        ),
        check_vma=False,
    )
```

```python
import functools
import math

import jax
import jax.numpy as jnp
from jax import lax
from jax.experimental import pallas as pl
from jax.experimental.layout import Layout, with_layout_constraint
from jax.experimental.pallas import tpu as pltpu
from jax.sharding import PartitionSpec as P

D = 1024
HEADS = 16
KV_HEADS = 8
HEAD_DIM = 64
FF = 512
TOP = 8
EXPERTS = 16
STEP = 10
HALF = D // 2
PACK = 128
AXES = ("dp", "blk")


NORM_EPS = 1e-05
ATTN_MULT = 0.015625
RESID_MULT = 0.22
ROPE_BASE = 10000.0
NEG_FILL = -1e30
POLY_ONE = 3.4445
POLY_TWO = -4.775
POLY_THREE = 2.0315
ORTHO_EPS = 1e-07
MOMENTUM = 0.95
MUON_RATE = 0.6
MUON_SHAPE = 0.2
WEIGHT_DECAY = 0.01
ADAM_RATE = 0.8
BETA_ONE = 0.9
BETA_TWO = 0.95
ADAM_EPS = 1e-08
EMA_KEEP = 0.9
GAIN_EMA_KEEP = 0.6


def plain_dot(left_side, right_side, contract_left, contract_right):
    return lax.dot_general(
        left_side,
        right_side,
        (((contract_left,), (contract_right,)), ((), ())),
        preferred_element_type=jnp.float32,
    )


def rotary_tables(length, head_width):
    position = jnp.arange(length).astype(jnp.float32)
    inverse = ROPE_BASE ** (-jnp.arange(0, head_width, 2).astype(jnp.float32) / head_width)
    angles = position[:, None] * inverse[None, :]
    return (jnp.cos(angles), jnp.sin(angles))


def norm_back(grad_normed, unit_rows, scale_rows, gain_row):
    grad_unit = grad_normed * gain_row
    return scale_rows * (
        grad_unit - unit_rows * jnp.mean(grad_unit * unit_rows, axis=-1, keepdims=True)
    )


def pin(values):
    return with_layout_constraint(values, Layout(major_to_minor=tuple(range(values.ndim))))


def swap_bit(values, count, bit):
    pairs = [(place, place ^ bit) for place in range(count)]
    return pin(lax.ppermute(pin(values), AXES, pairs))


def after(values, *done):
    return lax.optimization_barrier((values,) + done)[0]


def low_add(left_side, right_side):
    return (left_side.astype(jnp.float32) + right_side.astype(jnp.float32)).astype(jnp.bfloat16)


def bits_below(low_bit, high_bit):
    bits = []
    while low_bit < high_bit:
        bits.append(low_bit)
        low_bit *= 2
    return bits


def gather_rows(values, axis, count, place, bits):
    for bit in bits:
        other = swap_bit(values, count, bit)
        upper = (place // bit) % 2 == 1
        values = jnp.where(
            upper,
            jnp.concatenate([other, values], axis=axis),
            jnp.concatenate([values, other], axis=axis),
        )
    return values


def reduce_rows(values, count, place, bits):
    for bit in bits:
        split = values.reshape((2, values.shape[0] // 2) + values.shape[1:])
        own = (place // bit) % 2
        keep = lax.dynamic_index_in_dim(split, own, 0, keepdims=False)
        other = swap_bit(
            lax.dynamic_index_in_dim(split, 1 - own, 0, keepdims=False), count, bit
        )
        values = low_add(keep, other)
    return values


def dot_nn(left_side, right_side):
    return plain_dot(left_side, right_side, 1, 0)


def dot_nt(left_side, right_side):
    return plain_dot(left_side, right_side, 1, 1)


def dot_tn(left_side, right_side):
    return plain_dot(left_side, right_side, 0, 0)


def turn(values, cosine, sine, lanes):
    far = jnp.where(
        lanes % HEAD_DIM < HEAD_DIM // 2,
        pltpu.roll(values, PACK - HEAD_DIM // 2, 1),
        pltpu.roll(values, HEAD_DIM // 2, 1),
    )
    return values * cosine + far * sine


def project_kernel(
    tok_ref, gain_ref, wq_ref, wkv_ref, cos_ref, sin_ref, norm_ref, q_ref, k_ref, v_ref
):
    rows = tok_ref.shape[0]
    inputs = tok_ref[...].astype(jnp.float32)
    scale = lax.rsqrt(jnp.mean(inputs * inputs, axis=-1, keepdims=True) + NORM_EPS)
    normed = (inputs * scale * gain_ref[...]).astype(jnp.bfloat16)
    norm_ref[...] = normed
    cosine, sine = cos_ref[...], sin_ref[...]
    lanes = lax.broadcasted_iota(jnp.int32, (rows, PACK), 1)
    query = dot_nn(normed, wq_ref[...])
    for start in range(0, HEADS * HEAD_DIM, PACK):
        turned = turn(query[:, start : start + PACK], cosine, sine, lanes)
        q_ref[:, start : start + PACK] = turned.astype(jnp.bfloat16) * ATTN_MULT
    both = dot_nn(normed, wkv_ref[...])
    width = KV_HEADS * HEAD_DIM
    for start in range(0, width, PACK):
        turned = turn(both[:, start : start + PACK], cosine, sine, lanes)
        k_ref[:, start : start + PACK] = turned.astype(jnp.bfloat16)
    v_ref[...] = both[:, width:].astype(jnp.bfloat16)


def project_call(tokens, gain_row, wq, wkv, cosine, sine):
    seq_rows = cosine.shape[0]
    rows = min(256, seq_rows)
    repeats = seq_rows // rows
    tok_here = tokens.shape[0]
    width = KV_HEADS * HEAD_DIM
    low = jnp.bfloat16
    return pl.pallas_call(
        project_kernel,
        grid=(tok_here // rows,),
        in_specs=[
            pl.BlockSpec((rows, D), lambda b: (b, 0)),
            pl.BlockSpec((1, D), lambda b: (0, 0)),
            pl.BlockSpec((D, HEADS * HEAD_DIM), lambda b: (0, 0)),
            pl.BlockSpec((D, 2 * width), lambda b: (0, 1)),
            pl.BlockSpec((rows, PACK), lambda b: (b % repeats, 0)),
            pl.BlockSpec((rows, PACK), lambda b: (b % repeats, 0)),
        ],
        out_specs=[
            pl.BlockSpec((rows, D), lambda b: (b, 0)),
            pl.BlockSpec((rows, HEADS * HEAD_DIM), lambda b: (b, 0)),
            pl.BlockSpec((rows, width), lambda b: (b, 0)),
            pl.BlockSpec((rows, width), lambda b: (b, 0)),
        ],
        out_shape=[
            jax.ShapeDtypeStruct((tok_here, D), low),
            jax.ShapeDtypeStruct((tok_here, HEADS * HEAD_DIM), low),
            jax.ShapeDtypeStruct((tok_here, width), low),
            jax.ShapeDtypeStruct((tok_here, width), low),
        ],
        compiler_params=pltpu.CompilerParams(
            dimension_semantics=("arbitrary",), vmem_limit_bytes=40 * 1024 * 1024
        ),
        cost_estimate=pl.CostEstimate(
            flops=8_000_000_000, bytes_accessed=14_000_000, transcendentals=0
        ),
        name="project",
    )(tokens, gain_row, wq, wkv, cosine, sine)


def attend_kernel(len_ref, q_ref, k_ref, v_ref, *refs):
    o_ref, lse_ref = refs[-2:]
    seq_len = q_ref.shape[0]
    rows = min(256, seq_len)
    length = len_ref[0, 0]
    for first in range(0, seq_len, rows):
        keys = first + rows
        key_index = lax.broadcasted_iota(jnp.int32, (rows, keys), 1)
        query_index = first + lax.broadcasted_iota(jnp.int32, (rows, keys), 0)
        bias = jnp.where((key_index <= query_index) & (key_index < length), 0.0, NEG_FILL)
        lanes = lax.broadcasted_iota(jnp.int32, (rows, PACK), 1)
        totals = jnp.zeros((rows, PACK), jnp.float32)
        for head in range(4):
            shared = (head // 2) * HEAD_DIM
            key_rows = k_ref[:keys, shared : shared + HEAD_DIM]
            value_rows = v_ref[:keys, shared : shared + HEAD_DIM]
            query = q_ref[first:keys, head * HEAD_DIM : (head + 1) * HEAD_DIM]
            scores = dot_nt(query, key_rows) + bias
            largest = jnp.max(scores, axis=1, keepdims=True)
            exponent = jnp.exp(scores - largest)
            total = jnp.sum(exponent, axis=1, keepdims=True)
            probability = (exponent * (1.0 / total)).astype(jnp.bfloat16)
            o_ref[first:keys, head * HEAD_DIM : (head + 1) * HEAD_DIM] = dot_nn(
                probability, value_rows
            ).astype(jnp.bfloat16)
            totals = jnp.where(lanes == head, largest + jnp.log(total), totals)
        lse_ref[0, :, first:keys] = totals.T[:8]


def attend_call(lengths, query, key_rows, value_rows, seq_len, done):
    tok_here = query.shape[0]
    seqs = tok_here // seq_len
    groups = KV_HEADS // 2
    return pl.pallas_call(
        attend_kernel,
        grid=(seqs, groups),
        in_specs=[
            pl.BlockSpec((1, 1), lambda s, g: (s, 0), memory_space=pltpu.SMEM),
            pl.BlockSpec((seq_len, 4 * HEAD_DIM), lambda s, g: (s, g)),
            pl.BlockSpec((seq_len, PACK), lambda s, g: (s, g)),
            pl.BlockSpec((seq_len, PACK), lambda s, g: (s, g)),
        ]
        + [pl.BlockSpec(memory_space=pl.ANY)] * len(done),
        out_specs=[
            pl.BlockSpec((seq_len, 4 * HEAD_DIM), lambda s, g: (s, g)),
            pl.BlockSpec((1, 8, seq_len), lambda s, g: (g, 0, s)),
        ],
        out_shape=[
            jax.ShapeDtypeStruct((tok_here, HEADS * HEAD_DIM), jnp.bfloat16),
            jax.ShapeDtypeStruct((groups, 8, tok_here), jnp.float32),
        ],
        compiler_params=pltpu.CompilerParams(
            dimension_semantics=("arbitrary", "arbitrary"), vmem_limit_bytes=40 * 1024 * 1024
        ),
        cost_estimate=pl.CostEstimate(
            flops=20_000_000_000, bytes_accessed=8_000_000, transcendentals=12_000_000
        ),
        name="attend",
    )(lengths.reshape(seqs, 1), query, key_rows, value_rows, *done)


def attend_back_kernel(
    len_ref,
    q_ref,
    k_ref,
    v_ref,
    do_ref,
    lse_ref,
    cos_ref,
    sin_ref,
    *refs,
):
    dq_ref, dk_ref, dv_ref, k_acc, v_acc = refs[-5:]
    seq_len = q_ref.shape[0]
    rows = min(256, seq_len)
    length = len_ref[0, 0]
    k_acc[...] = jnp.zeros_like(k_acc)
    v_acc[...] = jnp.zeros_like(v_acc)
    lanes = lax.broadcasted_iota(jnp.int32, (rows, PACK), 1)
    turned_keys = [
        k_ref[:, shared : shared + HEAD_DIM].T for shared in (0, HEAD_DIM)
    ]
    for first in range(0, seq_len, rows):
        keys = first + rows
        key_index = lax.broadcasted_iota(jnp.int32, (keys, rows), 0)
        query_index = first + lax.broadcasted_iota(jnp.int32, (keys, rows), 1)
        bias = jnp.where((key_index <= query_index) & (key_index < length), 0.0, NEG_FILL)
        for pair in range(2):
            shared = pair * HEAD_DIM
            key_rows = k_ref[:keys, shared : shared + HEAD_DIM]
            value_rows = v_ref[:keys, shared : shared + HEAD_DIM]
            key_grad = None
            value_grad = None
            query_grads = []
            for head in (2 * pair, 2 * pair + 1):
                query = q_ref[first:keys, head * HEAD_DIM : (head + 1) * HEAD_DIM]
                grad = do_ref[first:keys, head * HEAD_DIM : (head + 1) * HEAD_DIM]
                scores = dot_nt(key_rows, query) + bias
                probability = jnp.exp(scores - lse_ref[0, head : head + 1, first:keys])
                prob_grad = dot_nt(value_rows, grad)
                inner = jnp.sum(probability * prob_grad, axis=0, keepdims=True)
                score_grad = (probability * (prob_grad - inner)).astype(jnp.bfloat16)
                key_part = dot_nn(score_grad, query)
                value_part = dot_nn(probability.astype(jnp.bfloat16), grad)
                key_grad = key_part if key_grad is None else key_grad + key_part
                value_grad = value_part if value_grad is None else value_grad + value_part
                query_grads.append(dot_nn(turned_keys[pair][:, :keys], score_grad))
            k_acc[:keys, shared : shared + HEAD_DIM] += key_grad
            v_acc[:keys, shared : shared + HEAD_DIM] += value_grad
            query_grad = jnp.concatenate(query_grads, axis=0).T * ATTN_MULT
            dq_ref[first:keys, pair * PACK : (pair + 1) * PACK] = turn(
                query_grad, cos_ref[first:keys, :], -sin_ref[first:keys, :], lanes
            ).astype(jnp.bfloat16)
    for first in range(0, seq_len, rows):
        keys = first + rows
        dk_ref[first:keys, :] = turn(
            k_acc[first:keys, :], cos_ref[first:keys, :], -sin_ref[first:keys, :], lanes
        ).astype(jnp.bfloat16)
        dv_ref[first:keys, :] = v_acc[first:keys, :].astype(jnp.bfloat16)


def attend_back_call(
    part, lengths, query, key_rows, value_rows, grad, totals, cosine, sine, held, done
):
    tok_here = query.shape[0]
    seq_len = cosine.shape[0]
    seqs = tok_here // seq_len
    groups = KV_HEADS // 4
    skip = part * groups
    wide = pl.BlockSpec((seq_len, 4 * HEAD_DIM), lambda s, g: (s, g + skip))
    narrow = pl.BlockSpec((seq_len, PACK), lambda s, g: (s, g + skip))
    table = pl.BlockSpec((seq_len, PACK), lambda s, g: (0, 0))
    return pl.pallas_call(
        attend_back_kernel,
        grid=(seqs, groups),
        in_specs=[
            pl.BlockSpec((1, 1), lambda s, g: (s, 0), memory_space=pltpu.SMEM),
            wide,
            narrow,
            narrow,
            wide,
            pl.BlockSpec((1, 8, seq_len), lambda s, g: (g + skip, 0, s)),
            table,
            table,
        ]
        + [pl.BlockSpec(memory_space=pl.ANY)] * (len(held) + len(done)),
        out_specs=[wide, narrow, narrow],
        out_shape=[
            jax.ShapeDtypeStruct((tok_here, HEADS * HEAD_DIM), jnp.bfloat16),
            jax.ShapeDtypeStruct((tok_here, KV_HEADS * HEAD_DIM), jnp.bfloat16),
            jax.ShapeDtypeStruct((tok_here, KV_HEADS * HEAD_DIM), jnp.bfloat16),
        ],
        input_output_aliases={8 + index: index for index in range(len(held))},
        scratch_shapes=[
            pltpu.VMEM((seq_len, PACK), jnp.float32),
            pltpu.VMEM((seq_len, PACK), jnp.float32),
        ],
        compiler_params=pltpu.CompilerParams(
            dimension_semantics=("arbitrary", "arbitrary"), vmem_limit_bytes=40 * 1024 * 1024
        ),
        cost_estimate=pl.CostEstimate(
            flops=24_000_000_000, bytes_accessed=8_000_000, transcendentals=6_000_000
        ),
        name="attend_back",
    )(
        lengths.reshape(seqs, 1),
        query,
        key_rows,
        value_rows,
        grad,
        totals,
        cosine,
        sine,
        *held,
        *done,
    )


def expert_kernel(waits, first, *refs):
    n2_ref, dy_ref, gate_ref = refs[:3]
    own_w_ref, other_w_ref = refs[3:5]
    outs = refs[5 + waits :]
    own_ref, pair_ref, dgate_ref, grad_own_ref, grad_other_ref = outs[:5]
    m_acc, dn_acc, g_acc, u_acc, d_acc, turned_ref = outs[5:]
    step = pl.program_id(0)
    block = pl.program_id(1)
    blocks = pl.num_programs(1)
    rows = n2_ref.shape[0]
    place = pl.ds(pl.multiple_of(block * rows, rows), rows)
    lane = lax.broadcasted_iota(jnp.int32, (rows, PACK), 1)

    @pl.when(step == 0)
    def _():
        turned_ref[:, place] = n2_ref[...].T

    wg_own, wg_other = own_w_ref[0, 0], other_w_ref[0, 0]
    wu_own, wu_other = own_w_ref[1, 0], other_w_ref[1, 0]
    wd_own, wd_other = own_w_ref[2, 0], other_w_ref[2, 0]
    column = lane == step + first
    gate = jnp.sum(jnp.where(column, gate_ref[...], 0.0), axis=1, keepdims=True)
    dm = RESID_MULT * dy_ref[...].astype(jnp.float32)
    dout = (gate * dm).astype(jnp.bfloat16)
    ug = dot_nn(n2_ref[:, :HALF], wg_own) + dot_nn(n2_ref[:, HALF:], wg_other)
    uu = dot_nn(n2_ref[:, :HALF], wu_own) + dot_nn(n2_ref[:, HALF:], wu_other)
    dh = dot_nn(dout[:, :HALF], wd_own) + dot_nn(dout[:, HALF:], wd_other)
    sig = 1.0 / (1.0 + jnp.exp(-ug))
    silu = ug * sig
    hidden = (silu * uu).astype(jnp.bfloat16)
    dug = (dh * uu * sig * (1.0 + ug * (1.0 - sig))).astype(jnp.bfloat16)
    duu = (dh * silu).astype(jnp.bfloat16)
    y_own = dot_nt(hidden, wd_own)
    y_other = dot_nt(hidden, wd_other)
    n2t = turned_ref[:, place]
    g_acc[...] = jnp.where(block == 0, 0.0, g_acc[...]) + dot_nn(n2t, dug)
    dgate = jnp.sum(dm[:, :HALF] * y_own, axis=1, keepdims=True) + jnp.sum(
        dm[:, HALF:] * y_other, axis=1, keepdims=True
    )
    dgate_ref[place, :] = jnp.where(
        column, dgate, jnp.where(step == 0, 0.0, dgate_ref[place, :])
    )
    m_acc[place, :HALF] = jnp.where(step == 0, 0.0, m_acc[place, :HALF]) + gate * y_own
    m_acc[place, HALF:] = jnp.where(step == 0, 0.0, m_acc[place, HALF:]) + gate * y_other
    u_acc[...] = jnp.where(block == 0, 0.0, u_acc[...]) + dot_nn(n2t, duu)
    dn_acc[place, :HALF] = (
        jnp.where(step == 0, 0.0, dn_acc[place, :HALF]) + dot_nt(dug, wg_own) + dot_nt(duu, wu_own)
    )
    dn_acc[place, HALF:] = (
        jnp.where(step == 0, 0.0, dn_acc[place, HALF:])
        + dot_nt(dug, wg_other)
        + dot_nt(duu, wu_other)
    )
    d_acc[...] = jnp.where(block == 0, 0.0, d_acc[...]) + dot_tn(hidden, dout)
    last = step == pl.num_programs(0) - 1

    @pl.when(last & (block < blocks // 2))
    def _():
        own_ref[0] = m_acc[place, :].astype(jnp.bfloat16)
        own_ref[1] = dn_acc[place, :].astype(jnp.bfloat16)

    @pl.when(last & (block >= blocks // 2))
    def _():
        pair_ref[0] = m_acc[place, :].astype(jnp.bfloat16)
        pair_ref[1] = dn_acc[place, :].astype(jnp.bfloat16)

    @pl.when(block == blocks - 1)
    def _():
        grad_own_ref[0, 0] = g_acc[:HALF, :].astype(jnp.bfloat16)
        grad_own_ref[1, 0] = u_acc[:HALF, :].astype(jnp.bfloat16)
        grad_own_ref[2, 0] = d_acc[:, :HALF].astype(jnp.bfloat16)
        grad_other_ref[0, 0] = g_acc[HALF:, :].astype(jnp.bfloat16)
        grad_other_ref[1, 0] = u_acc[HALF:, :].astype(jnp.bfloat16)
        grad_other_ref[2, 0] = d_acc[:, HALF:].astype(jnp.bfloat16)


def expert_call(first, n2, dy, gates, weights, done):
    tokens_all = n2.shape[0]
    rows = min(512, tokens_all // 2)
    half_blocks = tokens_all // rows // 2
    steps = weights[0].shape[1]

    def own_block(step, block):
        return (0, jnp.where(step == steps - 1, jnp.minimum(block, half_blocks - 1), 0), 0)

    def pair_block(step, block):
        return (0, jnp.where(step == steps - 1, jnp.maximum(block - half_blocks, 0), 0), 0)

    low = jnp.bfloat16

    def pieces(kinds):
        return pl.BlockSpec((kinds, 1, HALF, FF), lambda s, b: (0, s, 0, 0))

    half_shape = jax.ShapeDtypeStruct((2, tokens_all // 2, D), low)
    piece_shape = jax.ShapeDtypeStruct((3, steps, HALF, FF), low)
    outputs = pl.pallas_call(
        functools.partial(expert_kernel, len(done), first),
        grid=(steps, 2 * half_blocks),
        in_specs=[
            pl.BlockSpec((rows, D), lambda s, b: (b, 0)),
            pl.BlockSpec((rows, D), lambda s, b: (b, 0)),
            pl.BlockSpec((rows, PACK), lambda s, b: (b, 0)),
            pieces(3),
            pieces(3),
        ]
        + [pl.BlockSpec(memory_space=pl.ANY)] * len(done),
        out_specs=[
            pl.BlockSpec((2, rows, D), own_block, pipeline_mode=pl.Buffered(1)),
            pl.BlockSpec((2, rows, D), pair_block, pipeline_mode=pl.Buffered(1)),
            pl.BlockSpec((tokens_all, PACK), lambda s, b: (0, 0)),
            pieces(3),
            pieces(3),
        ],
        out_shape=[
            half_shape,
            half_shape,
            jax.ShapeDtypeStruct((tokens_all, PACK), jnp.float32),
            piece_shape,
            piece_shape,
        ],
        scratch_shapes=[
            pltpu.VMEM((tokens_all, D), jnp.float32),
            pltpu.VMEM((tokens_all, D), jnp.float32),
            pltpu.VMEM((D, FF), jnp.float32),
            pltpu.VMEM((D, FF), jnp.float32),
            pltpu.VMEM((FF, D), jnp.float32),
            pltpu.VMEM((D, tokens_all), low),
        ],
        compiler_params=pltpu.CompilerParams(
            dimension_semantics=("arbitrary", "arbitrary"), vmem_limit_bytes=62 * 1024 * 1024
        ),
        cost_estimate=pl.CostEstimate(
            flops=9 * 2 * tokens_all * D * FF * steps * 3 // 2,
            bytes_accessed=48 * 1024 * 1024,
            transcendentals=steps * tokens_all * FF,
        ),
        name="experts",
    )(n2, dy, gates, *weights, *done)
    return outputs


def split_high(values):
    high = values.astype(jnp.bfloat16)
    return high, (values - high.astype(jnp.float32)).astype(jnp.bfloat16)


def triple_dot(left_side, right_side):
    left_high, left_low = left_side
    right_high, right_low = right_side
    return dot_nn(left_high, right_high) + (
        dot_nn(left_high, right_low) + dot_nn(left_low, right_high)
    )


def symmetric_product(left_pair, right_pair, size, put):
    tile = min(256, size)
    for first in range(0, size, tile):
        rows = slice(first, first + tile)
        part = triple_dot(
            tuple(side[rows, :] for side in left_pair),
            tuple(side[:, first:] for side in right_pair),
        )
        put(rows, slice(first, size), part)
        for second in range(first + tile, size, tile):
            columns = slice(second, second + tile)
            put(columns, rows, part[:, second - first : second - first + tile].T)


def store_pair(pair, rows, columns, values):
    high, low = split_high(values)
    pair[0][rows, columns] = high
    pair[1][rows, columns] = low


def ortho_block_kernel(fresh, steps, halves_ref, m_ref, x_ref, xh, xl, th, tl, gram, gh, gl, sh, sl):
    size = m_ref.shape[0]
    tile = 256
    halves = halves_ref[0] == 1
    half = size // 2

    def square_sum(columns):
        total = jnp.zeros((1, half), jnp.float32)
        for first in range(0, size, tile):
            piece = m_ref[first : first + tile, columns]
            total = total + jnp.sum(piece * piece, axis=0, keepdims=True)
        return jnp.sum(total)

    if fresh:
        lower, upper = square_sum(slice(0, half)), square_sum(slice(half, size))
        for columns, own in ((slice(0, half), lower), (slice(half, size), upper)):
            squares = jnp.full((1, half), jnp.where(halves, own, lower + upper), jnp.float32)
            scale = 1.0 / (jnp.sqrt(squares) + ORTHO_EPS)
            for first in range(0, size, tile):
                rows = slice(first, first + tile)
                x_ref[rows, columns] = m_ref[rows, columns] * scale
    else:
        x_ref[...] = m_ref[...]

    def mask(rows, columns, values):
        row = rows.start + lax.broadcasted_iota(jnp.int32, values.shape, 0)
        column = columns.start + lax.broadcasted_iota(jnp.int32, values.shape, 1)
        return jnp.where(((row < half) != (column < half)) & halves, 0.0, values)

    def put_gram(rows, columns, values):
        values = mask(rows, columns, values)
        gram[rows, columns] = values
        store_pair((gh, gl), rows, columns, values)

    def put_change(rows, columns, values):
        values = POLY_TWO * gram[rows, columns] + POLY_THREE * values
        store_pair((sh, sl), rows, columns, values)

    def iterate(iteration, carry):
        for first in range(0, size, tile):
            rows = slice(first, first + tile)
            high, low = split_high(x_ref[rows, :])
            xh[rows, :] = high
            xl[rows, :] = low
            th[:, rows] = high.T
            tl[:, rows] = low.T
        symmetric_product((th, tl), (xh, xl), size, put_gram)
        symmetric_product((gh, gl), (gh, gl), size, put_change)
        for first in range(0, size, tile):
            rows = slice(first, first + tile)
            change = triple_dot((xh[rows, :], xl[rows, :]), (sh[...], sl[...]))
            x_ref[rows, :] = POLY_ONE * x_ref[rows, :] + change
        return carry

    lax.fori_loop(0, steps, iterate, 0)


def ortho_block_call(fresh, steps, block, halves):
    size = block.shape[0]
    low = pltpu.VMEM((size, size), jnp.bfloat16)
    return pl.pallas_call(
        functools.partial(ortho_block_kernel, fresh, steps),
        in_specs=[
            pl.BlockSpec(memory_space=pltpu.SMEM),
            pl.BlockSpec(memory_space=pltpu.VMEM),
        ],
        out_specs=pl.BlockSpec(memory_space=pltpu.VMEM),
        out_shape=jax.ShapeDtypeStruct((size, size), jnp.float32),
        scratch_shapes=[low] * 4 + [pltpu.VMEM((size, size), jnp.float32)] + [low] * 4,
        compiler_params=pltpu.CompilerParams(vmem_limit_bytes=56 * 1024 * 1024),
        cost_estimate=pl.CostEstimate(
            flops=steps * 9 * 2 * size**3, bytes_accessed=8 * size * size, transcendentals=0
        ),
        name="ortho_block",
    )(halves.reshape(1), block)


def ortho_rows_kernel(m_ref, n_ref, o_ref, xh, xl, th, tl, gram, pair_g, pair_p, pair_t, product, pair_q):
    side_rows, size = m_ref.shape
    own = o_ref.shape[0]
    tile = 256
    sides = [(side, first) for side in (m_ref, n_ref) for first in range(0, side_rows, tile)]
    squares = jnp.zeros((1, size), jnp.float32)
    for side, first in sides:
        piece = side[first : first + tile, :]
        squares = squares + jnp.sum(piece * piece, axis=0, keepdims=True)
    total = jnp.full((1, size), jnp.sum(squares), jnp.float32)
    scale = 1.0 / (jnp.sqrt(total) + ORTHO_EPS)
    for index, (side, first) in enumerate(sides):
        rows = slice(index * tile, (index + 1) * tile)
        high, low = split_high(side[first : first + tile, :] * scale)
        xh[rows, :] = high
        xl[rows, :] = low
        th[:, rows] = high.T
        tl[:, rows] = low.T
    pair_g, pair_p, pair_t, pair_q = [
        (pair.at[0], pair.at[1]) for pair in (pair_g, pair_p, pair_t, pair_q)
    ]

    def put_gram(rows, columns, values):
        gram[rows, columns] = values
        store_pair(pair_g, rows, columns, values)

    def put_factor(rows, columns, values):
        row = rows.start + lax.broadcasted_iota(jnp.int32, values.shape, 0)
        column = columns.start + lax.broadcasted_iota(jnp.int32, values.shape, 1)
        values = POLY_TWO * gram[rows, columns] + POLY_THREE * values
        values = values + jnp.where(row == column, POLY_ONE, 0.0)
        product[rows, columns] = values
        store_pair(pair_p, rows, columns, values)

    def put_turn(rows, columns, values):
        store_pair(pair_t, rows, columns, values)

    def put_product(rows, columns, values):
        product[rows, columns] = values

    def keep_product():
        for first in range(0, size, tile):
            rows = slice(first, first + tile)
            store_pair(pair_q, rows, slice(0, size), product[rows, :])

    symmetric_product((th, tl), (xh, xl), size, put_gram)
    symmetric_product(pair_g, pair_g, size, put_factor)
    keep_product()

    def iterate(iteration, carry):
        symmetric_product(pair_g, pair_p, size, put_turn)
        symmetric_product(pair_t, pair_p, size, put_gram)
        symmetric_product(pair_g, pair_g, size, put_factor)
        symmetric_product(pair_q, pair_p, size, put_product)
        keep_product()
        return carry

    lax.fori_loop(0, 4, iterate, 0)
    o_ref[...] = triple_dot((xh[:own, :], xl[:own, :]), (pair_q[0][...], pair_q[1][...]))


def ortho_rows_call(side_rows, other_rows, own_rows):
    rows_all, size = 2 * side_rows.shape[0], side_rows.shape[1]
    low = jnp.bfloat16
    pair = pltpu.VMEM((2, size, size), low)
    square = pltpu.VMEM((size, size), jnp.float32)
    return pl.pallas_call(
        ortho_rows_kernel,
        in_specs=[pl.BlockSpec(memory_space=pltpu.VMEM)] * 2,
        out_specs=pl.BlockSpec(memory_space=pltpu.VMEM),
        out_shape=jax.ShapeDtypeStruct((own_rows, size), jnp.float32),
        scratch_shapes=[pltpu.VMEM((rows_all, size), low)] * 2
        + [pltpu.VMEM((size, rows_all), low)] * 2
        + [square, pair, pair, pair, square, pair],
        compiler_params=pltpu.CompilerParams(vmem_limit_bytes=40 * 1024 * 1024),
        cost_estimate=pl.CostEstimate(
            flops=60 * 2 * size**3, bytes_accessed=16 * size * size, transcendentals=0
        ),
        name="ortho_rows",
    )(side_rows, other_rows)


def take_half(values, axis, own):
    keep = lax.dynamic_index_in_dim(values, own, axis, keepdims=False)
    send = lax.dynamic_index_in_dim(values, 1 - own, axis, keepdims=False)
    return keep, send


def reduce_to_owner(values, bits, count, place, order):
    left = bits[::-1]
    width = values.shape[1]
    for bit in order:
        before = 2 ** left.index(bit)
        left.remove(bit)
        split = values.reshape(before, 2, values.shape[0] // (2 * before), width)
        keep, send = take_half(split, 1, (place // bit) % 2)
        values = low_add(keep, swap_bit(send, count, bit)).reshape(-1, width)
    return values


def gather_from_owners(values, count, place, order, held=()):
    held = list(held)
    for bit in order:
        other = swap_bit(values, count, bit)
        held.append(bit)
        held.sort(reverse=True)
        after_bits = 2 ** (len(held) - 1 - held.index(bit))
        upper = (place // bit) % 2 == 1
        width = values.shape[1]
        pieces = (2 ** (len(held) - 1) // after_bits, 1, -1, width)
        own, other = values.reshape(pieces), other.reshape(pieces)
        values = jnp.where(
            upper,
            jnp.concatenate([other, own], axis=1),
            jnp.concatenate([own, other], axis=1),
        ).reshape(-1, width)
    return values


def muon_update(weight, ortho):
    return weight * (1.0 - MUON_RATE * WEIGHT_DECAY) - MUON_RATE * MUON_SHAPE * math.sqrt(D) * ortho


def shards(
    tokens,
    out_grad,
    lengths,
    routes,
    attn_weight,
    router_weight,
    expert_weight,
    gains,
    attn_moment,
    router_moment,
    expert_moment,
    gain_first,
    gain_second,
    attn_ema,
    router_ema,
    expert_ema,
    gain_ema,
):
    seqs_here = lengths.shape[0]
    tok_here = tokens.shape[0]
    seq_len = tok_here // seqs_here
    query_width = HEADS * HEAD_DIM
    kv_width = KV_HEADS * HEAD_DIM
    qkv_width = query_width + 2 * kv_width
    n_dp, n_blk = lax.axis_size("dp"), lax.axis_size("blk")
    count = n_dp * n_blk
    place = lax.axis_index(AXES)
    own_rows = expert_weight.shape[1]
    parts = D // own_rows
    half_bit, pair_bit = parts // 2, n_blk
    bit_z, bit_x, bit_y = [bit for bit in bits_below(parts, count) if bit != pair_bit]
    low_bits = bits_below(1, parts)
    upper_half = (place // half_bit) % 2 == 1
    groups = ((0, 0), (1, 0), (1, 1), (0, 1))
    far_bits = [
        far_x * bit_x + far_y * bit_y + far_z * bit_z
        for far_x, far_y in groups
        for far_z in range(2)
    ]
    own_experts = [(place ^ bits) // parts for bits in far_bits]
    pair_experts = [(place ^ pair_bit ^ bits) // parts for bits in far_bits]
    expert_ids = jnp.stack(own_experts + pair_experts)

    def relative(values):
        swapped = jnp.concatenate([values[:, HALF:], values[:, :HALF]], axis=1)
        return jnp.where(upper_half, swapped, values)

    attn_cols = attn_weight.shape[1]
    attn_low = attn_weight.astype(jnp.bfloat16)
    small_low = jnp.concatenate(
        [
            router_weight.astype(jnp.bfloat16),
            gains.astype(jnp.bfloat16).T,
            jnp.zeros((attn_weight.shape[0], PACK - EXPERTS - 2), jnp.bfloat16),
        ],
        axis=1,
    )
    full_packed = lax.all_gather(
        jnp.concatenate([attn_low, small_low], axis=1), AXES, axis=0, tiled=True
    )
    w_query = full_packed[:, :query_width]
    w_shared = full_packed[:, query_width:qkv_width]
    w_out = full_packed[:, qkv_width:attn_cols]
    full_router = full_packed[:, attn_cols : attn_cols + EXPERTS]
    full_gains = full_packed[:, attn_cols + EXPERTS : attn_cols + EXPERTS + 2].T
    early_bits = bits_below(1, half_bit)
    own_half = gather_rows(expert_weight.astype(jnp.bfloat16), 1, count, place, early_bits)
    level_one = (((1, 0, 0), half_bit), ((0, 1, 0), bit_x), ((0, 0, 1), bit_y))
    level_two = (((1, 1, 0), bit_x), ((0, 1, 1), bit_y), ((1, 0, 1), half_bit))
    hop_of = {half_bit: 0, bit_x: 1, bit_y: 2}

    def before_hop(chunk, bit):
        return tuple(
            side ^ 1 if index == hop_of[bit] else side for index, side in enumerate(chunk)
        )

    own_half = after(own_half, full_packed)
    from_z = swap_bit(own_half, count, bit_z)
    gain_one = full_gains[0].astype(jnp.float32)
    gain_two = full_gains[1].astype(jnp.float32)
    inputs = tokens.astype(jnp.float32)
    cosine, sine = rotary_tables(seq_len, HEAD_DIM)
    cosine = jnp.concatenate([cosine] * 4, axis=1)
    sine = jnp.concatenate([-sine, sine, -sine, sine], axis=1)
    normed_one, query, key_rows, value_rows = project_call(
        tokens, gain_one[None], full_packed, full_packed, cosine, sine
    )
    position = jnp.arange(seq_len)
    live_rows = (position[None, :] < lengths[:, None]).reshape(tok_here, 1)
    live_grad = jnp.where(live_rows, out_grad, jnp.zeros_like(out_grad))
    live_relative = after(relative(live_grad), normed_one)
    both_grad = jnp.concatenate([live_relative, swap_bit(live_relative, count, pair_bit)])
    rows_each = attn_moment.shape[0]
    block_width = attn_cols // 3

    def spread(values):
        return lax.all_to_all(values, "blk", split_axis=0, concat_axis=0, tiled=True)

    old_pieces = [attn_moment[:, :block_width], attn_moment[:, block_width : 2 * block_width]]
    old_pieces += [
        attn_moment[:, 2 * block_width :],
        jnp.pad(router_moment, ((0, 0), (0, block_width - EXPERTS))),
    ]
    old_tasks = jnp.pad(jnp.stack(old_pieces), ((0, n_blk - 4), (0, 0), (0, 0)))
    old_tasks = spread(old_tasks).reshape(n_blk * rows_each, block_width)
    attended, totals = attend_call(
        lengths,
        query,
        key_rows,
        value_rows,
        seq_len,
        [old_tasks],
    )
    attended, own_half, from_z = lax.optimization_barrier((attended, own_half, from_z))
    chunks = {(0, 0, 0): jnp.stack([own_half, from_z], axis=1)}
    for chunk, bit in level_one:
        chunks[chunk] = swap_bit(chunks[before_hop(chunk, bit)], count, bit)
    branch = plain_dot(attended, w_out, 1, 1)
    for chunk, bit in level_two:
        chunks[chunk] = swap_bit(after(chunks[before_hop(chunk, bit)], branch), count, bit)
    hidden_state = inputs + RESID_MULT * branch
    scale_two = lax.rsqrt(jnp.mean(hidden_state * hidden_state, axis=-1, keepdims=True) + NORM_EPS)
    unit_two = hidden_state * scale_two
    normed_two = (unit_two * gain_two).astype(jnp.bfloat16)
    pick = (jnp.arange(EXPERTS)[:, None] == expert_ids[None, :]).astype(jnp.bfloat16)
    router_here = jnp.dot(full_router, pick, preferred_element_type=jnp.float32).astype(
        jnp.bfloat16
    )
    logits = jnp.dot(normed_two, router_here, preferred_element_type=jnp.float32)
    used = jnp.any(routes[:, :, None] == expert_ids[None, None, :], axis=1)
    chosen_top = jnp.max(jnp.where(used, logits, NEG_FILL), axis=1, keepdims=True)
    exponent = jnp.where(used, jnp.exp(jnp.where(used, logits - chosen_top, 0.0)), 0.0)
    gate_weights = exponent / jnp.sum(exponent, axis=1, keepdims=True)
    second = relative(normed_two)
    other_second = swap_bit(second, count, pair_bit)
    gates_here = jnp.pad(gate_weights[:, :8], ((0, 0), (0, PACK - 8)))
    gates_there = jnp.pad(gate_weights[:, 8:], ((0, 0), (0, PACK - 8)))
    other_gates = swap_bit(gates_there, count, pair_bit)
    both_second = jnp.concatenate([second, other_second])
    both_gates = jnp.concatenate([gates_here, other_gates])
    own_parts, pair_parts, dgates = [], [], []
    grads, moved = {}, {}

    def send(chunk, bit):
        moved[chunk] = swap_bit(grads[chunk], count, bit)

    waits = {
        (0, 0): lambda: [chunks[0, 1, 0], chunks[0, 0, 1]],
        (1, 0): lambda: [chunks[0, 1, 1], chunks[1, 0, 1]],
        (1, 1): lambda: [moved[1, 0, 0], pair_parts[0]],
        (0, 1): lambda: [moved[1, 1, 0], pair_parts[1]],
    }
    for turn_index, (far_x, far_y) in enumerate(groups):
        weights = [chunks[half, far_x, far_y] for half in range(2)]
        own_part, pair_part, dgate, grad_own, grad_other = expert_call(
            2 * turn_index,
            both_second,
            both_grad,
            both_gates,
            weights,
            waits[far_x, far_y](),
        )
        own_parts.append(own_part)
        pair_parts.append(swap_bit(pair_part, count, pair_bit))
        dgates.append(dgate)
        grads[0, far_x, far_y] = grad_own
        grads[1, far_x, far_y] = grad_other
        if (far_x, far_y) == (0, 0):
            send((1, 0, 0), half_bit)
            chunks[1, 1, 1] = swap_bit(after(chunks[1, 0, 1], own_part), count, bit_x)
        if (far_x, far_y) == (1, 0):
            send((1, 1, 0), half_bit)
        if (far_x, far_y) == (1, 1):
            send((1, 1, 1), bit_x)
            send((0, 1, 1), bit_y)

    def total_of(*pieces):
        total = pieces[0].astype(jnp.float32)
        for piece in pieces[1:]:
            total = total + piece.astype(jnp.float32)
        return total.astype(jnp.bfloat16)

    last_other, grads[0, 0, 1], own_parts[3], dgates[3], *others = (
        lax.optimization_barrier(
            (
                grads[1, 0, 1],
                grads[0, 0, 1],
                own_parts[3],
                dgates[3],
                moved[1, 1, 1],
                moved[0, 1, 1],
                pair_parts[2],
            )
        )
    )
    moved[1, 1, 1], moved[0, 1, 1], pair_parts[2] = others
    half_y = [
        swap_bit(total_of(last_other[kind], moved[1, 1, 1][kind]), count, half_bit)
        for kind in range(3)
    ]
    grads[0, 1, 0] = total_of(grads[0, 1, 0], moved[1, 1, 0], moved[0, 1, 1])
    send((0, 1, 0), bit_x)
    dgate_sum = (dgates[0] + dgates[1]) + (dgates[2] + dgates[3])
    pair_dgates = swap_bit(dgate_sum[tok_here:], count, pair_bit)

    def gather_sum(parts):
        total = None
        for part in parts:
            part = part.astype(jnp.float32)
            total = part if total is None else total + part
        return relative(total)

    grad_normed_two = gather_sum([part[1] for part in own_parts + pair_parts])
    grad_gates = jnp.concatenate([dgate_sum[:tok_here, :8], pair_dgates[:, :8]], axis=1)
    grad_out = live_grad.astype(jnp.float32)
    inner_sum = jnp.sum(gate_weights * grad_gates, axis=1, keepdims=True)
    grad_logits = (gate_weights * (grad_gates - inner_sum)).astype(jnp.bfloat16)
    grad_normed_two = grad_normed_two + plain_dot(grad_logits, router_here, 1, 1)
    grad_router = jnp.matmul(
        plain_dot(normed_two, grad_logits, 0, 0),
        pick.astype(jnp.float32).T,
        precision=lax.Precision.HIGHEST,
    )
    grad_hidden_state = grad_out + norm_back(grad_normed_two, unit_two, scale_two, gain_two)
    grad_gain_two = jnp.sum(grad_normed_two * unit_two, axis=0)
    grad_branch = (RESID_MULT * grad_hidden_state).astype(jnp.bfloat16)
    grad_w_out = plain_dot(grad_branch, attended, 0, 0)
    dp_bits = bits_below(n_blk, count)
    far_dp = [bit for bit in dp_bits if bit not in (pair_bit, bit_x, bit_y)]
    first_x = [pair_bit, bit_x, bit_y] + far_dp
    first_y = [pair_bit, bit_y, bit_x] + far_dp

    def to_dp(values, order):
        return reduce_to_owner(values, dp_bits, count, place, order)

    low_grad_out = pin(grad_w_out.astype(jnp.bfloat16))
    grad_attended = jnp.dot(grad_branch, w_out, preferred_element_type=jnp.float32).astype(
        jnp.bfloat16
    )
    def attend_back(part, held, done):
        return attend_back_call(
            part,
            lengths,
            query,
            key_rows,
            value_rows,
            grad_attended,
            totals,
            cosine,
            sine,
            held,
            done,
        )

    first_heads = attend_back(0, [], [])
    last_own, half_y[0], _ = lax.optimization_barrier((grads[0, 0, 1], half_y[0], first_heads[0]))
    grad_query, grad_key, grad_value = attend_back(1, first_heads, [half_y[0], moved[0, 1, 0]])
    half_y[1:], _ = lax.optimization_barrier((half_y[1:], grad_query))
    from_y = [
        swap_bit(total_of(last_own[kind], half_y[kind]), count, bit_y) for kind in range(3)
    ]
    late_parts = after(tuple(own_parts + pair_parts), grad_query)
    block_out = (hidden_state + RESID_MULT * gather_sum([part[0] for part in late_parts])).astype(
        jnp.bfloat16
    )
    low_grad = [
        pin(plain_dot(normed_one, piece, 0, 0).astype(jnp.bfloat16))
        for piece in (grad_query, grad_key, grad_value)
    ]
    grad_normed_one = (
        plain_dot(grad_query, w_query, 1, 1)
        + plain_dot(grad_key, w_shared[:, :kv_width], 1, 1)
        + plain_dot(grad_value, w_shared[:, kv_width:], 1, 1)
    )
    nearest, from_y[0], grad_normed_one, low_grad[1:] = lax.optimization_barrier(
        (grads[0, 0, 0], from_y[0], grad_normed_one, low_grad[1:])
    )
    scale_one = lax.rsqrt(jnp.mean(inputs * inputs, axis=-1, keepdims=True) + NORM_EPS)
    unit_one = inputs * scale_one
    input_grad = grad_hidden_state + norm_back(grad_normed_one, unit_one, scale_one, gain_one)
    grad_gain_one = jnp.sum(grad_normed_one * unit_one, axis=0)
    grad_small = jnp.concatenate(
        [
            grad_router,
            jnp.stack([grad_gain_one, grad_gain_two], axis=1),
            jnp.zeros((D, PACK - EXPERTS - 2), jnp.float32),
        ],
        axis=1,
    ).astype(jnp.bfloat16)
    wide_sum = to_dp(
        jnp.concatenate([low_grad[0], after(low_grad_out, grad_query)], axis=1), first_x
    )
    query_sum, out_sum = wide_sum[:, :query_width], wide_sum[:, query_width:]
    shared_sum = to_dp(jnp.concatenate([low_grad[1], low_grad[2], pin(grad_small)], axis=1), first_y)

    def as_tasks(first, second, third, small):
        small = jnp.pad(small, ((0, 0), (0, block_width - PACK)))
        tasks = jnp.stack([first, second, third, small])
        return jnp.pad(tasks, ((0, n_blk - 4), (0, 0), (0, 0)))

    task_parts = spread(
        as_tasks(
            query_sum, shared_sum[:, :block_width], out_sum, shared_sum[:, block_width:]
        )
    )
    task_block = MOMENTUM * old_tasks + jnp.sum(task_parts.astype(jnp.float32), axis=0)
    moment_rows = spread(task_block.reshape(n_blk, rows_each, block_width))
    moment_attn = jnp.concatenate([moment_rows[0], moment_rows[1], moment_rows[2]], axis=1)
    moment_router = moment_rows[3][:, :EXPERTS]
    gain_grad = moment_rows[3][:, EXPERTS : EXPERTS + 2].T
    used_columns = (jnp.arange(block_width) < EXPERTS) | (lax.axis_index("blk") != 3)
    task_block = jnp.where(used_columns, task_block, 0.0)
    wide_x, wide_y = far_dp + [bit_y, bit_x], far_dp + [bit_x, bit_y]
    sides = [
        gather_from_owners(task_block[:, : block_width // 2], count, place, wide_x),
        gather_from_owners(task_block[:, block_width // 2 :], count, place, wide_y),
    ]
    attn_block = jnp.concatenate(
        [gather_from_owners(side, count, place, [pair_bit], wide_x) for side in sides], axis=1
    )
    from_y[1] = after(from_y[1], wide_sum)
    from_y[2] = after(from_y[2], task_block)
    expert_sums = [
        total_of(nearest[kind], moved[1, 0, 0][kind], moved[0, 1, 0][kind], from_y[kind])
        for kind in range(3)
    ]
    z_hops = [swap_bit(expert_sums[kind][1], count, bit_z) for kind in range(3)]
    halves = (lax.axis_index("blk") == 1).astype(jnp.int32)
    half_way = ortho_block_call(True, 3, attn_block, halves)
    moment_expert, group_rows = [], []
    for kind in range(3):
        total, from_z = after((expert_sums[kind], z_hops[kind]), half_way)
        total = total[0].astype(jnp.float32) + from_z.astype(jnp.float32)
        total = total.T if kind == 2 else total
        if early_bits:
            total = reduce_rows(total.astype(jnp.bfloat16), count, place, early_bits[::-1])
        moment = MOMENTUM * expert_moment[kind] + total.astype(jnp.float32)
        rows = pin(moment)
        for bit in low_bits[:-1]:
            rows = jnp.concatenate([rows, swap_bit(rows, count, bit)])
        moment_expert.append(moment)
        group_rows.append((rows, swap_bit(rows, count, low_bits[-1])))
    attn_iter = ortho_block_call(False, 2, after(half_way, *moment_expert), halves)
    ortho_expert = [attn_iter]
    for pieces in group_rows:
        rows, other_rows = after(pieces, ortho_expert[-1])
        ortho_expert.append(ortho_rows_call(rows, other_rows, own_rows))
    ortho_expert = jnp.stack(ortho_expert[1:])
    returned = lax.dynamic_slice_in_dim(
        attn_iter, lax.axis_index("dp") * (n_blk * rows_each), n_blk * rows_each, 0
    )
    returned = spread(returned.reshape(n_blk, rows_each, block_width))
    ortho_attn = jnp.concatenate([returned[0], returned[1], returned[2]], axis=1)
    ortho_router = returned[3][:, :EXPERTS]
    moment_expert = jnp.stack(moment_expert)
    attn_new = muon_update(attn_weight, ortho_attn)
    router_new = muon_update(router_weight, ortho_router)
    expert_new = muon_update(expert_weight, ortho_expert)
    first_new = BETA_ONE * gain_first + (1.0 - BETA_ONE) * gain_grad
    second_new = BETA_TWO * gain_second + (1.0 - BETA_TWO) * gain_grad * gain_grad
    corrected_first = first_new / (1.0 - BETA_ONE**STEP)
    corrected_second = second_new / (1.0 - BETA_TWO**STEP)
    gain_new = gains - ADAM_RATE * corrected_first / (jnp.sqrt(corrected_second) + ADAM_EPS)
    return (
        block_out,
        input_grad,
        moment_attn,
        moment_router,
        moment_expert,
        attn_new,
        router_new,
        expert_new,
        attn_new.astype(jnp.bfloat16),
        router_new.astype(jnp.bfloat16),
        expert_new.astype(jnp.bfloat16),
        EMA_KEEP * attn_ema + (1.0 - EMA_KEEP) * attn_new,
        EMA_KEEP * router_ema + (1.0 - EMA_KEEP) * router_new,
        EMA_KEEP * expert_ema + (1.0 - EMA_KEEP) * expert_new,
        first_new,
        second_new,
        gain_new,
        gain_new.astype(jnp.bfloat16),
        GAIN_EMA_KEEP * gain_ema + (1.0 - GAIN_EMA_KEEP) * gain_new,
    )


def solution(mesh):
    placed = (
        P(("dp", "blk"), None),
        P(("dp", "blk"), None),
        P(("dp", "blk")),
        P(("dp", "blk"), None),
        P(("dp", "blk"), None),
        P(("dp", "blk"), None),
        P(None, ("dp", "blk"), None),
        P(None, ("dp", "blk")),
        P(("dp", "blk"), None),
        P(("dp", "blk"), None),
        P(None, ("dp", "blk"), None),
        P(None, ("dp", "blk")),
        P(None, ("dp", "blk")),
        P(("dp", "blk"), None),
        P(("dp", "blk"), None),
        P(None, ("dp", "blk"), None),
        P(None, ("dp", "blk")),
    )
    return jax.shard_map(
        shards,
        mesh=mesh,
        in_specs=placed,
        out_specs=(
            P(("dp", "blk"), None),
            P(("dp", "blk"), None),
            P(("dp", "blk"), None),
            P(("dp", "blk"), None),
            P(None, ("dp", "blk"), None),
            P(("dp", "blk"), None),
            P(("dp", "blk"), None),
            P(None, ("dp", "blk"), None),
            P(("dp", "blk"), None),
            P(("dp", "blk"), None),
            P(None, ("dp", "blk"), None),
            P(("dp", "blk"), None),
            P(("dp", "blk"), None),
            P(None, ("dp", "blk"), None),
            P(None, ("dp", "blk")),
            P(None, ("dp", "blk")),
            P(None, ("dp", "blk")),
            P(None, ("dp", "blk")),
            P(None, ("dp", "blk")),
        ),
        check_vma=False,
    )
```
